512 devices in a mesh: visit: 128 (over z, x_hi, y), patch: 4 (over x_lo, core).
Axes of the slice: x: 4 (x_hi: 2, x_lo: 2; x = x_hi * 2 + x_lo), y: 4, z: 16, core: 2. Of those that a mesh axis runs over, the one named last changes fastest.
Arguments:
- template: float32 [4, 8192, 512], P('patch', 'visit'), may hold values from -24 to 24
- science: float32 [128, 4, 64, 512], P('visit', 'patch'), may hold values from -28 to 28
- inverse_variance: float32 [128, 4, 64, 512], P('visit', 'patch'), may hold values from 0.2 to 5
- intersections: int32 [128, 4, 3], P('visit', 'patch'), may hold values from -6 to 127, as said below
Outputs:
- difference: float32 [128, 4, 64, 512], P('visit', 'patch')
- coadd_difference: float32 [4, 8192, 512], P('patch', 'visit')
The draws below stay inside these ranges and needn't reach their ends.
Inputs may be any that keep to these rules, and one draw needn't show every extreme that they name: Entry 0 of intersections[v, p] is the tile of patch p under visit v's stamp, at most 6 away from v, and that distance is reached; entries 1 and 2 are the stamp's row and column offsets against the tile, from -6 to 6, both ends reached.
All inputs are finite; a program needn't handle non-finite values.
Results may differ from the reference program's by a relative error of at most 0.0003.
Values sent between devices are 32-bit elements; how exact they have to be, the bound alone decides.
No kernel may reach another device: no remote copies, remote signals or barrier semaphores. Data moves between devices by JAX's collectives and lax.ppermute only.
A program may use at most 128 MiB of HBM per device.

```python
import math
import jax
import jax.numpy as jnp
import numpy as np
from jax import lax

TILE_ROWS = 64
TILE_COLS = 512
KHALF = 10
SHIFT = 6
REACH = 6
NBASIS = 28
VISITS = 128
PATCHES = 4
HALO = 16


def intersection_table(key):
    keys = jax.random.split(jax.random.fold_in(key, 11), 4)
    popularity = jax.random.randint(keys[0], (PATCHES, VISITS), 0, 4)
    jitter = jax.random.randint(keys[1], (VISITS, PATCHES, 2 * REACH + 1), 0, 8)
    visit_ids = jnp.arange(VISITS, dtype=jnp.int32)[:, None, None]
    patch_ids = jnp.arange(PATCHES, dtype=jnp.int32)[None, :, None]
    relative = jnp.arange(-REACH, REACH + 1, dtype=jnp.int32)[None, None, :]
    candidate = visit_ids + relative
    valid = (candidate >= 0) & (candidate < VISITS)
    favour = popularity[patch_ids, jnp.clip(candidate, 0, VISITS - 1)]
    scores = jnp.where(valid, (favour * 8 + jitter) * 64 + relative + REACH, -1)
    tiles = visit_ids[:, :, 0] + jnp.argmax(scores, axis=-1).astype(jnp.int32) - REACH
    middle = VISITS // 2
    for distance in range(1, REACH + 1):
        if middle + distance < VISITS:
            tiles = tiles.at[middle + distance, :].set(middle)
    for distance in range(1, REACH + 1):
        if VISITS - 1 - distance >= 0:
            tiles = tiles.at[VISITS - 1 - distance, :].set(VISITS - 1)
    for patch_number in range(PATCHES):
        tiles = tiles.at[middle, patch_number].set(max(middle - 1 - patch_number % REACH, 0))
        if middle - 1 >= 0:
            tiles = tiles.at[middle - 1, patch_number].set(max(middle - 1 - min(3 + patch_number, REACH), 0))
    tiles = tiles.at[0, 0].set(REACH).at[VISITS - 1, 0].set(VISITS - 1)
    row_moves = jax.random.randint(keys[2], (VISITS, PATCHES), -SHIFT, SHIFT + 1)
    row_moves = row_moves.at[0, 0].set(SHIFT).at[1, 0].set(-SHIFT)
    col_moves = jax.random.randint(keys[3], (VISITS, PATCHES), -SHIFT, SHIFT + 1)
    col_moves = col_moves.at[0, 0].set(-SHIFT).at[1, 0].set(SHIFT)
    return jnp.stack([tiles, row_moves, col_moves], axis=-1).astype(jnp.int32)


def template_field(key):
    keys = jax.random.split(jax.random.fold_in(key, 23), 3)
    field_shape = (PATCHES, VISITS * TILE_ROWS, TILE_COLS)
    rough = jnp.clip(jax.random.normal(keys[0], field_shape, jnp.float32), -5.0, 5.0)
    row_scale = jnp.exp(jax.random.uniform(keys[1], (PATCHES, VISITS * TILE_ROWS, 1), jnp.float32, -1.15, 1.15))
    col_scale = jnp.exp(jax.random.uniform(keys[2], (PATCHES, 1, TILE_COLS), jnp.float32, -0.35, 0.35))
    return rough * row_scale * col_scale


def draw_intersections(key, part):
    return intersection_table(key)


def draw_template(key, part):
    return template_field(key)


def draw_science(key, part):
    table = intersection_table(key)
    field = template_field(key)
    padded = jnp.pad(field, ((0, 0), (HALO, HALO), (HALO, HALO)))
    patch_grid = jnp.broadcast_to(jnp.arange(PATCHES, dtype=jnp.int32)[None, :], (VISITS, PATCHES))

    def cut_one(patch_index, entry):
        block = lax.dynamic_slice(padded, (patch_index, entry[0] * TILE_ROWS + HALO + entry[1], HALO + entry[2]), (1, TILE_ROWS, TILE_COLS))
        return block[0]
    cutouts = jax.vmap(jax.vmap(cut_one))(patch_grid, table)
    keys = jax.random.split(jax.random.fold_in(key, 37), 3)
    noise = jnp.clip(jax.random.normal(keys[0], (VISITS, PATCHES, TILE_ROWS, TILE_COLS), jnp.float32), -5.0, 5.0)
    level = jax.random.uniform(keys[1], (VISITS, PATCHES, 1, 1), jnp.float32, -1.0, 1.0)
    gain_factor = jax.random.uniform(keys[2], (VISITS, PATCHES, 1, 1), jnp.float32, 0.6, 1.0)
    return gain_factor * cutouts + 0.5 * noise + level


def shard_levels(key, shape, shards, low, top_value):
    factor_of, own = 1.0, jax.random.fold_in(key, 6)
    for dim, blocks in shards:
        heights = jnp.exp(jax.random.uniform(jax.random.fold_in(own, dim), (blocks,), jnp.float32, low / len(shards), top_value / len(shards)))
        factor_of = factor_of * jnp.repeat(heights, shape[dim] // blocks).reshape([-1 if axis == dim else 1 for axis in range(len(shape))])
    return factor_of


def setup_inputs(seed: int = 0) -> dict:
    streams_of = jax.random.split(jax.random.key(seed), 5)
    template = draw_template(jax.random.fold_in(streams_of[4], 71), 0)
    science = draw_science(jax.random.fold_in(streams_of[4], 71), 0)
    inverse_variance = jnp.clip(jnp.exp(math.log(5.0) - 3.218876 * jax.random.uniform(streams_of[2], (VISITS, PATCHES, TILE_ROWS, TILE_COLS), jnp.float32) ** shard_levels(streams_of[2], (VISITS, PATCHES, TILE_ROWS, TILE_COLS), ((0, 128), (1, 4)), -0.2, 0.2)), 0.2, 5.0)
    intersections = draw_intersections(jax.random.fold_in(streams_of[4], 71), 0)
    return {"template": template, "science": science, "inverse_variance": inverse_variance, "intersections": intersections}


SIGMAS = (1.0, 2.0, 4.0)
DEGREES = (4, 2, 2)
ridge_weight = 0.01

def factor_table(khalf):
    listed = []
    for width_sigma, degree in zip(SIGMAS, DEGREES):
        for exponent in range(degree + 1):
            values = [math.exp(-(offset * offset) / (2.0 * width_sigma * width_sigma)) * (offset / khalf) ** exponent for offset in range(-khalf, khalf + 1)]
            scale_norm = math.sqrt(sum((entry * entry for entry in values)))
            listed.append([entry / scale_norm for entry in values])
    return np.array(listed, dtype=np.float32)

def basis_pairs():
    pairs = []
    first_index = 0
    for degree in DEGREES:
        for power_row in range(degree + 1):
            for power_col in range(degree + 1 - power_row):
                pairs.append((first_index + power_row, first_index + power_col))
        first_index += degree + 1
    return pairs

def shifted_sum(field, factor, axis_dim, length):
    total = factor[0] * lax.slice_in_dim(field, 0, length, axis=axis_dim)
    for offset_index in range(1, factor.shape[0]):
        total = total + factor[offset_index] * lax.slice_in_dim(field, offset_index, offset_index + length, axis=axis_dim)
    return total

def reference(template, science, inverse_variance, intersections):
    table = jnp.asarray(factor_table(KHALF))
    halo_pad = jnp.pad(template, ((0, 0), (HALO, HALO), (HALO, HALO)))
    patch_ids = jnp.arange(PATCHES, dtype=jnp.int32)

    def stamp_basis(cutout):
        across = [shifted_sum(cutout, table[index], 1, TILE_COLS) for index in range(table.shape[0])]
        planes = [shifted_sum(across[pair[1]], table[pair[0]], 0, TILE_ROWS) for pair in basis_pairs()]
        planes.append(jnp.ones((TILE_ROWS, TILE_COLS), jnp.float32))
        return jnp.stack(planes)

    def cut_one(patch_index, entry):
        start_row = (entry[0] * TILE_ROWS + SHIFT + entry[1]).astype(jnp.int32)
        start_col = (SHIFT + entry[2]).astype(jnp.int32)
        block = lax.dynamic_slice(halo_pad, (patch_index.astype(jnp.int32), start_row, start_col), (1, TILE_ROWS + 2 * KHALF, TILE_COLS + 2 * KHALF))
        return block[0]

    def place_one(stamp, entry):
        padded = jnp.pad(stamp, SHIFT)
        return lax.dynamic_slice(padded, ((SHIFT - entry[1]).astype(jnp.int32), (SHIFT - entry[2]).astype(jnp.int32)), (TILE_ROWS, TILE_COLS))

    def one_visit(inputs):
        observed, weight, entries = inputs
        cutouts = jax.vmap(cut_one)(patch_ids, entries)
        basis = jax.vmap(stamp_basis)(cutouts)
        flattened = basis.reshape(PATCHES, NBASIS, TILE_ROWS * TILE_COLS)
        weighted = flattened * weight.reshape(PATCHES, 1, TILE_ROWS * TILE_COLS)
        normal = jnp.einsum('pkn,pln->kl', weighted, flattened, precision=lax.Precision.HIGHEST)
        moments = jnp.einsum('pkn,pn->k', weighted, observed.reshape(PATCHES, TILE_ROWS * TILE_COLS), precision=lax.Precision.HIGHEST)
        regular = normal + ridge_weight * jnp.trace(normal) / NBASIS * jnp.eye(NBASIS, dtype=jnp.float32)
        lower_factor = jnp.linalg.cholesky(regular)
        coefficients = jax.scipy.linalg.cho_solve((lower_factor, True), moments)
        model = jnp.einsum('k,pkab->pab', coefficients, basis, precision=lax.Precision.HIGHEST)
        difference = (observed - model) * jnp.sqrt(weight)
        placed = jax.vmap(place_one)(difference, entries)
        return (difference, placed)
    difference, placed = lax.map(one_visit, (science, inverse_variance, intersections))
    tiles = intersections[:, :, 0]
    results = []
    for patch_index in range(PATCHES):
        sums = jax.ops.segment_sum(placed[:, patch_index], tiles[:, patch_index], num_segments=VISITS)
        counts = jax.ops.segment_sum(jnp.ones((VISITS,), jnp.int32), tiles[:, patch_index], num_segments=VISITS)
        divisor = jnp.maximum(counts, 1).astype(jnp.float32)
        results.append((sums / divisor[:, None, None]).reshape(VISITS * TILE_ROWS, TILE_COLS))
    return (difference, jnp.stack(results))
```

```python
import functools
import math

import jax
import jax.numpy as jnp
import ml_dtypes
import numpy as np
from jax import lax
from jax.experimental import pallas as pl
from jax.experimental.pallas import tpu as pltpu
from jax.sharding import PartitionSpec as P

KHALF = 10
SHIFT = 6
REACH = 6
NBASIS = 28
ROWS = 64
COLS = 512
PLANE = 8
SPAN = 96
SLOTS = 32
BLOCK = 128
BLOCKS = COLS // BLOCK
USED = NBASIS + 1
HALF = 32
DEPTH = 64

SIGMAS = (1.0, 2.0, 4.0)
DEGREES = (4, 2, 2)
RIDGE = 0.01
LIMIT = 32 * 1024 * 1024

SMEM = pl.BlockSpec(memory_space=pltpu.SMEM)
VMEM = pl.BlockSpec(memory_space=pltpu.VMEM)
ANY = pl.BlockSpec(memory_space=pl.ANY)


def factor_table():
    listed = []
    for width_sigma, degree in zip(SIGMAS, DEGREES):
        for exponent in range(degree + 1):
            values = [
                math.exp(-(offset * offset) / (2.0 * width_sigma * width_sigma))
                * (offset / KHALF) ** exponent
                for offset in range(-KHALF, KHALF + 1)
            ]
            scale_norm = math.sqrt(sum((entry * entry for entry in values)))
            listed.append([entry / scale_norm for entry in values])
    return np.array(listed, dtype=np.float32)


def row_factors_by_column_factor():
    groups = []
    first = 0
    for degree in DEGREES:
        for power_col in range(degree + 1):
            groups.append([first + power_row for power_row in range(degree + 1 - power_col)])
        first += degree + 1
    return groups


GROUPS = row_factors_by_column_factor()
NFACTORS = len(GROUPS)


def split_constant(values):
    high = values.astype(ml_dtypes.bfloat16)
    low = (values - high.astype(np.float32)).astype(ml_dtypes.bfloat16)
    return high, low


def column_tables():
    table = factor_table()
    distance = np.arange(2 * BLOCK)[:, None] - np.arange(BLOCK)[None, :]
    bands = np.zeros((2 * BLOCK, NFACTORS, BLOCK), np.float32)
    for offset in range(2 * KHALF + 1):
        bands += table[None, :, offset, None] * (distance == offset)[:, None, :]
    return split_constant(bands.reshape(2 * BLOCK, NFACTORS * BLOCK))


def row_tables():
    table = factor_table()
    distance = np.arange(DEPTH)[None, :] - np.arange(HALF)[:, None]
    planes = [index for group in GROUPS for index in group]
    bands = np.zeros((len(planes), HALF, DEPTH), np.float32)
    for offset in range(2 * KHALF + 1):
        bands += table[planes, offset][:, None, None] * (distance == offset)[None]
    high, low = split_constant(bands.reshape(len(planes) * HALF, DEPTH))
    return np.concatenate([high, high, low], axis=1)


def split(values):
    high = values.astype(jnp.bfloat16)
    low = (values - high.astype(jnp.float32)).astype(jnp.bfloat16)
    return high, low


def put_plane(planes, slot, row, values):
    for block in range(BLOCKS):
        at = (block * SLOTS + slot) * ROWS + row
        planes[at : at + values.shape[0], :] = values[:, block * BLOCK : (block + 1) * BLOCK]


def serve_kernel(window, own, below, above, piece_own, piece_up, piece_down):
    base = (lax.axis_index("visit") // PLANE) * PLANE
    for entries, piece in ((own, piece_own), (below, piece_down), (above, piece_up)):
        start = (entries[0, 0] - base) * ROWS + entries[0, 1] - KHALF
        first = lax.shift_right_arithmetic(start, 3)
        for part in range(SPAN // 8):
            index = first + part
            inside = jnp.logical_and(index >= 0, index < PLANE * ROWS // 8)
            source = pl.multiple_of(jnp.clip(index, 0, PLANE * ROWS // 8 - 1) * 8, 8)
            rows = window[pl.ds(source, 8), :]
            piece[8 * part : 8 * part + 8, :] = jnp.where(inside, rows, 0.0)


def serve(window, own, below, above):
    shape = jax.ShapeDtypeStruct((SPAN, COLS), jnp.float32)
    return pl.pallas_call(
        serve_kernel,
        out_shape=(shape, shape, shape),
        in_specs=[VMEM, SMEM, SMEM, SMEM],
        out_specs=(VMEM, VMEM, VMEM),
        compiler_params=pltpu.CompilerParams(vmem_limit_bytes=LIMIT),
        name="serve",
    )(window, own, below, above)


def basis_kernel(
    piece_a, piece_b, piece_c, science, weight, col_high, col_low, row_table, entries,
    planes_out, gram_out,
    high_rows, low_rows, planes, sems,
):
    remainder = lax.bitwise_and(entries[0, 1] + SHIFT, 7)
    rows = piece_a[...] + piece_b[...] + piece_c[...]
    rows = pltpu.roll(rows, lax.rem(SPAN - remainder, SPAN), axis=0)
    padded = jnp.concatenate([rows, jnp.zeros((SPAN, BLOCK), jnp.float32)], axis=1)
    cutout = pltpu.roll(padded, KHALF - entries[0, 2], axis=1)
    cut_high, cut_low = split(cutout)
    for block in range(COLS // BLOCK):
        cols = slice(block * BLOCK, (block + 2) * BLOCK)
        both = jnp.concatenate([cut_high[:, cols], cut_low[:, cols]], axis=0)
        main = jnp.dot(both, col_high[...], preferred_element_type=jnp.float32)
        rest = jnp.dot(cut_high[:, cols], col_low[...], preferred_element_type=jnp.float32)
        across = main[:SPAN] + main[SPAN:] + rest
        across_high, across_low = split(across)
        for factor in range(NFACTORS):
            take = slice(factor * BLOCK, (factor + 1) * BLOCK)
            put = slice(block * BLOCK, (block + 1) * BLOCK)
            high_rows[factor, :, put] = across_high[:, take]
            low_rows[factor, :, put] = across_low[:, take]
    root = jnp.sqrt(weight[...])
    first = 0
    for factor, group in enumerate(GROUPS):
        table = row_table[first * HALF : (first + len(group)) * HALF, :]
        for half in range(ROWS // HALF):
            take = slice(half * HALF, half * HALF + DEPTH)
            high = high_rows[factor, take, :]
            stacked = jnp.concatenate([high, low_rows[factor, take, :], high], axis=0)
            out = jnp.dot(table, stacked, preferred_element_type=jnp.float32)
            for member in range(len(group)):
                scaled = (
                    out[member * HALF : (member + 1) * HALF] * root[half * HALF : (half + 1) * HALF]
                )
                put_plane(planes, first + member, half * HALF, scaled)
        first += len(group)
    put_plane(planes, NBASIS - 1, 0, root)
    put_plane(planes, NBASIS, 0, root * science[...])
    for slot in range(USED, SLOTS):
        put_plane(planes, slot, 0, jnp.zeros((ROWS, COLS), jnp.float32))
    copies = [
        pltpu.make_async_copy(
            planes.at[pl.ds(block * SLOTS * ROWS, USED * ROWS), :],
            planes_out.at[block],
            sems.at[block],
        )
        for block in range(BLOCKS)
    ]
    for copy in copies:
        copy.start()

    def gram_step(chunk, total):
        highs, lows = [], []
        for inner in range(8):
            for block in range(BLOCKS):
                row = block * SLOTS * ROWS + chunk * 8 + inner
                high, low = split(planes[pl.ds(row, SLOTS, stride=ROWS), :])
                highs.append(high)
                lows.append(low)
        high = jnp.concatenate(highs, axis=1)
        low = jnp.concatenate(lows, axis=1)
        both = jnp.concatenate([high, low], axis=0)
        return total + lax.dot_general(
            high, both, (((1,), (1,)), ((), ())), preferred_element_type=jnp.float32
        )

    total = lax.fori_loop(0, ROWS // 8, gram_step, jnp.zeros((SLOTS, 2 * SLOTS), jnp.float32))
    gram_out[...] = jnp.concatenate(
        [total, jnp.zeros((SLOTS, BLOCK - 2 * SLOTS), jnp.float32)], axis=1
    )
    for copy in copies:
        copy.wait()


def basis(pieces, science, weight, entries):
    col_high, col_low = column_tables()
    return pl.pallas_call(
        basis_kernel,
        out_shape=(
            jax.ShapeDtypeStruct((BLOCKS, USED * ROWS, BLOCK), jnp.float32),
            jax.ShapeDtypeStruct((SLOTS, BLOCK), jnp.float32),
        ),
        in_specs=[VMEM] * 8 + [SMEM],
        out_specs=(ANY, VMEM),
        scratch_shapes=[
            pltpu.VMEM((NFACTORS, SPAN, COLS), jnp.bfloat16),
            pltpu.VMEM((NFACTORS, SPAN, COLS), jnp.bfloat16),
            pltpu.VMEM((BLOCKS * SLOTS * ROWS, BLOCK), jnp.float32),
            pltpu.SemaphoreType.DMA((BLOCKS,)),
        ],
        compiler_params=pltpu.CompilerParams(vmem_limit_bytes=LIMIT),
        name="basis",
    )(
        *pieces, science, weight, jnp.asarray(col_high), jnp.asarray(col_low),
        jnp.asarray(row_tables()), entries,
    )


def solve_kernel(grams, planes_in, entries, difference, placed, planes, sem):
    copy = pltpu.make_async_copy(planes_in, planes, sem)
    copy.start()
    total = grams[0] + grams[1] + grams[2] + grams[3]
    cross = total[:, SLOTS : 2 * SLOTS]
    normal = total[:, :SLOTS] + cross + cross.T
    row_id = lax.broadcasted_iota(jnp.int32, (SLOTS, SLOTS), 0)
    col_id = lax.broadcasted_iota(jnp.int32, (SLOTS, SLOTS), 1)
    diagonal = jnp.logical_and(row_id == col_id, row_id < NBASIS)
    trace = jnp.sum(jnp.where(diagonal, normal, 0.0), keepdims=True)
    matrix = normal + jnp.where(diagonal, RIDGE * trace / NBASIS, 0.0)
    for step in range(NBASIS):
        row = matrix[step : step + 1, :]
        inverse = 1.0 / row[:, step : step + 1]
        scaled = row * inverse
        column = jnp.where(row_id[:, :1] == step, 0.0, matrix[:, step : step + 1])
        matrix = jnp.where(row_id == step, scaled, matrix - column * scaled)
    answer = jnp.broadcast_to(matrix[:, NBASIS : NBASIS + 1], (SLOTS, BLOCK))
    copy.wait()
    for block in range(BLOCKS):
        total = planes[block, NBASIS * ROWS : USED * ROWS, :]
        for plane in range(NBASIS):
            factor = jnp.broadcast_to(answer[plane : plane + 1, :], (ROWS, BLOCK))
            total = total - factor * planes[block, plane * ROWS : (plane + 1) * ROWS, :]
        difference[:, block * BLOCK : (block + 1) * BLOCK] = total
    row_move, col_move = entries[0, 1], entries[0, 2]
    moved = pltpu.roll(difference[...], lax.rem(row_move + ROWS, ROWS), axis=0)
    moved = pltpu.roll(moved, lax.rem(col_move + COLS, COLS), axis=1)
    from_row = lax.broadcasted_iota(jnp.int32, (ROWS, COLS), 0) - row_move
    from_col = lax.broadcasted_iota(jnp.int32, (ROWS, COLS), 1) - col_move
    inside = (from_row >= 0) & (from_row < ROWS) & (from_col >= 0) & (from_col < COLS)
    placed[...] = jnp.where(inside, moved, 0.0)


def solve(grams, planes, entries):
    shape = jax.ShapeDtypeStruct((ROWS, COLS), jnp.float32)
    return pl.pallas_call(
        solve_kernel,
        out_shape=(shape, shape),
        in_specs=[VMEM, ANY, SMEM],
        out_specs=(VMEM, VMEM),
        scratch_shapes=[
            pltpu.VMEM((BLOCKS, USED * ROWS, BLOCK), jnp.float32),
            pltpu.SemaphoreType.DMA,
        ],
        compiler_params=pltpu.CompilerParams(vmem_limit_bytes=LIMIT),
        name="solve",
    )(grams, planes, entries)


def gather_kernel(stamp_own, stamp_below, stamp_above, own, below, above, tiles):
    base = (lax.axis_index("visit") // PLANE) * PLANE
    hits = [entries[0, 0] - base for entries in (own, below, above)]
    for tile in range(PLANE):
        total = jnp.zeros((ROWS, COLS), jnp.float32)
        count = jnp.float32(0.0)
        for hit, stamp in zip(hits, (stamp_own, stamp_below, stamp_above)):
            total = total + jnp.where(hit == tile, stamp[...], 0.0)
            count = count + jnp.where(hit == tile, 1.0, 0.0)
        tiles[tile, :ROWS, :] = total
        tiles[tile, ROWS:, :] = jnp.full((8, COLS), count, jnp.float32)


def gather(stamps, own, below, above):
    return pl.pallas_call(
        gather_kernel,
        out_shape=jax.ShapeDtypeStruct((PLANE, ROWS + 8, COLS), jnp.float32),
        in_specs=[VMEM] * 3 + [SMEM] * 3,
        out_specs=VMEM,
        compiler_params=pltpu.CompilerParams(vmem_limit_bytes=LIMIT),
        name="gather",
    )(*stamps, own, below, above)


def mean_kernel(parts, coadd):
    total = parts[0]
    for index in range(1, PLANE):
        total = total + parts[index]
    count = jnp.maximum(total[ROWS : ROWS + 1, :], 1.0)
    coadd[...] = total[:ROWS] / count


def mean(parts):
    return pl.pallas_call(
        mean_kernel,
        out_shape=jax.ShapeDtypeStruct((ROWS, COLS), jnp.float32),
        in_specs=[VMEM],
        out_specs=VMEM,
        compiler_params=pltpu.CompilerParams(vmem_limit_bytes=LIMIT),
        name="mean",
    )(parts)


def shards(template, science, inverse_variance, intersections):
    visits = lax.axis_size("visit")
    groups = [list(range(first, first + PLANE)) for first in range(0, visits, PLANE)]
    upward = [(i, (i + PLANE) % visits) for i in range(visits)]
    downward = [(target, source) for source, target in upward]
    own = intersections[0]
    below = lax.ppermute(own, "visit", upward)
    above = lax.ppermute(own, "visit", downward)
    copies = jnp.broadcast_to(template, (PLANE, ROWS, COLS))
    window = lax.all_to_all(copies, "visit", 0, 0, axis_index_groups=groups)
    piece_own, piece_up, piece_down = serve(
        window.reshape(PLANE * ROWS, COLS), own, below, above
    )
    from_above = lax.ppermute(piece_down, "visit", downward)
    from_below = lax.ppermute(piece_up, "visit", upward)
    planes, gram = basis(
        (piece_own, from_above, from_below), science[0, 0], inverse_variance[0, 0], own
    )
    grams = lax.all_gather(gram, "patch")
    difference, placed = solve(grams, planes, own)
    stamp_below = lax.ppermute(placed, "visit", upward)
    stamp_above = lax.ppermute(placed, "visit", downward)
    tiles = gather((placed, stamp_below, stamp_above), own, below, above)
    parts = lax.all_to_all(tiles, "visit", 0, 0, axis_index_groups=groups)
    return (difference[None, None], mean(parts)[None])


def solution(mesh):
    in_specs = (
        P("patch", "visit", None),
        P("visit", "patch", None, None),
        P("visit", "patch", None, None),
        P("visit", "patch", None),
    )
    out_specs = (P("visit", "patch", None, None), P("patch", "visit", None))
    return jax.shard_map(shards, mesh=mesh, in_specs=in_specs, out_specs=out_specs, check_vma=False)
```

```python
import functools
import math

import jax
import jax.numpy as jnp
import ml_dtypes
import numpy as np
from jax import lax
from jax.experimental import pallas as pl
from jax.experimental.pallas import tpu as pltpu
from jax.sharding import PartitionSpec as P

KHALF = 10
SHIFT = 6
REACH = 6
NBASIS = 28
ROWS = 64
COLS = 512
PLANE = 8
SPAN = 96
SLOTS = 32
BLOCK = 128
BLOCKS = COLS // BLOCK
PITCH = 72
TALL = BLOCKS * ROWS
HALF = 32
DEPTH = 64

SIGMAS = (1.0, 2.0, 4.0)
DEGREES = (4, 2, 2)
RIDGE = 0.01
LIMIT = 32 * 1024 * 1024

SMEM = pl.BlockSpec(memory_space=pltpu.SMEM)
VMEM = pl.BlockSpec(memory_space=pltpu.VMEM)


def factor_table():
    listed = []
    for width_sigma, degree in zip(SIGMAS, DEGREES):
        for exponent in range(degree + 1):
            values = [
                math.exp(-(offset * offset) / (2.0 * width_sigma * width_sigma))
                * (offset / KHALF) ** exponent
                for offset in range(-KHALF, KHALF + 1)
            ]
            scale_norm = math.sqrt(sum((entry * entry for entry in values)))
            listed.append([entry / scale_norm for entry in values])
    return np.array(listed, dtype=np.float32)


def row_factors_by_column_factor():
    groups = []
    first = 0
    for degree in DEGREES:
        for power_col in range(degree + 1):
            groups.append([first + power_row for power_row in range(degree + 1 - power_col)])
        first += degree + 1
    return groups


GROUPS = row_factors_by_column_factor()
NFACTORS = len(GROUPS)


def split_constant(values):
    high = values.astype(ml_dtypes.bfloat16)
    low = (values - high.astype(np.float32)).astype(ml_dtypes.bfloat16)
    return high, low


def column_tables():
    table = factor_table()
    distance = np.arange(2 * BLOCK)[:, None] - np.arange(BLOCK)[None, :]
    bands = np.zeros((2 * BLOCK, NFACTORS, BLOCK), np.float32)
    for offset in range(2 * KHALF + 1):
        bands += table[None, :, offset, None] * (distance == offset)[:, None, :]
    return split_constant(bands.reshape(2 * BLOCK, NFACTORS * BLOCK))


def row_tables():
    table = factor_table()
    distance = np.arange(DEPTH)[None, :] - np.arange(HALF)[:, None]
    planes = [index for group in GROUPS for index in group]
    bands = np.zeros((len(planes), HALF, DEPTH), np.float32)
    for offset in range(2 * KHALF + 1):
        bands += table[planes, offset][:, None, None] * (distance == offset)[None]
    high, low = split_constant(bands.reshape(len(planes) * HALF, DEPTH))
    return np.concatenate([high, high, low], axis=1)


def split(values):
    high = values.astype(jnp.bfloat16)
    low = (values - high.astype(jnp.float32)).astype(jnp.bfloat16)
    return high, low


def put_plane(planes, slot, row, values):
    for block in range(BLOCKS):
        at = (block * SLOTS + slot) * PITCH + row
        planes[at : at + values.shape[0], :] = values[:, block * BLOCK : (block + 1) * BLOCK]


def spread_kernel(tile, copies):
    for copy in range(PLANE):
        for block in range(BLOCKS):
            copies[copy, block * ROWS : (block + 1) * ROWS, :] = tile[
                :, block * BLOCK : (block + 1) * BLOCK
            ]


def spread(tile):
    return pl.pallas_call(
        spread_kernel,
        out_shape=jax.ShapeDtypeStruct((PLANE, TALL, BLOCK), jnp.float32),
        in_specs=[VMEM],
        out_specs=VMEM,
        compiler_params=pltpu.CompilerParams(vmem_limit_bytes=LIMIT),
        name="spread",
    )(tile)


def serve_kernel(window, own, below, above, piece_own, piece_up, piece_down):
    base = (lax.axis_index("visit") // PLANE) * PLANE
    for entries, piece in ((own, piece_own), (below, piece_down), (above, piece_up)):
        start = (entries[0, 0] - base) * ROWS + entries[0, 1] - KHALF
        first = lax.shift_right_arithmetic(start, 3)
        for part in range(SPAN // 8):
            index = first + part
            inside = jnp.logical_and(index >= 0, index < PLANE * ROWS // 8)
            index = jnp.clip(index, 0, PLANE * ROWS // 8 - 1)
            tile = lax.shift_right_logical(index, 3)
            row = pl.multiple_of(lax.bitwise_and(index, 7) * 8, 8)
            for block in range(BLOCKS):
                rows = window[tile, pl.ds(block * ROWS + row, 8), :]
                piece[8 * part : 8 * part + 8, block * BLOCK : (block + 1) * BLOCK] = jnp.where(
                    inside, rows, 0.0
                )


def serve(window, own, below, above):
    shape = jax.ShapeDtypeStruct((SPAN, COLS), jnp.float32)
    return pl.pallas_call(
        serve_kernel,
        out_shape=(shape, shape, shape),
        in_specs=[VMEM, SMEM, SMEM, SMEM],
        out_specs=(VMEM, VMEM, VMEM),
        compiler_params=pltpu.CompilerParams(vmem_limit_bytes=LIMIT),
        name="serve",
    )(window, own, below, above)


def basis_kernel(
    piece_a, piece_b, piece_c, science, weight, col_high, col_low, row_table, entries,
    planes, gram_out,
    high_rows, low_rows,
):
    remainder = lax.bitwise_and(entries[0, 1] + SHIFT, 7)
    rows = piece_a[...] + piece_b[...] + piece_c[...]
    rows = pltpu.roll(rows, lax.rem(SPAN - remainder, SPAN), axis=0)
    padded = jnp.concatenate([rows, jnp.zeros((SPAN, BLOCK), jnp.float32)], axis=1)
    cutout = pltpu.roll(padded, KHALF - entries[0, 2], axis=1)
    cut_high, cut_low = split(cutout)
    for block in range(COLS // BLOCK):
        cols = slice(block * BLOCK, (block + 2) * BLOCK)
        both = jnp.concatenate([cut_high[:, cols], cut_low[:, cols]], axis=0)
        main = jnp.dot(both, col_high[...], preferred_element_type=jnp.float32)
        rest = jnp.dot(cut_high[:, cols], col_low[...], preferred_element_type=jnp.float32)
        across = main[:SPAN] + main[SPAN:] + rest
        across_high, across_low = split(across)
        for factor in range(NFACTORS):
            take = slice(factor * BLOCK, (factor + 1) * BLOCK)
            put = slice(block * BLOCK, (block + 1) * BLOCK)
            high_rows[factor, :, put] = across_high[:, take]
            low_rows[factor, :, put] = across_low[:, take]
    root = jnp.sqrt(weight[...])
    first = 0
    for factor, group in enumerate(GROUPS):
        table = row_table[first * HALF : (first + len(group)) * HALF, :]
        for half in range(ROWS // HALF):
            take = slice(half * HALF, half * HALF + DEPTH)
            high = high_rows[factor, take, :]
            stacked = jnp.concatenate([high, low_rows[factor, take, :], high], axis=0)
            out = jnp.dot(table, stacked, preferred_element_type=jnp.float32)
            for member in range(len(group)):
                scaled = (
                    out[member * HALF : (member + 1) * HALF] * root[half * HALF : (half + 1) * HALF]
                )
                put_plane(planes, first + member, half * HALF, scaled)
        first += len(group)
    put_plane(planes, NBASIS - 1, 0, root)
    put_plane(planes, NBASIS, 0, root * science[...])
    for slot in range(NBASIS + 1, SLOTS):
        put_plane(planes, slot, 0, jnp.zeros((ROWS, COLS), jnp.float32))
    def gram_step(chunk, total):
        highs, lows = [], []
        for inner in range(8):
            for block in range(BLOCKS):
                row = block * SLOTS * PITCH + chunk * 8 + inner
                high, low = split(planes[pl.ds(row, SLOTS, stride=PITCH), :])
                highs.append(high)
                lows.append(low)
        high = jnp.concatenate(highs, axis=1)
        low = jnp.concatenate(lows, axis=1)
        both = jnp.concatenate([high, low], axis=0)
        return total + lax.dot_general(
            high, both, (((1,), (1,)), ((), ())), preferred_element_type=jnp.float32
        )

    total = lax.fori_loop(0, ROWS // 8, gram_step, jnp.zeros((SLOTS, 2 * SLOTS), jnp.float32))
    gram_out[...] = jnp.concatenate(
        [total, jnp.zeros((SLOTS, BLOCK - 2 * SLOTS), jnp.float32)], axis=1
    )


def basis(pieces, science, weight, entries):
    col_high, col_low = column_tables()
    return pl.pallas_call(
        basis_kernel,
        out_shape=(
            jax.ShapeDtypeStruct((BLOCKS * SLOTS * PITCH, BLOCK), jnp.float32),
            jax.ShapeDtypeStruct((SLOTS, BLOCK), jnp.float32),
        ),
        in_specs=[VMEM] * 8 + [SMEM],
        out_specs=(VMEM, VMEM),
        scratch_shapes=[
            pltpu.VMEM((NFACTORS, SPAN, COLS), jnp.bfloat16),
            pltpu.VMEM((NFACTORS, SPAN, COLS), jnp.bfloat16),
        ],
        compiler_params=pltpu.CompilerParams(vmem_limit_bytes=LIMIT),
        name="basis",
    )(
        *pieces, science, weight, jnp.asarray(col_high), jnp.asarray(col_low),
        jnp.asarray(row_tables()), entries,
    )


def solve_kernel(grams, planes, entries, difference, placed):
    total = grams[0] + grams[1] + grams[2] + grams[3]
    cross = total[:, SLOTS : 2 * SLOTS]
    normal = total[:, :SLOTS] + cross + cross.T
    row_id = lax.broadcasted_iota(jnp.int32, (SLOTS, SLOTS), 0)
    col_id = lax.broadcasted_iota(jnp.int32, (SLOTS, SLOTS), 1)
    diagonal = jnp.logical_and(row_id == col_id, row_id < NBASIS)
    trace = jnp.sum(jnp.where(diagonal, normal, 0.0), keepdims=True)
    matrix = normal + jnp.where(diagonal, RIDGE * trace / NBASIS, 0.0)
    for step in range(NBASIS):
        row = matrix[step : step + 1, :]
        inverse = 1.0 / row[:, step : step + 1]
        scaled = row * inverse
        column = jnp.where(row_id[:, :1] == step, 0.0, matrix[:, step : step + 1])
        matrix = jnp.where(row_id == step, scaled, matrix - column * scaled)
    answer = jnp.broadcast_to(matrix[:, NBASIS : NBASIS + 1], (SLOTS, BLOCK))
    for block in range(BLOCKS):
        at = (block * SLOTS + NBASIS) * PITCH
        total = planes[at : at + ROWS, :]
        for plane in range(NBASIS):
            factor = jnp.broadcast_to(answer[plane : plane + 1, :], (ROWS, BLOCK))
            at = (block * SLOTS + plane) * PITCH
            total = total - factor * planes[at : at + ROWS, :]
        difference[:, block * BLOCK : (block + 1) * BLOCK] = total
    row_move, col_move = entries[0, 1], entries[0, 2]
    moved = pltpu.roll(difference[...], lax.rem(row_move + ROWS, ROWS), axis=0)
    moved = pltpu.roll(moved, lax.rem(col_move + COLS, COLS), axis=1)
    from_row = lax.broadcasted_iota(jnp.int32, (ROWS, COLS), 0) - row_move
    from_col = lax.broadcasted_iota(jnp.int32, (ROWS, COLS), 1) - col_move
    inside = (from_row >= 0) & (from_row < ROWS) & (from_col >= 0) & (from_col < COLS)
    placed[...] = jnp.where(inside, moved, 0.0)


def solve(grams, planes, entries):
    shape = jax.ShapeDtypeStruct((ROWS, COLS), jnp.float32)
    return pl.pallas_call(
        solve_kernel,
        out_shape=(shape, shape),
        in_specs=[VMEM, VMEM, SMEM],
        out_specs=(VMEM, VMEM),
        compiler_params=pltpu.CompilerParams(vmem_limit_bytes=LIMIT),
        name="solve",
    )(grams, planes, entries)


def gather_kernel(stamp_own, stamp_below, stamp_above, own, below, above, tiles):
    base = (lax.axis_index("visit") // PLANE) * PLANE
    hits = [entries[0, 0] - base for entries in (own, below, above)]
    for tile in range(PLANE):
        total = jnp.zeros((ROWS, COLS), jnp.float32)
        count = jnp.float32(0.0)
        for hit, stamp in zip(hits, (stamp_own, stamp_below, stamp_above)):
            total = total + jnp.where(hit == tile, stamp[...], 0.0)
            count = count + jnp.where(hit == tile, 1.0, 0.0)
        for block in range(BLOCKS):
            tiles[tile, block * ROWS : (block + 1) * ROWS, :] = total[
                :, block * BLOCK : (block + 1) * BLOCK
            ]
        tiles[tile, TALL:, :] = jnp.full((8, BLOCK), count, jnp.float32)


def gather(stamps, own, below, above):
    return pl.pallas_call(
        gather_kernel,
        out_shape=jax.ShapeDtypeStruct((PLANE, TALL + 8, BLOCK), jnp.float32),
        in_specs=[VMEM] * 3 + [SMEM] * 3,
        out_specs=VMEM,
        compiler_params=pltpu.CompilerParams(vmem_limit_bytes=LIMIT),
        name="gather",
    )(*stamps, own, below, above)


def mean_kernel(parts, coadd):
    count = parts[0, TALL:, :]
    for index in range(1, PLANE):
        count = count + parts[index, TALL:, :]
    count = jnp.maximum(count[:1], 1.0)
    for block in range(BLOCKS):
        rows = slice(block * ROWS, (block + 1) * ROWS)
        total = parts[0, rows, :]
        for index in range(1, PLANE):
            total = total + parts[index, rows, :]
        coadd[:, block * BLOCK : (block + 1) * BLOCK] = total / count


def mean(parts):
    return pl.pallas_call(
        mean_kernel,
        out_shape=jax.ShapeDtypeStruct((ROWS, COLS), jnp.float32),
        in_specs=[VMEM],
        out_specs=VMEM,
        compiler_params=pltpu.CompilerParams(vmem_limit_bytes=LIMIT),
        name="mean",
    )(parts)


def shards(template, science, inverse_variance, intersections):
    visits = lax.axis_size("visit")
    groups = [list(range(first, first + PLANE)) for first in range(0, visits, PLANE)]
    upward = [(i, (i + PLANE) % visits) for i in range(visits)]
    downward = [(target, source) for source, target in upward]
    own = intersections[0]
    below = lax.ppermute(own, "visit", upward)
    above = lax.ppermute(own, "visit", downward)
    window = lax.all_to_all(spread(template[0]), "visit", 0, 0, axis_index_groups=groups)
    piece_own, piece_up, piece_down = serve(window, own, below, above)
    from_above = lax.ppermute(piece_down, "visit", downward)
    from_below = lax.ppermute(piece_up, "visit", upward)
    planes, gram = basis(
        (piece_own, from_above, from_below), science[0, 0], inverse_variance[0, 0], own
    )
    grams = lax.all_gather(gram, "patch")
    difference, placed = solve(grams, planes, own)
    stamp_below = lax.ppermute(placed, "visit", upward)
    stamp_above = lax.ppermute(placed, "visit", downward)
    tiles = gather((placed, stamp_below, stamp_above), own, below, above)
    parts = lax.all_to_all(tiles, "visit", 0, 0, axis_index_groups=groups)
    return (difference[None, None], mean(parts)[None])


def solution(mesh):
    in_specs = (
        P("patch", "visit", None),
        P("visit", "patch", None, None),
        P("visit", "patch", None, None),
        P("visit", "patch", None),
    )
    out_specs = (P("visit", "patch", None, None), P("patch", "visit", None))
    return jax.shard_map(shards, mesh=mesh, in_specs=in_specs, out_specs=out_specs, check_vma=False)
```

```python
import functools
import math

import jax
import jax.numpy as jnp
import ml_dtypes
import numpy as np
from jax import lax
from jax.experimental import pallas as pl
from jax.experimental.pallas import tpu as pltpu
from jax.sharding import PartitionSpec as P

KHALF = 10
SHIFT = 6
REACH = 6
NBASIS = 28
ROWS = 64
COLS = 512
PLANE = 8
SPAN = 96
SLOTS = 32
BLOCK = 128
BLOCKS = COLS // BLOCK
PITCH = 72
TALL = BLOCKS * ROWS
HALF = 32
CHUNK = 32
DEPTH = 64

SIGMAS = (1.0, 2.0, 4.0)
DEGREES = (4, 2, 2)
RIDGE = 0.01
LIMIT = 32 * 1024 * 1024

SMEM = pl.BlockSpec(memory_space=pltpu.SMEM)
VMEM = pl.BlockSpec(memory_space=pltpu.VMEM)


def factor_table():
    listed = []
    for width_sigma, degree in zip(SIGMAS, DEGREES):
        for exponent in range(degree + 1):
            values = [
                math.exp(-(offset * offset) / (2.0 * width_sigma * width_sigma))
                * (offset / KHALF) ** exponent
                for offset in range(-KHALF, KHALF + 1)
            ]
            scale_norm = math.sqrt(sum((entry * entry for entry in values)))
            listed.append([entry / scale_norm for entry in values])
    return np.array(listed, dtype=np.float32)


def row_factors_by_column_factor():
    groups = []
    first = 0
    for degree in DEGREES:
        for power_col in range(degree + 1):
            groups.append([first + power_row for power_row in range(degree + 1 - power_col)])
        first += degree + 1
    return groups


GROUPS = row_factors_by_column_factor()
NFACTORS = len(GROUPS)


def split_constant(values):
    high = values.astype(ml_dtypes.bfloat16)
    low = (values - high.astype(np.float32)).astype(ml_dtypes.bfloat16)
    return high, low


def column_tables():
    table = factor_table()
    distance = np.arange(2 * BLOCK)[:, None] - np.arange(BLOCK)[None, :]
    bands = np.zeros((2 * BLOCK, NFACTORS, BLOCK), np.float32)
    for offset in range(2 * KHALF + 1):
        bands += table[None, :, offset, None] * (distance == offset)[:, None, :]
    return split_constant(bands.reshape(2 * BLOCK, NFACTORS * BLOCK))


def row_tables():
    table = factor_table()
    distance = np.arange(DEPTH)[None, :] - np.arange(HALF)[:, None]
    planes = [index for group in GROUPS for index in group]
    bands = np.zeros((len(planes), HALF, DEPTH), np.float32)
    for offset in range(2 * KHALF + 1):
        bands += table[planes, offset][:, None, None] * (distance == offset)[None]
    high, low = split_constant(bands.reshape(len(planes) * HALF, DEPTH))
    return np.concatenate([high, high, low], axis=1)


def split(values):
    high = values.astype(jnp.bfloat16)
    low = (values - high.astype(jnp.float32)).astype(jnp.bfloat16)
    return high, low


def put_plane(planes, slot, row, values):
    for block in range(BLOCKS):
        at = (block * SLOTS + slot) * PITCH + row
        planes[at : at + values.shape[0], :] = values[:, block * BLOCK : (block + 1) * BLOCK]


def spread_kernel(tile, copies):
    for copy in range(PLANE):
        for block in range(BLOCKS):
            copies[copy, block * ROWS : (block + 1) * ROWS, :] = tile[
                :, block * BLOCK : (block + 1) * BLOCK
            ]


def spread(tile):
    return pl.pallas_call(
        spread_kernel,
        out_shape=jax.ShapeDtypeStruct((PLANE, TALL, BLOCK), jnp.float32),
        in_specs=[VMEM],
        out_specs=VMEM,
        compiler_params=pltpu.CompilerParams(vmem_limit_bytes=LIMIT),
        name="spread",
    )(tile)


def serve_kernel(window, own, below, above, piece_own, piece_up, piece_down):
    base = (lax.axis_index("visit") // PLANE) * PLANE
    for entries, piece in ((own, piece_own), (below, piece_down), (above, piece_up)):
        start = (entries[0, 0] - base) * ROWS + entries[0, 1] - KHALF
        first = lax.shift_right_arithmetic(start, 3)
        for part in range(SPAN // 8):
            index = first + part
            inside = jnp.logical_and(index >= 0, index < PLANE * ROWS // 8)
            index = jnp.clip(index, 0, PLANE * ROWS // 8 - 1)
            tile = lax.shift_right_logical(index, 3)
            row = pl.multiple_of(lax.bitwise_and(index, 7) * 8, 8)
            for block in range(BLOCKS):
                rows = window[tile, pl.ds(block * ROWS + row, 8), :]
                piece[8 * part : 8 * part + 8, block * BLOCK : (block + 1) * BLOCK] = jnp.where(
                    inside, rows, 0.0
                )


def serve(window, own, below, above):
    shape = jax.ShapeDtypeStruct((SPAN, COLS), jnp.float32)
    return pl.pallas_call(
        serve_kernel,
        out_shape=(shape, shape, shape),
        in_specs=[VMEM, SMEM, SMEM, SMEM],
        out_specs=(VMEM, VMEM, VMEM),
        compiler_params=pltpu.CompilerParams(vmem_limit_bytes=LIMIT),
        name="serve",
    )(window, own, below, above)


def basis_kernel(
    piece_a, piece_b, piece_c, science, weight, col_high, col_low, row_table, entries,
    planes, gram_out,
    high_rows, low_rows,
):
    remainder = lax.bitwise_and(entries[0, 1] + SHIFT, 7)
    rows = piece_a[...] + piece_b[...] + piece_c[...]
    rows = pltpu.roll(rows, lax.rem(SPAN - remainder, SPAN), axis=0)
    padded = jnp.concatenate([rows, jnp.zeros((SPAN, BLOCK), jnp.float32)], axis=1)
    cutout = pltpu.roll(padded, KHALF - entries[0, 2], axis=1)
    cut_high, cut_low = split(cutout)
    for block in range(COLS // BLOCK):
        cols = slice(block * BLOCK, (block + 2) * BLOCK)
        both = jnp.concatenate([cut_high[:, cols], cut_low[:, cols]], axis=0)
        main = jnp.dot(both, col_high[...], preferred_element_type=jnp.float32)
        rest = jnp.dot(cut_high[:, cols], col_low[...], preferred_element_type=jnp.float32)
        across = main[:SPAN] + main[SPAN:] + rest
        across_high, across_low = split(across)
        for factor in range(NFACTORS):
            take = slice(factor * BLOCK, (factor + 1) * BLOCK)
            put = slice(block * BLOCK, (block + 1) * BLOCK)
            high_rows[factor, :, put] = across_high[:, take]
            low_rows[factor, :, put] = across_low[:, take]
    root = jnp.sqrt(weight[...])
    first = 0
    for factor, group in enumerate(GROUPS):
        table = row_table[first * HALF : (first + len(group)) * HALF, :]
        for half in range(ROWS // HALF):
            take = slice(half * HALF, half * HALF + DEPTH)
            high = high_rows[factor, take, :]
            stacked = jnp.concatenate([high, low_rows[factor, take, :], high], axis=0)
            out = jnp.dot(table, stacked, preferred_element_type=jnp.float32)
            for member in range(len(group)):
                scaled = (
                    out[member * HALF : (member + 1) * HALF] * root[half * HALF : (half + 1) * HALF]
                )
                put_plane(planes, first + member, half * HALF, scaled)
        first += len(group)
    put_plane(planes, NBASIS - 1, 0, root)
    put_plane(planes, NBASIS, 0, root * science[...])
    for slot in range(NBASIS + 1, SLOTS):
        put_plane(planes, slot, 0, jnp.zeros((ROWS, COLS), jnp.float32))
    def gram_step(chunk, total):
        highs, lows = [], []
        for inner in range(CHUNK):
            for block in range(BLOCKS):
                row = block * SLOTS * PITCH + chunk * CHUNK + inner
                high, low = split(planes[pl.ds(row, SLOTS, stride=PITCH), :])
                highs.append(high)
                lows.append(low)
        high = jnp.concatenate(highs, axis=1)
        low = jnp.concatenate(lows, axis=1)
        both = jnp.concatenate([high, low], axis=0)
        return total + lax.dot_general(
            high, both, (((1,), (1,)), ((), ())), preferred_element_type=jnp.float32
        )

    total = lax.fori_loop(0, ROWS // CHUNK, gram_step, jnp.zeros((SLOTS, 2 * SLOTS), jnp.float32))
    gram_out[...] = jnp.concatenate(
        [total, jnp.zeros((SLOTS, BLOCK - 2 * SLOTS), jnp.float32)], axis=1
    )


def basis(pieces, science, weight, entries):
    col_high, col_low = column_tables()
    return pl.pallas_call(
        basis_kernel,
        out_shape=(
            jax.ShapeDtypeStruct((BLOCKS * SLOTS * PITCH, BLOCK), jnp.float32),
            jax.ShapeDtypeStruct((SLOTS, BLOCK), jnp.float32),
        ),
        in_specs=[VMEM] * 8 + [SMEM],
        out_specs=(VMEM, VMEM),
        scratch_shapes=[
            pltpu.VMEM((NFACTORS, SPAN, COLS), jnp.bfloat16),
            pltpu.VMEM((NFACTORS, SPAN, COLS), jnp.bfloat16),
        ],
        compiler_params=pltpu.CompilerParams(vmem_limit_bytes=LIMIT),
        name="basis",
    )(
        *pieces, science, weight, jnp.asarray(col_high), jnp.asarray(col_low),
        jnp.asarray(row_tables()), entries,
    )


def solve_kernel(grams, planes, entries, difference, placed):
    total = grams[0] + grams[1] + grams[2] + grams[3]
    cross = total[:, SLOTS : 2 * SLOTS]
    normal = total[:, :SLOTS] + cross + cross.T
    row_id = lax.broadcasted_iota(jnp.int32, (SLOTS, SLOTS), 0)
    col_id = lax.broadcasted_iota(jnp.int32, (SLOTS, SLOTS), 1)
    diagonal = jnp.logical_and(row_id == col_id, row_id < NBASIS)
    trace = jnp.sum(jnp.where(diagonal, normal, 0.0), keepdims=True)
    matrix = normal + jnp.where(diagonal, RIDGE * trace / NBASIS, 0.0)
    for step in range(0, NBASIS, 2):
        first = jnp.broadcast_to(matrix[:, step : step + 1], (SLOTS, SLOTS))
        second = jnp.broadcast_to(matrix[:, step + 1 : step + 2], (SLOTS, SLOTS))
        upper, lower = slice(step, step + 1), slice(step + 1, step + 2)
        inverse = 1.0 / (first[upper] * second[lower] - second[upper] * first[lower])
        row_upper = (second[lower] * matrix[upper] - second[upper] * matrix[lower]) * inverse
        row_lower = (first[upper] * matrix[lower] - first[lower] * matrix[upper]) * inverse
        others = matrix - first * row_upper - second * row_lower
        matrix = jnp.where(
            row_id == step, row_upper, jnp.where(row_id == step + 1, row_lower, others)
        )
    answer = jnp.broadcast_to(matrix[:, NBASIS : NBASIS + 1], (SLOTS, BLOCK))
    for block in range(BLOCKS):
        at = (block * SLOTS + NBASIS) * PITCH
        total = planes[at : at + ROWS, :]
        for plane in range(NBASIS):
            factor = jnp.broadcast_to(answer[plane : plane + 1, :], (ROWS, BLOCK))
            at = (block * SLOTS + plane) * PITCH
            total = total - factor * planes[at : at + ROWS, :]
        difference[:, block * BLOCK : (block + 1) * BLOCK] = total
    row_move, col_move = entries[0, 1], entries[0, 2]
    moved = pltpu.roll(difference[...], lax.rem(row_move + ROWS, ROWS), axis=0)
    moved = pltpu.roll(moved, lax.rem(col_move + COLS, COLS), axis=1)
    from_row = lax.broadcasted_iota(jnp.int32, (ROWS, COLS), 0) - row_move
    from_col = lax.broadcasted_iota(jnp.int32, (ROWS, COLS), 1) - col_move
    inside = (from_row >= 0) & (from_row < ROWS) & (from_col >= 0) & (from_col < COLS)
    placed[...] = jnp.where(inside, moved, 0.0)


def solve(grams, planes, entries):
    shape = jax.ShapeDtypeStruct((ROWS, COLS), jnp.float32)
    return pl.pallas_call(
        solve_kernel,
        out_shape=(shape, shape),
        in_specs=[VMEM, VMEM, SMEM],
        out_specs=(VMEM, VMEM),
        compiler_params=pltpu.CompilerParams(vmem_limit_bytes=LIMIT),
        name="solve",
    )(grams, planes, entries)


def gather_kernel(stamp_own, stamp_below, stamp_above, own, below, above, tiles):
    visit = lax.axis_index("visit")
    base = (visit // PLANE) * PLANE
    hits = [entries[0, 0] - base for entries in (own, below, above)]
    hits[1] = jnp.where(visit >= PLANE, hits[1], -1)
    hits[2] = jnp.where(visit < lax.axis_size("visit") - PLANE, hits[2], -1)
    for tile in range(PLANE):
        total = jnp.zeros((ROWS, COLS), jnp.float32)
        count = jnp.float32(0.0)
        for hit, stamp in zip(hits, (stamp_own, stamp_below, stamp_above)):
            total = total + jnp.where(hit == tile, stamp[...], 0.0)
            count = count + jnp.where(hit == tile, 1.0, 0.0)
        for block in range(BLOCKS):
            tiles[tile, block * ROWS : (block + 1) * ROWS, :] = total[
                :, block * BLOCK : (block + 1) * BLOCK
            ]
        tiles[tile, TALL:, :] = jnp.full((8, BLOCK), count, jnp.float32)


def gather(stamps, own, below, above):
    return pl.pallas_call(
        gather_kernel,
        out_shape=jax.ShapeDtypeStruct((PLANE, TALL + 8, BLOCK), jnp.float32),
        in_specs=[VMEM] * 3 + [SMEM] * 3,
        out_specs=VMEM,
        compiler_params=pltpu.CompilerParams(vmem_limit_bytes=LIMIT),
        name="gather",
    )(*stamps, own, below, above)


def mean_kernel(parts, coadd):
    count = parts[0, TALL:, :]
    for index in range(1, PLANE):
        count = count + parts[index, TALL:, :]
    count = jnp.maximum(count[:1], 1.0)
    for block in range(BLOCKS):
        rows = slice(block * ROWS, (block + 1) * ROWS)
        total = parts[0, rows, :]
        for index in range(1, PLANE):
            total = total + parts[index, rows, :]
        coadd[:, block * BLOCK : (block + 1) * BLOCK] = total / count


def mean(parts):
    return pl.pallas_call(
        mean_kernel,
        out_shape=jax.ShapeDtypeStruct((ROWS, COLS), jnp.float32),
        in_specs=[VMEM],
        out_specs=VMEM,
        compiler_params=pltpu.CompilerParams(vmem_limit_bytes=LIMIT),
        name="mean",
    )(parts)


def shards(template, science, inverse_variance, intersections):
    visits = lax.axis_size("visit")
    groups = [list(range(first, first + PLANE)) for first in range(0, visits, PLANE)]
    upward = [(i, i + PLANE) for i in range(visits - PLANE)]
    downward = [(target, source) for source, target in upward]
    own = intersections[0]
    below = lax.ppermute(own, "visit", upward)
    above = lax.ppermute(own, "visit", downward)
    window = lax.all_to_all(spread(template[0]), "visit", 0, 0, axis_index_groups=groups)
    piece_own, piece_up, piece_down = serve(window, own, below, above)
    from_above = lax.ppermute(piece_down, "visit", downward)
    from_below = lax.ppermute(piece_up, "visit", upward)
    planes, gram = basis(
        (piece_own, from_above, from_below), science[0, 0], inverse_variance[0, 0], own
    )
    grams = lax.all_gather(gram, "patch")
    difference, placed = solve(grams, planes, own)
    stamp_below = lax.ppermute(placed, "visit", upward)
    stamp_above = lax.ppermute(placed, "visit", downward)
    tiles = gather((placed, stamp_below, stamp_above), own, below, above)
    parts = lax.all_to_all(tiles, "visit", 0, 0, axis_index_groups=groups)
    return (difference[None, None], mean(parts)[None])


def solution(mesh):
    in_specs = (
        P("patch", "visit", None),
        P("visit", "patch", None, None),
        P("visit", "patch", None, None),
        P("visit", "patch", None),
    )
    out_specs = (P("visit", "patch", None, None), P("patch", "visit", None))
    return jax.shard_map(shards, mesh=mesh, in_specs=in_specs, out_specs=out_specs, check_vma=False)
```

```python
import functools
import math

import jax
import jax.numpy as jnp
import ml_dtypes
import numpy as np
from jax import lax
from jax.experimental import pallas as pl
from jax.experimental.pallas import tpu as pltpu
from jax.sharding import PartitionSpec as P

KHALF = 10
SHIFT = 6
REACH = 6
NBASIS = 28
ROWS = 64
COLS = 512
PLANE = 8
LINE = 4
SPAN = 96
SLOTS = 32
BLOCK = 128
BLOCKS = COLS // BLOCK
PITCH = 72
TALL = BLOCKS * ROWS
NOTED = TALL + 8
HALF = 32
CHUNK = 32
DEPTH = 64

SIGMAS = (1.0, 2.0, 4.0)
DEGREES = (4, 2, 2)
RIDGE = 0.01
LIMIT = 32 * 1024 * 1024

SMEM = pl.BlockSpec(memory_space=pltpu.SMEM)
VMEM = pl.BlockSpec(memory_space=pltpu.VMEM)


def factor_table():
    listed = []
    for width_sigma, degree in zip(SIGMAS, DEGREES):
        for exponent in range(degree + 1):
            values = [
                math.exp(-(offset * offset) / (2.0 * width_sigma * width_sigma))
                * (offset / KHALF) ** exponent
                for offset in range(-KHALF, KHALF + 1)
            ]
            scale_norm = math.sqrt(sum((entry * entry for entry in values)))
            listed.append([entry / scale_norm for entry in values])
    return np.array(listed, dtype=np.float32)


def row_factors_by_column_factor():
    groups = []
    first = 0
    for degree in DEGREES:
        for power_col in range(degree + 1):
            groups.append([first + power_row for power_row in range(degree + 1 - power_col)])
        first += degree + 1
    return groups


GROUPS = row_factors_by_column_factor()
NFACTORS = len(GROUPS)


def split_constant(values):
    high = values.astype(ml_dtypes.bfloat16)
    low = (values - high.astype(np.float32)).astype(ml_dtypes.bfloat16)
    return high, low


def column_tables():
    table = factor_table()
    distance = np.arange(2 * BLOCK)[:, None] - np.arange(BLOCK)[None, :]
    bands = np.zeros((2 * BLOCK, NFACTORS, BLOCK), np.float32)
    for offset in range(2 * KHALF + 1):
        bands += table[None, :, offset, None] * (distance == offset)[:, None, :]
    return split_constant(bands.reshape(2 * BLOCK, NFACTORS * BLOCK))


def row_tables():
    table = factor_table()
    distance = np.arange(DEPTH)[None, :] - np.arange(HALF)[:, None]
    planes = [index for group in GROUPS for index in group]
    bands = np.zeros((len(planes), HALF, DEPTH), np.float32)
    for offset in range(2 * KHALF + 1):
        bands += table[planes, offset][:, None, None] * (distance == offset)[None]
    high, low = split_constant(bands.reshape(len(planes) * HALF, DEPTH))
    return np.concatenate([high, high, low], axis=1)


def split(values):
    high = values.astype(jnp.bfloat16)
    low = (values - high.astype(jnp.float32)).astype(jnp.bfloat16)
    return high, low


def put_plane(planes, slot, row, values):
    for block in range(BLOCKS):
        at = (block * SLOTS + slot) * PITCH + row
        planes[at : at + values.shape[0], :] = values[:, block * BLOCK : (block + 1) * BLOCK]


def spread_kernel(tile, copies):
    for copy in range(PLANE):
        for block in range(BLOCKS):
            copies[copy, block * ROWS : (block + 1) * ROWS, :] = tile[
                :, block * BLOCK : (block + 1) * BLOCK
            ]


def spread(tile):
    return pl.pallas_call(
        spread_kernel,
        out_shape=jax.ShapeDtypeStruct((PLANE, TALL, BLOCK), jnp.float32),
        in_specs=[VMEM],
        out_specs=VMEM,
        compiler_params=pltpu.CompilerParams(vmem_limit_bytes=LIMIT),
        name="spread",
    )(tile)


def serve_kernel(window, own, below, above, piece_own, piece_up, piece_down):
    base = (lax.axis_index("visit") // PLANE) * PLANE
    for entries, piece in ((own, piece_own), (below, piece_down), (above, piece_up)):
        start = (entries[0, 0] - base) * ROWS + entries[0, 1] - KHALF
        first = lax.shift_right_arithmetic(start, 3)
        for part in range(SPAN // 8):
            index = first + part
            inside = jnp.logical_and(index >= 0, index < PLANE * ROWS // 8)
            index = jnp.clip(index, 0, PLANE * ROWS // 8 - 1)
            tile = lax.shift_right_logical(index, 3)
            row = pl.multiple_of(lax.bitwise_and(index, 7) * 8, 8)
            for block in range(BLOCKS):
                rows = window[tile, pl.ds(block * ROWS + row, 8), :]
                piece[8 * part : 8 * part + 8, block * BLOCK : (block + 1) * BLOCK] = jnp.where(
                    inside, rows, 0.0
                )


def serve(window, own, below, above):
    shape = jax.ShapeDtypeStruct((SPAN, COLS), jnp.float32)
    return pl.pallas_call(
        serve_kernel,
        out_shape=(shape, shape, shape),
        in_specs=[VMEM, SMEM, SMEM, SMEM],
        out_specs=(VMEM, VMEM, VMEM),
        compiler_params=pltpu.CompilerParams(vmem_limit_bytes=LIMIT),
        name="serve",
    )(window, own, below, above)


def basis_kernel(
    piece_a, piece_b, piece_c, science, weight, col_high, col_low, row_table, entries,
    planes, gram_out,
    high_rows, low_rows,
):
    remainder = lax.bitwise_and(entries[0, 1] + SHIFT, 7)
    rows = piece_a[...] + piece_b[...] + piece_c[...]
    rows = pltpu.roll(rows, lax.rem(SPAN - remainder, SPAN), axis=0)
    padded = jnp.concatenate([rows, jnp.zeros((SPAN, BLOCK), jnp.float32)], axis=1)
    cutout = pltpu.roll(padded, KHALF - entries[0, 2], axis=1)
    cut_high, cut_low = split(cutout)
    for block in range(COLS // BLOCK):
        cols = slice(block * BLOCK, (block + 2) * BLOCK)
        both = jnp.concatenate([cut_high[:, cols], cut_low[:, cols]], axis=0)
        main = jnp.dot(both, col_high[...], preferred_element_type=jnp.float32)
        rest = jnp.dot(cut_high[:, cols], col_low[...], preferred_element_type=jnp.float32)
        across = main[:SPAN] + main[SPAN:] + rest
        across_high, across_low = split(across)
        for factor in range(NFACTORS):
            take = slice(factor * BLOCK, (factor + 1) * BLOCK)
            put = slice(block * BLOCK, (block + 1) * BLOCK)
            high_rows[factor, :, put] = across_high[:, take]
            low_rows[factor, :, put] = across_low[:, take]
    root = jnp.sqrt(weight[...])
    first = 0
    for factor, group in enumerate(GROUPS):
        table = row_table[first * HALF : (first + len(group)) * HALF, :]
        for half in range(ROWS // HALF):
            take = slice(half * HALF, half * HALF + DEPTH)
            high = high_rows[factor, take, :]
            stacked = jnp.concatenate([high, low_rows[factor, take, :], high], axis=0)
            out = jnp.dot(table, stacked, preferred_element_type=jnp.float32)
            for member in range(len(group)):
                scaled = (
                    out[member * HALF : (member + 1) * HALF] * root[half * HALF : (half + 1) * HALF]
                )
                put_plane(planes, first + member, half * HALF, scaled)
        first += len(group)
    put_plane(planes, NBASIS - 1, 0, root)
    put_plane(planes, NBASIS, 0, root * science[...])
    for slot in range(NBASIS + 1, SLOTS):
        put_plane(planes, slot, 0, jnp.zeros((ROWS, COLS), jnp.float32))
    def gram_step(chunk, total):
        highs, lows = [], []
        for inner in range(CHUNK):
            for block in range(BLOCKS):
                row = block * SLOTS * PITCH + chunk * CHUNK + inner
                high, low = split(planes[pl.ds(row, SLOTS, stride=PITCH), :])
                highs.append(high)
                lows.append(low)
        high = jnp.concatenate(highs, axis=1)
        low = jnp.concatenate(lows, axis=1)
        both = jnp.concatenate([high, low], axis=0)
        return total + lax.dot_general(
            high, both, (((1,), (1,)), ((), ())), preferred_element_type=jnp.float32
        )

    total = lax.fori_loop(0, ROWS // CHUNK, gram_step, jnp.zeros((SLOTS, 2 * SLOTS), jnp.float32))
    gram_out[...] = jnp.concatenate(
        [total, jnp.zeros((SLOTS, BLOCK - 2 * SLOTS), jnp.float32)], axis=1
    )


def basis(pieces, science, weight, entries):
    col_high, col_low = column_tables()
    return pl.pallas_call(
        basis_kernel,
        out_shape=(
            jax.ShapeDtypeStruct((BLOCKS * SLOTS * PITCH, BLOCK), jnp.float32),
            jax.ShapeDtypeStruct((SLOTS, BLOCK), jnp.float32),
        ),
        in_specs=[VMEM] * 8 + [SMEM],
        out_specs=(VMEM, VMEM),
        scratch_shapes=[
            pltpu.VMEM((NFACTORS, SPAN, COLS), jnp.bfloat16),
            pltpu.VMEM((NFACTORS, SPAN, COLS), jnp.bfloat16),
        ],
        compiler_params=pltpu.CompilerParams(vmem_limit_bytes=LIMIT),
        name="basis",
    )(
        *pieces, science, weight, jnp.asarray(col_high), jnp.asarray(col_low),
        jnp.asarray(row_tables()), entries,
    )


def solve_kernel(grams, planes, entries, difference, stamps):
    total = grams[0] + grams[1] + grams[2] + grams[3]
    cross = total[:, SLOTS : 2 * SLOTS]
    normal = total[:, :SLOTS] + cross + cross.T
    row_id = lax.broadcasted_iota(jnp.int32, (SLOTS, SLOTS), 0)
    col_id = lax.broadcasted_iota(jnp.int32, (SLOTS, SLOTS), 1)
    diagonal = jnp.logical_and(row_id == col_id, row_id < NBASIS)
    trace = jnp.sum(jnp.where(diagonal, normal, 0.0), keepdims=True)
    matrix = normal + jnp.where(diagonal, RIDGE * trace / NBASIS, 0.0)
    for step in range(0, NBASIS, 2):
        first = jnp.broadcast_to(matrix[:, step : step + 1], (SLOTS, SLOTS))
        second = jnp.broadcast_to(matrix[:, step + 1 : step + 2], (SLOTS, SLOTS))
        upper, lower = slice(step, step + 1), slice(step + 1, step + 2)
        inverse = 1.0 / (first[upper] * second[lower] - second[upper] * first[lower])
        row_upper = (second[lower] * matrix[upper] - second[upper] * matrix[lower]) * inverse
        row_lower = (first[upper] * matrix[lower] - first[lower] * matrix[upper]) * inverse
        others = matrix - first * row_upper - second * row_lower
        matrix = jnp.where(
            row_id == step, row_upper, jnp.where(row_id == step + 1, row_lower, others)
        )
    answer = jnp.broadcast_to(matrix[:, NBASIS : NBASIS + 1], (SLOTS, BLOCK))
    for block in range(BLOCKS):
        at = (block * SLOTS + NBASIS) * PITCH
        total = planes[at : at + ROWS, :]
        for plane in range(NBASIS):
            factor = jnp.broadcast_to(answer[plane : plane + 1, :], (ROWS, BLOCK))
            at = (block * SLOTS + plane) * PITCH
            total = total - factor * planes[at : at + ROWS, :]
        difference[:, block * BLOCK : (block + 1) * BLOCK] = total
    row_move, col_move = entries[0, 1], entries[0, 2]
    moved = pltpu.roll(difference[...], lax.rem(row_move + ROWS, ROWS), axis=0)
    moved = pltpu.roll(moved, lax.rem(col_move + COLS, COLS), axis=1)
    from_row = lax.broadcasted_iota(jnp.int32, (ROWS, COLS), 0) - row_move
    from_col = lax.broadcasted_iota(jnp.int32, (ROWS, COLS), 1) - col_move
    inside = (from_row >= 0) & (from_row < ROWS) & (from_col >= 0) & (from_col < COLS)
    placed = jnp.where(inside, moved, 0.0)
    for place in range(LINE):
        mine = lax.bitwise_and(entries[0, 0], LINE - 1) == place
        for block in range(BLOCKS):
            stamps[place, block * ROWS : (block + 1) * ROWS, :] = jnp.where(
                mine, placed[:, block * BLOCK : (block + 1) * BLOCK], 0.0
            )
        stamps[place, TALL:, :] = jnp.full(
            (NOTED - TALL, BLOCK), entries[0, 0].astype(jnp.float32), jnp.float32
        )


def solve(grams, planes, entries):
    return pl.pallas_call(
        solve_kernel,
        out_shape=(
            jax.ShapeDtypeStruct((ROWS, COLS), jnp.float32),
            jax.ShapeDtypeStruct((LINE, NOTED, BLOCK), jnp.float32),
        ),
        in_specs=[VMEM, VMEM, SMEM],
        out_specs=(VMEM, VMEM),
        compiler_params=pltpu.CompilerParams(vmem_limit_bytes=LIMIT),
        name="solve",
    )(grams, planes, entries)


def gather_kernel(stamps, to_own, to_flip, to_next, to_far):
    visit = lax.axis_index("visit")
    even = lax.rem(visit // LINE, 2) == 0
    low = lax.rem(visit, LINE) < LINE // 2
    targets = (
        visit,
        jnp.where(even, visit + LINE, visit - LINE),
        jnp.where(even, visit - LINE, visit + LINE),
        jnp.where(low, visit + 2 * LINE, visit - 2 * LINE),
    )
    for target, out in zip(targets, (to_own, to_flip, to_next, to_far)):
        number = target.astype(jnp.float32)
        hits = [stamps[place, TALL:, :] == number for place in range(LINE)]
        count = jnp.zeros((NOTED - TALL, BLOCK), jnp.float32)
        for hit in hits:
            count = count + jnp.where(hit, 1.0, 0.0)
        out[TALL:, :] = count
        for block in range(BLOCKS):
            rows = slice(block * ROWS, (block + 1) * ROWS)
            total = jnp.zeros((ROWS, BLOCK), jnp.float32)
            for place in range(LINE):
                total = total + jnp.where(hits[place][:1], stamps[place, rows, :], 0.0)
            out[rows, :] = total


def gather(stamps):
    shape = jax.ShapeDtypeStruct((NOTED, BLOCK), jnp.float32)
    return pl.pallas_call(
        gather_kernel,
        out_shape=(shape,) * 4,
        in_specs=[VMEM],
        out_specs=(VMEM,) * 4,
        compiler_params=pltpu.CompilerParams(vmem_limit_bytes=LIMIT),
        name="gather",
    )(stamps)


def mean_kernel(part_a, part_b, part_c, part_d, coadd):
    parts = (part_a, part_b, part_c, part_d)
    count = sum(part[TALL:, :] for part in parts)
    count = jnp.maximum(count[:1], 1.0)
    for block in range(BLOCKS):
        rows = slice(block * ROWS, (block + 1) * ROWS)
        total = sum(part[rows, :] for part in parts)
        coadd[:, block * BLOCK : (block + 1) * BLOCK] = total / count


def mean(*parts):
    return pl.pallas_call(
        mean_kernel,
        out_shape=jax.ShapeDtypeStruct((ROWS, COLS), jnp.float32),
        in_specs=[VMEM] * 4,
        out_specs=VMEM,
        compiler_params=pltpu.CompilerParams(vmem_limit_bytes=LIMIT),
        name="mean",
    )(*parts)


def shards(template, science, inverse_variance, intersections):
    visits = lax.axis_size("visit")
    groups = [list(range(first, first + PLANE)) for first in range(0, visits, PLANE)]
    upward = [(i, i + PLANE) for i in range(visits - PLANE)]
    downward = [(target, source) for source, target in upward]
    own = intersections[0]
    below = lax.ppermute(own, "visit", upward)
    above = lax.ppermute(own, "visit", downward)
    window = lax.all_to_all(spread(template[0]), "visit", 0, 0, axis_index_groups=groups)
    piece_own, piece_up, piece_down = serve(window, own, below, above)
    from_above = lax.ppermute(piece_down, "visit", downward)
    from_below = lax.ppermute(piece_up, "visit", upward)
    planes, gram = basis(
        (piece_own, from_above, from_below), science[0, 0], inverse_variance[0, 0], own
    )
    grams = lax.all_gather(gram, "patch")
    difference, stamps = solve(grams, planes, own)
    lines = [list(range(first, first + LINE)) for first in range(0, visits, LINE)]
    to_own, to_flip, to_next, to_far = gather(
        lax.all_to_all(stamps, "visit", 0, 0, axis_index_groups=lines)
    )
    flip = [(i, i ^ LINE) for i in range(visits)]
    following = [(i, ((i + LINE) ^ LINE) - LINE) for i in range(LINE, visits - LINE)]
    far = [(i, i + 2 * LINE if i % LINE < LINE // 2 else i - 2 * LINE) for i in range(visits)]
    far = [(source, target) for source, target in far if 0 <= target < visits]
    from_far = lax.ppermute(to_far, "visit", far)
    from_next = lax.ppermute(to_next, "visit", following)
    from_flip = lax.ppermute(to_flip, "visit", flip)
    return (difference[None, None], mean(to_own, from_flip, from_next, from_far)[None])


def solution(mesh):
    in_specs = (
        P("patch", "visit", None),
        P("visit", "patch", None, None),
        P("visit", "patch", None, None),
        P("visit", "patch", None),
    )
    out_specs = (P("visit", "patch", None, None), P("patch", "visit", None))
    return jax.shard_map(shards, mesh=mesh, in_specs=in_specs, out_specs=out_specs, check_vma=False)
```

```python
import functools
import math

import jax
import jax.numpy as jnp
import ml_dtypes
import numpy as np
from jax import lax
from jax.experimental import pallas as pl
from jax.experimental.pallas import tpu as pltpu
from jax.sharding import PartitionSpec as P

KHALF = 10
SHIFT = 6
REACH = 6
NBASIS = 28
ROWS = 64
COLS = 512
PLANE = 8
LINE = 4
SPAN = 96
SLOTS = 32
BLOCK = 128
BLOCKS = COLS // BLOCK
PITCH = 72
TALL = BLOCKS * ROWS
NOTED = TALL + 8
HALF = 32
CHUNK = 32
DEPTH = 64

SIGMAS = (1.0, 2.0, 4.0)
DEGREES = (4, 2, 2)
RIDGE = 0.01
LIMIT = 32 * 1024 * 1024
BESIDE = 5
BESIDE_ROWS = -(-(NBASIS - 1) // BESIDE) * HALF

VMEM = pl.BlockSpec(memory_space=pltpu.VMEM)
HBM = pl.BlockSpec(memory_space=pltpu.HBM)


def factor_table():
    listed = []
    for width_sigma, degree in zip(SIGMAS, DEGREES):
        for exponent in range(degree + 1):
            values = [
                math.exp(-(offset * offset) / (2.0 * width_sigma * width_sigma))
                * (offset / KHALF) ** exponent
                for offset in range(-KHALF, KHALF + 1)
            ]
            scale_norm = math.sqrt(sum((entry * entry for entry in values)))
            listed.append([entry / scale_norm for entry in values])
    return np.array(listed, dtype=np.float32)


def row_factors_by_column_factor():
    groups = []
    first = 0
    for degree in DEGREES:
        for power_col in range(degree + 1):
            groups.append([first + power_row for power_row in range(degree + 1 - power_col)])
        first += degree + 1
    return groups


GROUPS = row_factors_by_column_factor()
NFACTORS = len(GROUPS)


def split_constant(values):
    high = values.astype(ml_dtypes.bfloat16)
    low = (values - high.astype(np.float32)).astype(ml_dtypes.bfloat16)
    return high, low


def tables():
    table = factor_table()
    distance = np.arange(2 * BLOCK)[:, None] - np.arange(BLOCK)[None, :]
    bands = np.zeros((2 * BLOCK, NFACTORS, BLOCK), np.float32)
    for offset in range(2 * KHALF + 1):
        bands += table[None, :, offset, None] * (distance == offset)[:, None, :]
    columns = split_constant(bands.reshape(2 * BLOCK, NFACTORS * BLOCK))
    distance = np.arange(DEPTH)[None, :] - np.arange(HALF)[:, None]
    chosen = [index for group in GROUPS for index in group]
    bands = np.zeros((len(chosen), HALF, DEPTH), np.float32)
    for offset in range(2 * KHALF + 1):
        bands += table[chosen, offset][:, None, None] * (distance == offset)[None]
    high, low = split_constant(bands)
    rows = np.zeros((BESIDE_ROWS, NFACTORS * BLOCK), ml_dtypes.bfloat16)
    for plane, band in enumerate(np.concatenate([high, high, low], axis=2)):
        row, lane = row_band_place(plane)
        rows[row : row + HALF, lane : lane + 3 * DEPTH] = band
    return np.concatenate([*columns, rows])


def row_band_place(plane):
    return plane // BESIDE * HALF, plane % BESIDE * 2 * BLOCK


def split(values):
    high = values.astype(jnp.bfloat16)
    low = (values - high.astype(jnp.float32)).astype(jnp.bfloat16)
    return high, low


def put_plane(planes, slot, row, values):
    for block in range(BLOCKS):
        at = (block * SLOTS + slot) * PITCH + row
        planes[at : at + values.shape[0], :] = values[:, block * BLOCK : (block + 1) * BLOCK]


def spread_kernel(tile, copies):
    for copy in range(PLANE):
        for block in range(BLOCKS):
            copies[copy, block * ROWS : (block + 1) * ROWS, :] = tile[
                :, block * BLOCK : (block + 1) * BLOCK
            ]


def spread(tile):
    return pl.pallas_call(
        spread_kernel,
        out_shape=jax.ShapeDtypeStruct((PLANE, TALL, BLOCK), jnp.float32),
        in_specs=[VMEM],
        out_specs=VMEM,
        compiler_params=pltpu.CompilerParams(vmem_limit_bytes=LIMIT),
        name="spread",
    )(tile)


def prepare_kernel(
    own, below, above, science, weight, table,
    requests, root, scaled_science, table_out,
):
    for index, entries in enumerate((own, below, above)):
        requests[index : index + 1, :] = entries[...]
    values = jnp.sqrt(weight[...])
    root[...] = values
    scaled_science[...] = values * science[...]
    table_out[...] = table[...]


def prepare(entries, science, weight, table):
    shape = jax.ShapeDtypeStruct((ROWS, COLS), jnp.float32)
    return pl.pallas_call(
        prepare_kernel,
        out_shape=(
            jax.ShapeDtypeStruct((3, 3), jnp.int32),
            shape,
            shape,
            jax.ShapeDtypeStruct(table.shape, table.dtype),
        ),
        in_specs=[VMEM] * 6,
        out_specs=(VMEM,) * 4,
        compiler_params=pltpu.CompilerParams(vmem_limit_bytes=LIMIT),
        name="prepare",
    )(*entries, science, weight, table)


def serve_kernel(window, requests, piece_own, piece_up, piece_down):
    base = (lax.axis_index("visit") // PLANE) * PLANE
    for index, piece in enumerate((piece_own, piece_down, piece_up)):
        start = (requests[...][index, 0] - base) * ROWS + requests[...][index, 1] - KHALF
        first = lax.shift_right_arithmetic(start, 3)
        for part in range(SPAN // 8):
            strip = first + part
            inside = jnp.logical_and(strip >= 0, strip < PLANE * ROWS // 8)
            strip = jnp.clip(strip, 0, PLANE * ROWS // 8 - 1)
            tile = lax.shift_right_logical(strip, 3)
            row = pl.multiple_of(lax.bitwise_and(strip, 7) * 8, 8)
            for block in range(BLOCKS):
                rows = window[tile, pl.ds(block * ROWS + row, 8), :]
                piece[8 * part : 8 * part + 8, block * BLOCK : (block + 1) * BLOCK] = jnp.where(
                    inside, rows, 0.0
                )


def serve(window, requests):
    shape = jax.ShapeDtypeStruct((SPAN, COLS), jnp.float32)
    return pl.pallas_call(
        serve_kernel,
        out_shape=(shape, shape, shape),
        in_specs=[VMEM, VMEM],
        out_specs=(VMEM, VMEM, VMEM),
        compiler_params=pltpu.CompilerParams(vmem_limit_bytes=LIMIT),
        name="serve",
    )(window, requests)


def basis_kernel(
    piece_a, piece_b, piece_c, root, scaled_science, table, entries,
    planes, gram_out,
    high_rows, low_rows,
):
    remainder = lax.bitwise_and(entries[...][0, 1] + SHIFT, 7)
    rows = piece_a[...] + piece_b[...] + piece_c[...]
    rows = pltpu.roll(rows, lax.rem(SPAN - remainder, SPAN), axis=0)
    padded = jnp.concatenate([rows, jnp.zeros((SPAN, BLOCK), jnp.float32)], axis=1)
    cutout = pltpu.roll(padded, KHALF - entries[...][0, 2], axis=1)
    cut_high, cut_low = split(cutout)
    col_high, col_low = table[: 2 * BLOCK, :], table[2 * BLOCK : 4 * BLOCK, :]
    for block in range(COLS // BLOCK):
        cols = slice(block * BLOCK, (block + 2) * BLOCK)
        both = jnp.concatenate([cut_high[:, cols], cut_low[:, cols]], axis=0)
        main = jnp.dot(both, col_high, preferred_element_type=jnp.float32)
        rest = jnp.dot(cut_high[:, cols], col_low, preferred_element_type=jnp.float32)
        across = main[:SPAN] + main[SPAN:] + rest
        across_high, across_low = split(across)
        for factor in range(NFACTORS):
            take = slice(factor * BLOCK, (factor + 1) * BLOCK)
            put = slice(block * BLOCK, (block + 1) * BLOCK)
            high_rows[factor, :, put] = across_high[:, take]
            low_rows[factor, :, put] = across_low[:, take]
    first = 0
    for factor, group in enumerate(GROUPS):
        bands = []
        for member in range(len(group)):
            row, lane = row_band_place(first + member)
            row += 4 * BLOCK
            bands.append(table[row : row + HALF, lane : lane + 3 * DEPTH])
        bands = jnp.concatenate(bands, axis=0)
        for half in range(ROWS // HALF):
            take = slice(half * HALF, half * HALF + DEPTH)
            high = high_rows[factor, take, :]
            stacked = jnp.concatenate([high, low_rows[factor, take, :], high], axis=0)
            out = jnp.dot(bands, stacked, preferred_element_type=jnp.float32)
            for member in range(len(group)):
                scaled = (
                    out[member * HALF : (member + 1) * HALF]
                    * root[half * HALF : (half + 1) * HALF, :]
                )
                put_plane(planes, first + member, half * HALF, scaled)
        first += len(group)
    put_plane(planes, NBASIS - 1, 0, root[...])
    put_plane(planes, NBASIS, 0, scaled_science[...])
    for slot in range(NBASIS + 1, SLOTS):
        put_plane(planes, slot, 0, jnp.zeros((ROWS, COLS), jnp.float32))
    def gram_step(chunk, total):
        highs, lows = [], []
        for inner in range(CHUNK):
            for block in range(BLOCKS):
                row = block * SLOTS * PITCH + chunk * CHUNK + inner
                high, low = split(planes[pl.ds(row, SLOTS, stride=PITCH), :])
                highs.append(high)
                lows.append(low)
        high = jnp.concatenate(highs, axis=1)
        low = jnp.concatenate(lows, axis=1)
        both = jnp.concatenate([high, low], axis=0)
        return total + lax.dot_general(
            high, both, (((1,), (1,)), ((), ())), preferred_element_type=jnp.float32
        )

    total = lax.fori_loop(0, ROWS // CHUNK, gram_step, jnp.zeros((SLOTS, 2 * SLOTS), jnp.float32))
    gram_out[...] = jnp.concatenate(
        [total, jnp.zeros((SLOTS, BLOCK - 2 * SLOTS), jnp.float32)], axis=1
    )


def basis(pieces, *operands):
    return pl.pallas_call(
        basis_kernel,
        out_shape=(
            jax.ShapeDtypeStruct((BLOCKS * SLOTS * PITCH, BLOCK), jnp.float32),
            jax.ShapeDtypeStruct((SLOTS, BLOCK), jnp.float32),
        ),
        in_specs=[VMEM] * 7,
        out_specs=(VMEM, VMEM),
        scratch_shapes=[
            pltpu.VMEM((NFACTORS, SPAN, COLS), jnp.bfloat16),
            pltpu.VMEM((NFACTORS, SPAN, COLS), jnp.bfloat16),
        ],
        compiler_params=pltpu.CompilerParams(vmem_limit_bytes=LIMIT),
        name="basis",
    )(*pieces, *operands)


def solve_kernel(grams, planes, entries, difference_out, stamps, difference, sem):
    total = grams[0] + grams[1] + grams[2] + grams[3]
    cross = total[:, SLOTS : 2 * SLOTS]
    normal = total[:, :SLOTS] + cross + cross.T
    row_id = lax.broadcasted_iota(jnp.int32, (SLOTS, SLOTS), 0)
    col_id = lax.broadcasted_iota(jnp.int32, (SLOTS, SLOTS), 1)
    diagonal = jnp.logical_and(row_id == col_id, row_id < NBASIS)
    trace = jnp.sum(jnp.where(diagonal, normal, 0.0), keepdims=True)
    matrix = normal + jnp.where(diagonal, RIDGE * trace / NBASIS, 0.0)
    for step in range(0, NBASIS, 2):
        first = jnp.broadcast_to(matrix[:, step : step + 1], (SLOTS, SLOTS))
        second = jnp.broadcast_to(matrix[:, step + 1 : step + 2], (SLOTS, SLOTS))
        upper, lower = slice(step, step + 1), slice(step + 1, step + 2)
        inverse = 1.0 / (first[upper] * second[lower] - second[upper] * first[lower])
        row_upper = (second[lower] * matrix[upper] - second[upper] * matrix[lower]) * inverse
        row_lower = (first[upper] * matrix[lower] - first[lower] * matrix[upper]) * inverse
        others = matrix - first * row_upper - second * row_lower
        matrix = jnp.where(
            row_id == step, row_upper, jnp.where(row_id == step + 1, row_lower, others)
        )
    answer = jnp.broadcast_to(matrix[:, NBASIS : NBASIS + 1], (SLOTS, BLOCK))
    for block in range(BLOCKS):
        at = (block * SLOTS + NBASIS) * PITCH
        total = planes[at : at + ROWS, :]
        for plane in range(NBASIS):
            factor = jnp.broadcast_to(answer[plane : plane + 1, :], (ROWS, BLOCK))
            at = (block * SLOTS + plane) * PITCH
            total = total - factor * planes[at : at + ROWS, :]
        difference[:, block * BLOCK : (block + 1) * BLOCK] = total
    copy = pltpu.make_async_copy(difference, difference_out, sem)
    copy.start()
    row_move, col_move = entries[...][0, 1], entries[...][0, 2]
    moved = pltpu.roll(difference[...], lax.rem(row_move + ROWS, ROWS), axis=0)
    moved = pltpu.roll(moved, lax.rem(col_move + COLS, COLS), axis=1)
    from_row = lax.broadcasted_iota(jnp.int32, (ROWS, COLS), 0) - row_move
    from_col = lax.broadcasted_iota(jnp.int32, (ROWS, COLS), 1) - col_move
    inside = (from_row >= 0) & (from_row < ROWS) & (from_col >= 0) & (from_col < COLS)
    placed = jnp.where(inside, moved, 0.0)
    for place in range(LINE):
        mine = lax.bitwise_and(entries[...][0, 0], LINE - 1) == place
        for block in range(BLOCKS):
            stamps[place, block * ROWS : (block + 1) * ROWS, :] = jnp.where(
                mine, placed[:, block * BLOCK : (block + 1) * BLOCK], 0.0
            )
        stamps[place, TALL:, :] = jnp.full(
            (NOTED - TALL, BLOCK), entries[...][0, 0].astype(jnp.float32), jnp.float32
        )
    copy.wait()


def solve(grams, planes, entries):
    return pl.pallas_call(
        solve_kernel,
        out_shape=(
            jax.ShapeDtypeStruct((ROWS, COLS), jnp.float32),
            jax.ShapeDtypeStruct((LINE, NOTED, BLOCK), jnp.float32),
        ),
        in_specs=[VMEM, VMEM, VMEM],
        out_specs=(HBM, VMEM),
        scratch_shapes=[pltpu.VMEM((ROWS, COLS), jnp.float32), pltpu.SemaphoreType.DMA],
        compiler_params=pltpu.CompilerParams(vmem_limit_bytes=LIMIT),
        name="solve",
    )(grams, planes, entries)


def gather_kernel(stamps, to_own, to_flip, to_next, to_far):
    visit = lax.axis_index("visit")
    even = lax.rem(visit // LINE, 2) == 0
    low = lax.rem(visit, LINE) < LINE // 2
    targets = (
        visit,
        jnp.where(even, visit + LINE, visit - LINE),
        jnp.where(even, visit - LINE, visit + LINE),
        jnp.where(low, visit + 2 * LINE, visit - 2 * LINE),
    )
    for target, out in zip(targets, (to_own, to_flip, to_next, to_far)):
        number = target.astype(jnp.float32)
        hits = [stamps[place, TALL:, :] == number for place in range(LINE)]
        count = jnp.zeros((NOTED - TALL, BLOCK), jnp.float32)
        for hit in hits:
            count = count + jnp.where(hit, 1.0, 0.0)
        out[TALL:, :] = count
        for block in range(BLOCKS):
            rows = slice(block * ROWS, (block + 1) * ROWS)
            total = jnp.zeros((ROWS, BLOCK), jnp.float32)
            for place in range(LINE):
                total = total + jnp.where(hits[place][:1], stamps[place, rows, :], 0.0)
            out[rows, :] = total


def gather(stamps):
    shape = jax.ShapeDtypeStruct((NOTED, BLOCK), jnp.float32)
    return pl.pallas_call(
        gather_kernel,
        out_shape=(shape,) * 4,
        in_specs=[VMEM],
        out_specs=(VMEM,) * 4,
        compiler_params=pltpu.CompilerParams(vmem_limit_bytes=LIMIT),
        name="gather",
    )(stamps)


def mean_kernel(part_a, part_b, part_c, part_d, coadd):
    parts = (part_a, part_b, part_c, part_d)
    count = sum(part[TALL:, :] for part in parts)
    count = jnp.maximum(count[:1], 1.0)
    for block in range(BLOCKS):
        rows = slice(block * ROWS, (block + 1) * ROWS)
        total = sum(part[rows, :] for part in parts)
        coadd[:, block * BLOCK : (block + 1) * BLOCK] = total / count


def mean(*parts):
    return pl.pallas_call(
        mean_kernel,
        out_shape=jax.ShapeDtypeStruct((ROWS, COLS), jnp.float32),
        in_specs=[VMEM] * 4,
        out_specs=VMEM,
        compiler_params=pltpu.CompilerParams(vmem_limit_bytes=LIMIT),
        name="mean",
    )(*parts)


def shards(template, science, inverse_variance, intersections):
    visits = lax.axis_size("visit")
    groups = [list(range(first, first + PLANE)) for first in range(0, visits, PLANE)]
    upward = [(i, i + PLANE) for i in range(visits - PLANE)]
    downward = [(target, source) for source, target in upward]
    own = intersections[0]
    below = lax.ppermute(own, "visit", upward)
    above = lax.ppermute(own, "visit", downward)
    requests, *prepared = prepare(
        (own, below, above), science[0, 0], inverse_variance[0, 0], jnp.asarray(tables())
    )
    window = lax.all_to_all(spread(template[0]), "visit", 0, 0, axis_index_groups=groups)
    piece_own, piece_up, piece_down = serve(window, requests)
    from_above = lax.ppermute(piece_down, "visit", downward)
    from_below = lax.ppermute(piece_up, "visit", upward)
    planes, gram = basis((piece_own, from_above, from_below), *prepared, requests)
    grams = lax.all_gather(gram, "patch")
    difference, stamps = solve(grams, planes, requests)
    lines = [list(range(first, first + LINE)) for first in range(0, visits, LINE)]
    to_own, to_flip, to_next, to_far = gather(
        lax.all_to_all(stamps, "visit", 0, 0, axis_index_groups=lines)
    )
    flip = [(i, i ^ LINE) for i in range(visits)]
    following = [(i, ((i + LINE) ^ LINE) - LINE) for i in range(LINE, visits - LINE)]
    far = [(i, i + 2 * LINE if i % LINE < LINE // 2 else i - 2 * LINE) for i in range(visits)]
    far = [(source, target) for source, target in far if 0 <= target < visits]
    from_far = lax.ppermute(to_far, "visit", far)
    from_next = lax.ppermute(to_next, "visit", following)
    from_flip = lax.ppermute(to_flip, "visit", flip)
    return (difference[None, None], mean(to_own, from_flip, from_next, from_far)[None])


def solution(mesh):
    in_specs = (
        P("patch", "visit", None),
        P("visit", "patch", None, None),
        P("visit", "patch", None, None),
        P("visit", "patch", None),
    )
    out_specs = (P("visit", "patch", None, None), P("patch", "visit", None))
    return jax.shard_map(shards, mesh=mesh, in_specs=in_specs, out_specs=out_specs, check_vma=False)
```

```python
import functools
import math

import jax
import jax.numpy as jnp
import ml_dtypes
import numpy as np
from jax import lax
from jax.experimental import pallas as pl
from jax.experimental.pallas import tpu as pltpu
from jax.sharding import PartitionSpec as P

KHALF = 10
SHIFT = 6
REACH = 6
NBASIS = 28
ROWS = 64
COLS = 512
PLANE = 8
LINE = 4
SPAN = 96
SLOTS = 32
BLOCK = 128
BLOCKS = COLS // BLOCK
PITCH = 72
TALL = BLOCKS * ROWS
NOTED = TALL + 8
HALF = 32
CHUNK = 32
DEPTH = 64

SIGMAS = (1.0, 2.0, 4.0)
DEGREES = (4, 2, 2)
RIDGE = 0.01
LIMIT = 32 * 1024 * 1024
BESIDE = 5
BESIDE_ROWS = -(-(NBASIS - 1) // BESIDE) * HALF

VMEM = pl.BlockSpec(memory_space=pltpu.VMEM)
HBM = pl.BlockSpec(memory_space=pltpu.HBM)


def factor_table():
    listed = []
    for width_sigma, degree in zip(SIGMAS, DEGREES):
        for exponent in range(degree + 1):
            values = [
                math.exp(-(offset * offset) / (2.0 * width_sigma * width_sigma))
                * (offset / KHALF) ** exponent
                for offset in range(-KHALF, KHALF + 1)
            ]
            scale_norm = math.sqrt(sum((entry * entry for entry in values)))
            listed.append([entry / scale_norm for entry in values])
    return np.array(listed, dtype=np.float32)


def row_factors_by_column_factor():
    groups = []
    first = 0
    for degree in DEGREES:
        for power_col in range(degree + 1):
            groups.append([first + power_row for power_row in range(degree + 1 - power_col)])
        first += degree + 1
    return groups


GROUPS = row_factors_by_column_factor()
NFACTORS = len(GROUPS)


def split_constant(values):
    high = values.astype(ml_dtypes.bfloat16)
    low = (values - high.astype(np.float32)).astype(ml_dtypes.bfloat16)
    return high, low


def tables():
    table = factor_table()
    distance = np.arange(2 * BLOCK)[:, None] - np.arange(BLOCK)[None, :]
    bands = np.zeros((2 * BLOCK, NFACTORS, BLOCK), np.float32)
    for offset in range(2 * KHALF + 1):
        bands += table[None, :, offset, None] * (distance == offset)[:, None, :]
    columns = split_constant(bands.reshape(2 * BLOCK, NFACTORS * BLOCK))
    distance = np.arange(DEPTH)[None, :] - np.arange(HALF)[:, None]
    chosen = [index for group in GROUPS for index in group]
    bands = np.zeros((len(chosen), HALF, DEPTH), np.float32)
    for offset in range(2 * KHALF + 1):
        bands += table[chosen, offset][:, None, None] * (distance == offset)[None]
    high, low = split_constant(bands)
    rows = np.zeros((BESIDE_ROWS, NFACTORS * BLOCK), ml_dtypes.bfloat16)
    for plane, band in enumerate(np.concatenate([high, high, low], axis=2)):
        row, lane = row_band_place(plane)
        rows[row : row + HALF, lane : lane + 3 * DEPTH] = band
    return np.concatenate([*columns, rows])


def row_band_place(plane):
    return plane // BESIDE * HALF, plane % BESIDE * 2 * BLOCK


def split(values):
    high = values.astype(jnp.bfloat16)
    low = (values - high.astype(jnp.float32)).astype(jnp.bfloat16)
    return high, low


def put_plane(planes, slot, row, values):
    for block in range(BLOCKS):
        at = (block * SLOTS + slot) * PITCH + row
        planes[at : at + values.shape[0], :] = values[:, block * BLOCK : (block + 1) * BLOCK]


def spread_kernel(tile, copies):
    for copy in range(PLANE):
        for block in range(BLOCKS):
            copies[copy, block * ROWS : (block + 1) * ROWS, :] = tile[
                :, block * BLOCK : (block + 1) * BLOCK
            ]


def spread(tile):
    return pl.pallas_call(
        spread_kernel,
        out_shape=jax.ShapeDtypeStruct((PLANE, TALL, BLOCK), jnp.float32),
        in_specs=[VMEM],
        out_specs=VMEM,
        compiler_params=pltpu.CompilerParams(vmem_limit_bytes=LIMIT),
        name="spread",
    )(tile)


def noted_number(sheet, index, part):
    return sheet[2 * ROWS : 2 * ROWS + 1, :BLOCK][0, 3 * index + part].astype(jnp.int32)


def prepare_kernel(
    own, below, above, science, weight, table,
    sheet, table_out,
):
    lane = lax.broadcasted_iota(jnp.int32, (8, COLS), 1)
    noted = jnp.zeros((8, COLS), jnp.float32)
    for index, entries in enumerate((own, below, above)):
        for part in range(3):
            number = entries[...][0, part].astype(jnp.float32)
            noted = jnp.where(lane == 3 * index + part, number, noted)
    sheet[2 * ROWS :, :] = noted
    values = jnp.sqrt(weight[...])
    sheet[:ROWS, :] = values
    sheet[ROWS : 2 * ROWS, :] = values * science[...]
    table_out[...] = table[...]


def prepare(entries, science, weight, table):
    return pl.pallas_call(
        prepare_kernel,
        out_shape=(
            jax.ShapeDtypeStruct((2 * ROWS + 8, COLS), jnp.float32),
            jax.ShapeDtypeStruct(table.shape, table.dtype),
        ),
        in_specs=[VMEM] * 6,
        out_specs=(VMEM,) * 2,
        compiler_params=pltpu.CompilerParams(vmem_limit_bytes=LIMIT),
        name="prepare",
    )(*entries, science, weight, table)


def serve_kernel(window, sheet, piece_own, piece_up, piece_down):
    base = (lax.axis_index("visit") // PLANE) * PLANE
    for index, piece in enumerate((piece_own, piece_down, piece_up)):
        tile_asked, row_move = noted_number(sheet, index, 0), noted_number(sheet, index, 1)
        start = (tile_asked - base) * ROWS + row_move - KHALF
        first = lax.shift_right_arithmetic(start, 3)
        for part in range(SPAN // 8):
            strip = first + part
            inside = jnp.logical_and(strip >= 0, strip < PLANE * ROWS // 8)
            strip = jnp.clip(strip, 0, PLANE * ROWS // 8 - 1)
            tile = lax.shift_right_logical(strip, 3)
            row = pl.multiple_of(lax.bitwise_and(strip, 7) * 8, 8)
            for block in range(BLOCKS):
                rows = window[tile, pl.ds(block * ROWS + row, 8), :]
                piece[8 * part : 8 * part + 8, block * BLOCK : (block + 1) * BLOCK] = jnp.where(
                    inside, rows, 0.0
                )


def serve(window, sheet):
    shape = jax.ShapeDtypeStruct((SPAN, COLS), jnp.float32)
    return pl.pallas_call(
        serve_kernel,
        out_shape=(shape, shape, shape),
        in_specs=[VMEM, VMEM],
        out_specs=(VMEM, VMEM, VMEM),
        compiler_params=pltpu.CompilerParams(vmem_limit_bytes=LIMIT),
        name="serve",
    )(window, sheet)


def basis_kernel(
    piece_a, piece_b, piece_c, sheet, table,
    planes, gram_out,
    high_rows, low_rows,
):
    remainder = lax.bitwise_and(noted_number(sheet, 0, 1) + SHIFT, 7)
    rows = piece_a[...] + piece_b[...] + piece_c[...]
    rows = pltpu.roll(rows, lax.rem(SPAN - remainder, SPAN), axis=0)
    padded = jnp.concatenate([rows, jnp.zeros((SPAN, BLOCK), jnp.float32)], axis=1)
    cutout = pltpu.roll(padded, KHALF - noted_number(sheet, 0, 2), axis=1)
    cut_high, cut_low = split(cutout)
    col_high, col_low = table[: 2 * BLOCK, :], table[2 * BLOCK : 4 * BLOCK, :]
    for block in range(COLS // BLOCK):
        cols = slice(block * BLOCK, (block + 2) * BLOCK)
        both = jnp.concatenate([cut_high[:, cols], cut_low[:, cols]], axis=0)
        main = jnp.dot(both, col_high, preferred_element_type=jnp.float32)
        rest = jnp.dot(cut_high[:, cols], col_low, preferred_element_type=jnp.float32)
        across = main[:SPAN] + main[SPAN:] + rest
        across_high, across_low = split(across)
        for factor in range(NFACTORS):
            take = slice(factor * BLOCK, (factor + 1) * BLOCK)
            put = slice(block * BLOCK, (block + 1) * BLOCK)
            high_rows[factor, :, put] = across_high[:, take]
            low_rows[factor, :, put] = across_low[:, take]
    first = 0
    for factor, group in enumerate(GROUPS):
        bands = []
        for member in range(len(group)):
            row, lane = row_band_place(first + member)
            row += 4 * BLOCK
            bands.append(table[row : row + HALF, lane : lane + 3 * DEPTH])
        bands = jnp.concatenate(bands, axis=0)
        for half in range(ROWS // HALF):
            take = slice(half * HALF, half * HALF + DEPTH)
            high = high_rows[factor, take, :]
            stacked = jnp.concatenate([high, low_rows[factor, take, :], high], axis=0)
            out = jnp.dot(bands, stacked, preferred_element_type=jnp.float32)
            for member in range(len(group)):
                scaled = (
                    out[member * HALF : (member + 1) * HALF]
                    * sheet[half * HALF : (half + 1) * HALF, :]
                )
                put_plane(planes, first + member, half * HALF, scaled)
        first += len(group)
    put_plane(planes, NBASIS - 1, 0, sheet[:ROWS, :])
    put_plane(planes, NBASIS, 0, sheet[ROWS : 2 * ROWS, :])
    for slot in range(NBASIS + 1, SLOTS):
        put_plane(planes, slot, 0, jnp.zeros((ROWS, COLS), jnp.float32))
    def gram_step(chunk, total):
        highs, lows = [], []
        for inner in range(CHUNK):
            for block in range(BLOCKS):
                row = block * SLOTS * PITCH + chunk * CHUNK + inner
                high, low = split(planes[pl.ds(row, SLOTS, stride=PITCH), :])
                highs.append(high)
                lows.append(low)
        high = jnp.concatenate(highs, axis=1)
        low = jnp.concatenate(lows, axis=1)
        both = jnp.concatenate([high, low], axis=0)
        return total + lax.dot_general(
            high, both, (((1,), (1,)), ((), ())), preferred_element_type=jnp.float32
        )

    total = lax.fori_loop(0, ROWS // CHUNK, gram_step, jnp.zeros((SLOTS, 2 * SLOTS), jnp.float32))
    gram_out[...] = jnp.concatenate(
        [total, jnp.zeros((SLOTS, BLOCK - 2 * SLOTS), jnp.float32)], axis=1
    )


def basis(pieces, *operands):
    return pl.pallas_call(
        basis_kernel,
        out_shape=(
            jax.ShapeDtypeStruct((BLOCKS * SLOTS * PITCH, BLOCK), jnp.float32),
            jax.ShapeDtypeStruct((SLOTS, BLOCK), jnp.float32),
        ),
        in_specs=[VMEM] * 5,
        out_specs=(VMEM, VMEM),
        scratch_shapes=[
            pltpu.VMEM((NFACTORS, SPAN, COLS), jnp.bfloat16),
            pltpu.VMEM((NFACTORS, SPAN, COLS), jnp.bfloat16),
        ],
        compiler_params=pltpu.CompilerParams(vmem_limit_bytes=LIMIT),
        name="basis",
    )(*pieces, *operands)


def solve_kernel(grams, planes, sheet, difference_out, stamps, difference, sem):
    total = grams[0] + grams[1] + grams[2] + grams[3]
    cross = total[:, SLOTS : 2 * SLOTS]
    normal = total[:, :SLOTS] + cross + cross.T
    row_id = lax.broadcasted_iota(jnp.int32, (SLOTS, SLOTS), 0)
    col_id = lax.broadcasted_iota(jnp.int32, (SLOTS, SLOTS), 1)
    diagonal = jnp.logical_and(row_id == col_id, row_id < NBASIS)
    trace = jnp.sum(jnp.where(diagonal, normal, 0.0), keepdims=True)
    matrix = normal + jnp.where(diagonal, RIDGE * trace / NBASIS, 0.0)
    for step in range(0, NBASIS, 2):
        first = jnp.broadcast_to(matrix[:, step : step + 1], (SLOTS, SLOTS))
        second = jnp.broadcast_to(matrix[:, step + 1 : step + 2], (SLOTS, SLOTS))
        upper, lower = slice(step, step + 1), slice(step + 1, step + 2)
        inverse = 1.0 / (first[upper] * second[lower] - second[upper] * first[lower])
        row_upper = (second[lower] * matrix[upper] - second[upper] * matrix[lower]) * inverse
        row_lower = (first[upper] * matrix[lower] - first[lower] * matrix[upper]) * inverse
        others = matrix - first * row_upper - second * row_lower
        matrix = jnp.where(
            row_id == step, row_upper, jnp.where(row_id == step + 1, row_lower, others)
        )
    answer = jnp.broadcast_to(matrix[:, NBASIS : NBASIS + 1], (SLOTS, BLOCK))
    for block in range(BLOCKS):
        at = (block * SLOTS + NBASIS) * PITCH
        total = planes[at : at + ROWS, :]
        for plane in range(NBASIS):
            factor = jnp.broadcast_to(answer[plane : plane + 1, :], (ROWS, BLOCK))
            at = (block * SLOTS + plane) * PITCH
            total = total - factor * planes[at : at + ROWS, :]
        difference[:, block * BLOCK : (block + 1) * BLOCK] = total
    copy = pltpu.make_async_copy(difference, difference_out, sem)
    copy.start()
    tile, row_move, col_move = (noted_number(sheet, 0, part) for part in range(3))
    moved = pltpu.roll(difference[...], lax.rem(row_move + ROWS, ROWS), axis=0)
    moved = pltpu.roll(moved, lax.rem(col_move + COLS, COLS), axis=1)
    from_row = lax.broadcasted_iota(jnp.int32, (ROWS, COLS), 0) - row_move
    from_col = lax.broadcasted_iota(jnp.int32, (ROWS, COLS), 1) - col_move
    inside = (from_row >= 0) & (from_row < ROWS) & (from_col >= 0) & (from_col < COLS)
    placed = jnp.where(inside, moved, 0.0)
    for place in range(LINE):
        mine = lax.bitwise_and(tile, LINE - 1) == place
        for block in range(BLOCKS):
            stamps[place, block * ROWS : (block + 1) * ROWS, :] = jnp.where(
                mine, placed[:, block * BLOCK : (block + 1) * BLOCK], 0.0
            )
        stamps[place, TALL:, :] = jnp.full(
            (NOTED - TALL, BLOCK), tile.astype(jnp.float32), jnp.float32
        )
    copy.wait()


def solve(grams, planes, sheet):
    return pl.pallas_call(
        solve_kernel,
        out_shape=(
            jax.ShapeDtypeStruct((ROWS, COLS), jnp.float32),
            jax.ShapeDtypeStruct((LINE, NOTED, BLOCK), jnp.float32),
        ),
        in_specs=[VMEM, VMEM, VMEM],
        out_specs=(HBM, VMEM),
        scratch_shapes=[pltpu.VMEM((ROWS, COLS), jnp.float32), pltpu.SemaphoreType.DMA],
        compiler_params=pltpu.CompilerParams(vmem_limit_bytes=LIMIT),
        name="solve",
    )(grams, planes, sheet)


def gather_kernel(stamps, to_own, to_flip, to_next, to_far):
    visit = lax.axis_index("visit")
    even = lax.rem(visit // LINE, 2) == 0
    low = lax.rem(visit, LINE) < LINE // 2
    targets = (
        visit,
        jnp.where(even, visit + LINE, visit - LINE),
        jnp.where(even, visit - LINE, visit + LINE),
        jnp.where(low, visit + 2 * LINE, visit - 2 * LINE),
    )
    for target, out in zip(targets, (to_own, to_flip, to_next, to_far)):
        number = target.astype(jnp.float32)
        hits = [stamps[place, TALL:, :] == number for place in range(LINE)]
        count = jnp.zeros((NOTED - TALL, BLOCK), jnp.float32)
        for hit in hits:
            count = count + jnp.where(hit, 1.0, 0.0)
        out[TALL:, :] = count
        for block in range(BLOCKS):
            rows = slice(block * ROWS, (block + 1) * ROWS)
            total = jnp.zeros((ROWS, BLOCK), jnp.float32)
            for place in range(LINE):
                total = total + jnp.where(hits[place][:1], stamps[place, rows, :], 0.0)
            out[rows, :] = total


def gather(stamps):
    shape = jax.ShapeDtypeStruct((NOTED, BLOCK), jnp.float32)
    return pl.pallas_call(
        gather_kernel,
        out_shape=(shape,) * 4,
        in_specs=[VMEM],
        out_specs=(VMEM,) * 4,
        compiler_params=pltpu.CompilerParams(vmem_limit_bytes=LIMIT),
        name="gather",
    )(stamps)


def mean_kernel(part_a, part_b, part_c, part_d, coadd):
    parts = (part_a, part_b, part_c, part_d)
    count = sum(part[TALL:, :] for part in parts)
    count = jnp.maximum(count[:1], 1.0)
    for block in range(BLOCKS):
        rows = slice(block * ROWS, (block + 1) * ROWS)
        total = sum(part[rows, :] for part in parts)
        coadd[:, block * BLOCK : (block + 1) * BLOCK] = total / count


def mean(*parts):
    return pl.pallas_call(
        mean_kernel,
        out_shape=jax.ShapeDtypeStruct((ROWS, COLS), jnp.float32),
        in_specs=[VMEM] * 4,
        out_specs=VMEM,
        compiler_params=pltpu.CompilerParams(vmem_limit_bytes=LIMIT),
        name="mean",
    )(*parts)


def shards(template, science, inverse_variance, intersections):
    visits = lax.axis_size("visit")
    groups = [list(range(first, first + PLANE)) for first in range(0, visits, PLANE)]
    upward = [(i, i + PLANE) for i in range(visits - PLANE)]
    downward = [(target, source) for source, target in upward]
    own = intersections[0]
    below = lax.ppermute(own, "visit", upward)
    above = lax.ppermute(own, "visit", downward)
    sheet, table = prepare(
        (own, below, above), science[0, 0], inverse_variance[0, 0], jnp.asarray(tables())
    )
    window = lax.all_to_all(spread(template[0]), "visit", 0, 0, axis_index_groups=groups)
    piece_own, piece_up, piece_down = serve(window, sheet)
    from_above = lax.ppermute(piece_down, "visit", downward)
    from_below = lax.ppermute(piece_up, "visit", upward)
    planes, gram = basis((piece_own, from_above, from_below), sheet, table)
    grams = lax.all_gather(gram, "patch")
    difference, stamps = solve(grams, planes, sheet)
    lines = [list(range(first, first + LINE)) for first in range(0, visits, LINE)]
    to_own, to_flip, to_next, to_far = gather(
        lax.all_to_all(stamps, "visit", 0, 0, axis_index_groups=lines)
    )
    flip = [(i, i ^ LINE) for i in range(visits)]
    following = [(i, ((i + LINE) ^ LINE) - LINE) for i in range(LINE, visits - LINE)]
    far = [(i, i + 2 * LINE if i % LINE < LINE // 2 else i - 2 * LINE) for i in range(visits)]
    far = [(source, target) for source, target in far if 0 <= target < visits]
    from_far = lax.ppermute(to_far, "visit", far)
    from_next = lax.ppermute(to_next, "visit", following)
    from_flip = lax.ppermute(to_flip, "visit", flip)
    return (difference[None, None], mean(to_own, from_flip, from_next, from_far)[None])


def solution(mesh):
    in_specs = (
        P("patch", "visit", None),
        P("visit", "patch", None, None),
        P("visit", "patch", None, None),
        P("visit", "patch", None),
    )
    out_specs = (P("visit", "patch", None, None), P("patch", "visit", None))
    return jax.shard_map(shards, mesh=mesh, in_specs=in_specs, out_specs=out_specs, check_vma=False)
```

```python
import functools
import math

import jax
import jax.numpy as jnp
import ml_dtypes
import numpy as np
from jax import lax
from jax.experimental import pallas as pl
from jax.experimental.pallas import tpu as pltpu
from jax.sharding import PartitionSpec as P

KHALF = 10
SHIFT = 6
REACH = 6
NBASIS = 28
ROWS = 64
COLS = 512
PLANE = 8
LINE = 4
SPAN = 96
SLOTS = 32
BLOCK = 128
BLOCKS = COLS // BLOCK
PITCH = 72
TALL = BLOCKS * ROWS
NOTED = TALL + 8
HALF = 32
CHUNK = 32
DEPTH = 64

SIGMAS = (1.0, 2.0, 4.0)
DEGREES = (4, 2, 2)
RIDGE = 0.01
LIMIT = 32 * 1024 * 1024
BESIDE = 5
BESIDE_ROWS = -(-(NBASIS - 1) // BESIDE) * HALF

VMEM = pl.BlockSpec(memory_space=pltpu.VMEM)
HBM = pl.BlockSpec(memory_space=pltpu.HBM)


def factor_table():
    listed = []
    for width_sigma, degree in zip(SIGMAS, DEGREES):
        for exponent in range(degree + 1):
            values = [
                math.exp(-(offset * offset) / (2.0 * width_sigma * width_sigma))
                * (offset / KHALF) ** exponent
                for offset in range(-KHALF, KHALF + 1)
            ]
            scale_norm = math.sqrt(sum((entry * entry for entry in values)))
            listed.append([entry / scale_norm for entry in values])
    return np.array(listed, dtype=np.float32)


def row_factors_by_column_factor():
    groups = []
    first = 0
    for degree in DEGREES:
        for power_col in range(degree + 1):
            groups.append([first + power_row for power_row in range(degree + 1 - power_col)])
        first += degree + 1
    return groups


GROUPS = row_factors_by_column_factor()
NFACTORS = len(GROUPS)


def split_constant(values):
    high = values.astype(ml_dtypes.bfloat16)
    low = (values - high.astype(np.float32)).astype(ml_dtypes.bfloat16)
    return high, low


def tables():
    table = factor_table()
    distance = np.arange(2 * BLOCK)[:, None] - np.arange(BLOCK)[None, :]
    bands = np.zeros((2 * BLOCK, NFACTORS, BLOCK), np.float32)
    for offset in range(2 * KHALF + 1):
        bands += table[None, :, offset, None] * (distance == offset)[:, None, :]
    columns = split_constant(bands.reshape(2 * BLOCK, NFACTORS * BLOCK))
    distance = np.arange(DEPTH)[None, :] - np.arange(HALF)[:, None]
    chosen = [index for group in GROUPS for index in group]
    bands = np.zeros((len(chosen), HALF, DEPTH), np.float32)
    for offset in range(2 * KHALF + 1):
        bands += table[chosen, offset][:, None, None] * (distance == offset)[None]
    high, low = split_constant(bands)
    rows = np.zeros((BESIDE_ROWS, NFACTORS * BLOCK), ml_dtypes.bfloat16)
    for plane, band in enumerate(np.concatenate([high, high, low], axis=2)):
        row, lane = row_band_place(plane)
        rows[row : row + HALF, lane : lane + 3 * DEPTH] = band
    return np.concatenate([*columns, rows])


def row_band_place(plane):
    return plane // BESIDE * HALF, plane % BESIDE * 2 * BLOCK


def split(values):
    high = values.astype(jnp.bfloat16)
    low = (values - high.astype(jnp.float32)).astype(jnp.bfloat16)
    return high, low


def put_plane(planes, slot, row, values):
    for block in range(BLOCKS):
        at = (block * SLOTS + slot) * PITCH + row
        planes[at : at + values.shape[0], :] = values[:, block * BLOCK : (block + 1) * BLOCK]


def spread_kernel(tile, copies):
    for copy in range(PLANE):
        for block in range(BLOCKS):
            copies[copy, block * ROWS : (block + 1) * ROWS, :] = tile[
                :, block * BLOCK : (block + 1) * BLOCK
            ]


def spread(tile):
    return pl.pallas_call(
        spread_kernel,
        out_shape=jax.ShapeDtypeStruct((PLANE, TALL, BLOCK), jnp.float32),
        in_specs=[VMEM],
        out_specs=VMEM,
        compiler_params=pltpu.CompilerParams(vmem_limit_bytes=LIMIT),
        name="spread",
    )(tile)


def noted_number(sheet, part):
    return sheet[2 * ROWS : 2 * ROWS + 1, :BLOCK][0, part].astype(jnp.int32)


def prepare_kernel(
    entries, science, weight, table,
    sheet, table_out,
):
    lane = lax.broadcasted_iota(jnp.int32, (8, COLS), 1)
    noted = jnp.zeros((8, COLS), jnp.float32)
    for part in range(3):
        noted = jnp.where(lane == part, entries[...][0, part].astype(jnp.float32), noted)
    sheet[2 * ROWS :, :] = noted
    values = jnp.sqrt(weight[...])
    sheet[:ROWS, :] = values
    sheet[ROWS : 2 * ROWS, :] = values * science[...]
    table_out[...] = table[...]


def prepare(entries, science, weight, table):
    return pl.pallas_call(
        prepare_kernel,
        out_shape=(
            jax.ShapeDtypeStruct((2 * ROWS + 8, COLS), jnp.float32),
            jax.ShapeDtypeStruct(table.shape, table.dtype),
        ),
        in_specs=[VMEM] * 4,
        out_specs=(VMEM,) * 2,
        compiler_params=pltpu.CompilerParams(vmem_limit_bytes=LIMIT),
        name="prepare",
    )(entries, science, weight, table)


def serve_kernel(window, sheet, below, above, piece_own, piece_up, piece_down):
    base = (lax.axis_index("visit") // PLANE) * PLANE
    own = (noted_number(sheet, 0), noted_number(sheet, 1))
    others = [(entries[...][0, 0], entries[...][0, 1]) for entries in (below, above)]
    for (asked, row_move), piece in zip((own, *others), (piece_own, piece_down, piece_up)):
        start = (asked - base) * ROWS + row_move - KHALF
        first = lax.shift_right_arithmetic(start, 3)
        for part in range(SPAN // 8):
            strip = first + part
            inside = jnp.logical_and(strip >= 0, strip < PLANE * ROWS // 8)
            strip = jnp.clip(strip, 0, PLANE * ROWS // 8 - 1)
            tile = lax.shift_right_logical(strip, 3)
            row = pl.multiple_of(lax.bitwise_and(strip, 7) * 8, 8)
            for block in range(BLOCKS):
                rows = window[tile, pl.ds(block * ROWS + row, 8), :]
                piece[8 * part : 8 * part + 8, block * BLOCK : (block + 1) * BLOCK] = jnp.where(
                    inside, rows, 0.0
                )


def serve(window, sheet, below, above):
    shape = jax.ShapeDtypeStruct((SPAN, COLS), jnp.float32)
    return pl.pallas_call(
        serve_kernel,
        out_shape=(shape, shape, shape),
        in_specs=[VMEM] * 4,
        out_specs=(VMEM, VMEM, VMEM),
        compiler_params=pltpu.CompilerParams(vmem_limit_bytes=LIMIT),
        name="serve",
    )(window, sheet, below, above)


def basis_kernel(
    piece_a, piece_b, piece_c, sheet, table,
    planes, gram_out,
    high_rows, low_rows,
):
    remainder = lax.bitwise_and(noted_number(sheet, 1) + SHIFT, 7)
    rows = piece_a[...] + piece_b[...] + piece_c[...]
    rows = pltpu.roll(rows, lax.rem(SPAN - remainder, SPAN), axis=0)
    padded = jnp.concatenate([rows, jnp.zeros((SPAN, BLOCK), jnp.float32)], axis=1)
    cutout = pltpu.roll(padded, KHALF - noted_number(sheet, 2), axis=1)
    cut_high, cut_low = split(cutout)
    col_high, col_low = table[: 2 * BLOCK, :], table[2 * BLOCK : 4 * BLOCK, :]
    for block in range(COLS // BLOCK):
        cols = slice(block * BLOCK, (block + 2) * BLOCK)
        both = jnp.concatenate([cut_high[:, cols], cut_low[:, cols]], axis=0)
        main = jnp.dot(both, col_high, preferred_element_type=jnp.float32)
        rest = jnp.dot(cut_high[:, cols], col_low, preferred_element_type=jnp.float32)
        across = main[:SPAN] + main[SPAN:] + rest
        across_high, across_low = split(across)
        for factor in range(NFACTORS):
            take = slice(factor * BLOCK, (factor + 1) * BLOCK)
            put = slice(block * BLOCK, (block + 1) * BLOCK)
            high_rows[factor, :, put] = across_high[:, take]
            low_rows[factor, :, put] = across_low[:, take]
    first = 0
    for factor, group in enumerate(GROUPS):
        bands = []
        for member in range(len(group)):
            row, lane = row_band_place(first + member)
            row += 4 * BLOCK
            bands.append(table[row : row + HALF, lane : lane + 3 * DEPTH])
        bands = jnp.concatenate(bands, axis=0)
        for half in range(ROWS // HALF):
            take = slice(half * HALF, half * HALF + DEPTH)
            high = high_rows[factor, take, :]
            stacked = jnp.concatenate([high, low_rows[factor, take, :], high], axis=0)
            out = jnp.dot(bands, stacked, preferred_element_type=jnp.float32)
            for member in range(len(group)):
                scaled = (
                    out[member * HALF : (member + 1) * HALF]
                    * sheet[half * HALF : (half + 1) * HALF, :]
                )
                put_plane(planes, first + member, half * HALF, scaled)
        first += len(group)
    put_plane(planes, NBASIS - 1, 0, sheet[:ROWS, :])
    put_plane(planes, NBASIS, 0, sheet[ROWS : 2 * ROWS, :])
    for slot in range(NBASIS + 1, SLOTS):
        put_plane(planes, slot, 0, jnp.zeros((ROWS, COLS), jnp.float32))
    def gram_step(chunk, total):
        highs, lows = [], []
        for inner in range(CHUNK):
            for block in range(BLOCKS):
                row = block * SLOTS * PITCH + chunk * CHUNK + inner
                high, low = split(planes[pl.ds(row, SLOTS, stride=PITCH), :])
                highs.append(high)
                lows.append(low)
        high = jnp.concatenate(highs, axis=1)
        low = jnp.concatenate(lows, axis=1)
        both = jnp.concatenate([high, low], axis=0)
        return total + lax.dot_general(
            high, both, (((1,), (1,)), ((), ())), preferred_element_type=jnp.float32
        )

    total = lax.fori_loop(0, ROWS // CHUNK, gram_step, jnp.zeros((SLOTS, 2 * SLOTS), jnp.float32))
    gram_out[...] = jnp.concatenate(
        [total, jnp.zeros((SLOTS, BLOCK - 2 * SLOTS), jnp.float32)], axis=1
    )


def basis(pieces, *operands):
    return pl.pallas_call(
        basis_kernel,
        out_shape=(
            jax.ShapeDtypeStruct((BLOCKS * SLOTS * PITCH, BLOCK), jnp.float32),
            jax.ShapeDtypeStruct((SLOTS, BLOCK), jnp.float32),
        ),
        in_specs=[VMEM] * 5,
        out_specs=(VMEM, VMEM),
        scratch_shapes=[
            pltpu.VMEM((NFACTORS, SPAN, COLS), jnp.bfloat16),
            pltpu.VMEM((NFACTORS, SPAN, COLS), jnp.bfloat16),
        ],
        compiler_params=pltpu.CompilerParams(vmem_limit_bytes=LIMIT),
        name="basis",
    )(*pieces, *operands)


def solve_pair(corner, heads):
    (a, b), (c, d) = corner
    inverse = 1.0 / (a * d - b * c)
    return (d * heads[0] - b * heads[1]) * inverse, (a * heads[1] - c * heads[0]) * inverse


def solve_corner(corner, heads):
    first = [row[:2] for row in corner[:2]]
    right = [solve_pair(first, [corner[0][col], corner[1][col]]) for col in (2, 3)]
    upper = solve_pair(first, heads[:2])
    rest = [
        [
            corner[row][col] - corner[row][0] * right[col - 2][0] - corner[row][1] * right[col - 2][1]
            for col in (2, 3)
        ]
        for row in (2, 3)
    ]
    lower = solve_pair(
        rest,
        [heads[row] - corner[row][0] * upper[0] - corner[row][1] * upper[1] for row in (2, 3)],
    )
    return (
        *(upper[row] - right[0][row] * lower[0] - right[1][row] * lower[1] for row in range(2)),
        *lower,
    )


def solve_kernel(grams, planes, sheet, model_out, stamps):
    total = grams[0] + grams[1] + grams[2] + grams[3]
    cross = total[:, SLOTS : 2 * SLOTS]
    normal = total[:, :SLOTS] + cross + cross.T
    row_id = lax.broadcasted_iota(jnp.int32, (SLOTS, SLOTS), 0)
    col_id = lax.broadcasted_iota(jnp.int32, (SLOTS, SLOTS), 1)
    diagonal = jnp.logical_and(row_id == col_id, row_id < NBASIS)
    trace = jnp.sum(jnp.where(diagonal, normal, 0.0), keepdims=True)
    matrix = normal + jnp.where(diagonal, RIDGE * trace / NBASIS, 0.0)
    for step in range(0, NBASIS, 4):
        columns = [
            jnp.broadcast_to(matrix[:, step + part : step + part + 1], (SLOTS, SLOTS))
            for part in range(4)
        ]
        heads = [matrix[step + part : step + part + 1] for part in range(4)]
        corner = [[columns[col][step + row : step + row + 1] for col in range(4)] for row in range(4)]
        solved = solve_corner(corner, heads)
        others = matrix
        for part in range(4):
            others = others - columns[part] * solved[part]
        matrix = others
        for part in range(4):
            matrix = jnp.where(row_id == step + part, solved[part], matrix)
    answer = jnp.broadcast_to(matrix[:, NBASIS : NBASIS + 1], (SLOTS, BLOCK))
    for block in range(BLOCKS):
        model = jnp.zeros((ROWS, BLOCK), jnp.float32)
        for plane in range(NBASIS):
            factor = jnp.broadcast_to(answer[plane : plane + 1, :], (ROWS, BLOCK))
            at = (block * SLOTS + plane) * PITCH
            model = model + factor * planes[at : at + ROWS, :]
        model_out[:, block * BLOCK : (block + 1) * BLOCK] = model
    difference = sheet[ROWS : 2 * ROWS, :] - model_out[...]
    tile, row_move, col_move = (noted_number(sheet, part) for part in range(3))
    moved = pltpu.roll(difference, lax.rem(row_move + ROWS, ROWS), axis=0)
    moved = pltpu.roll(moved, lax.rem(col_move + COLS, COLS), axis=1)
    from_row = lax.broadcasted_iota(jnp.int32, (ROWS, COLS), 0) - row_move
    from_col = lax.broadcasted_iota(jnp.int32, (ROWS, COLS), 1) - col_move
    inside = (from_row >= 0) & (from_row < ROWS) & (from_col >= 0) & (from_col < COLS)
    placed = jnp.where(inside, moved, 0.0)
    for place in range(LINE):
        mine = lax.bitwise_and(tile, LINE - 1) == place
        for block in range(BLOCKS):
            stamps[place, block * ROWS : (block + 1) * ROWS, :] = jnp.where(
                mine, placed[:, block * BLOCK : (block + 1) * BLOCK], 0.0
            )
        stamps[place, TALL:, :] = jnp.full(
            (NOTED - TALL, BLOCK), tile.astype(jnp.float32), jnp.float32
        )


def solve(grams, planes, sheet):
    return pl.pallas_call(
        solve_kernel,
        out_shape=(
            jax.ShapeDtypeStruct((ROWS, COLS), jnp.float32),
            jax.ShapeDtypeStruct((LINE, NOTED, BLOCK), jnp.float32),
        ),
        in_specs=[VMEM, VMEM, VMEM],
        out_specs=(VMEM, VMEM),
        compiler_params=pltpu.CompilerParams(vmem_limit_bytes=LIMIT),
        name="solve",
    )(grams, planes, sheet)


def gather_kernel(stamps, to_own, to_flip, to_next, to_far):
    visit = lax.axis_index("visit")
    even = lax.rem(visit // LINE, 2) == 0
    low = lax.rem(visit, LINE) < LINE // 2
    targets = (
        visit,
        jnp.where(even, visit + LINE, visit - LINE),
        jnp.where(even, visit - LINE, visit + LINE),
        jnp.where(low, visit + 2 * LINE, visit - 2 * LINE),
    )
    for target, out in zip(targets, (to_own, to_flip, to_next, to_far)):
        number = target.astype(jnp.float32)
        hits = [stamps[place, TALL:, :] == number for place in range(LINE)]
        count = jnp.zeros((NOTED - TALL, BLOCK), jnp.float32)
        for hit in hits:
            count = count + jnp.where(hit, 1.0, 0.0)
        out[TALL:, :] = count
        for block in range(BLOCKS):
            rows = slice(block * ROWS, (block + 1) * ROWS)
            total = jnp.zeros((ROWS, BLOCK), jnp.float32)
            for place in range(LINE):
                total = total + jnp.where(hits[place][:1], stamps[place, rows, :], 0.0)
            out[rows, :] = total


def gather(stamps):
    shape = jax.ShapeDtypeStruct((NOTED, BLOCK), jnp.float32)
    return pl.pallas_call(
        gather_kernel,
        out_shape=(shape,) * 4,
        in_specs=[VMEM],
        out_specs=(VMEM,) * 4,
        compiler_params=pltpu.CompilerParams(vmem_limit_bytes=LIMIT),
        name="gather",
    )(stamps)


def mean_kernel(part_a, part_b, part_c, part_d, coadd):
    parts = (part_a, part_b, part_c, part_d)
    count = sum(part[TALL:, :] for part in parts)
    count = jnp.maximum(count[:1], 1.0)
    for block in range(BLOCKS):
        rows = slice(block * ROWS, (block + 1) * ROWS)
        total = sum(part[rows, :] for part in parts)
        coadd[:, block * BLOCK : (block + 1) * BLOCK] = total / count


def mean(*parts):
    return pl.pallas_call(
        mean_kernel,
        out_shape=jax.ShapeDtypeStruct((ROWS, COLS), jnp.float32),
        in_specs=[VMEM] * 4,
        out_specs=VMEM,
        compiler_params=pltpu.CompilerParams(vmem_limit_bytes=LIMIT),
        name="mean",
    )(*parts)


def shards(template, science, inverse_variance, intersections):
    visits = lax.axis_size("visit")
    groups = [list(range(first, first + PLANE)) for first in range(0, visits, PLANE)]
    upward = [(i, i + PLANE) for i in range(visits - PLANE)]
    downward = [(target, source) for source, target in upward]
    own = intersections[0]
    below = lax.ppermute(own, "visit", upward)
    above = lax.ppermute(own, "visit", downward)
    sheet, table = prepare(
        own, science[0, 0], inverse_variance[0, 0], jnp.asarray(tables())
    )
    window = lax.all_to_all(spread(template[0]), "visit", 0, 0, axis_index_groups=groups)
    piece_own, piece_up, piece_down = serve(window, sheet, below, above)
    from_above = lax.ppermute(piece_down, "visit", downward)
    from_below = lax.ppermute(piece_up, "visit", upward)
    planes, gram = basis((piece_own, from_above, from_below), sheet, table)
    grams = lax.all_gather(gram, "patch")
    model, stamps = solve(grams, planes, sheet)
    lines = [list(range(first, first + LINE)) for first in range(0, visits, LINE)]
    to_own, to_flip, to_next, to_far = gather(
        lax.all_to_all(stamps, "visit", 0, 0, axis_index_groups=lines)
    )
    flip = [(i, i ^ LINE) for i in range(visits)]
    following = [(i, ((i + LINE) ^ LINE) - LINE) for i in range(LINE, visits - LINE)]
    far = [(i, i + 2 * LINE if i % LINE < LINE // 2 else i - 2 * LINE) for i in range(visits)]
    far = [(source, target) for source, target in far if 0 <= target < visits]
    from_far = lax.ppermute(to_far, "visit", far)
    from_next = lax.ppermute(to_next, "visit", following)
    from_flip = lax.ppermute(to_flip, "visit", flip)
    difference = sheet[ROWS : 2 * ROWS] - model
    return (difference[None, None], mean(to_own, from_flip, from_next, from_far)[None])


def solution(mesh):
    in_specs = (
        P("patch", "visit", None),
        P("visit", "patch", None, None),
        P("visit", "patch", None, None),
        P("visit", "patch", None),
    )
    out_specs = (P("visit", "patch", None, None), P("patch", "visit", None))
    return jax.shard_map(shards, mesh=mesh, in_specs=in_specs, out_specs=out_specs, check_vma=False)
```

```python
import functools
import math

import jax
import jax.numpy as jnp
import ml_dtypes
import numpy as np
from jax import lax
from jax.experimental import pallas as pl
from jax.experimental.pallas import tpu as pltpu
from jax.sharding import PartitionSpec as P

KHALF = 10
SHIFT = 6
REACH = 6
NBASIS = 28
ROWS = 64
COLS = 512
PLANE = 8
LINE = 4
SPAN = 96
SLOTS = 32
BLOCK = 128
BLOCKS = COLS // BLOCK
PITCH = 72
TALL = BLOCKS * ROWS
NOTED = TALL + 8
HALF = 32
CHUNK = 32
DEPTH = 64

SIGMAS = (1.0, 2.0, 4.0)
DEGREES = (4, 2, 2)
RIDGE = 0.01
LIMIT = 32 * 1024 * 1024
BESIDE = 5
BESIDE_ROWS = -(-(NBASIS - 1) // BESIDE) * HALF

VMEM = pl.BlockSpec(memory_space=pltpu.VMEM)
HBM = pl.BlockSpec(memory_space=pltpu.HBM)


def factor_table():
    listed = []
    for width_sigma, degree in zip(SIGMAS, DEGREES):
        for exponent in range(degree + 1):
            values = [
                math.exp(-(offset * offset) / (2.0 * width_sigma * width_sigma))
                * (offset / KHALF) ** exponent
                for offset in range(-KHALF, KHALF + 1)
            ]
            scale_norm = math.sqrt(sum((entry * entry for entry in values)))
            listed.append([entry / scale_norm for entry in values])
    return np.array(listed, dtype=np.float32)


def row_factors_by_column_factor():
    groups = []
    first = 0
    for degree in DEGREES:
        for power_col in range(degree + 1):
            groups.append([first + power_row for power_row in range(degree + 1 - power_col)])
        first += degree + 1
    return groups


GROUPS = row_factors_by_column_factor()
NFACTORS = len(GROUPS)


def split_constant(values):
    high = values.astype(ml_dtypes.bfloat16)
    low = (values - high.astype(np.float32)).astype(ml_dtypes.bfloat16)
    return high, low


def tables():
    table = factor_table()
    distance = np.arange(2 * BLOCK)[:, None] - np.arange(BLOCK)[None, :]
    bands = np.zeros((2 * BLOCK, NFACTORS, BLOCK), np.float32)
    for offset in range(2 * KHALF + 1):
        bands += table[None, :, offset, None] * (distance == offset)[:, None, :]
    columns = split_constant(bands.reshape(2 * BLOCK, NFACTORS * BLOCK))
    distance = np.arange(DEPTH)[None, :] - np.arange(HALF)[:, None]
    chosen = [index for group in GROUPS for index in group]
    bands = np.zeros((len(chosen), HALF, DEPTH), np.float32)
    for offset in range(2 * KHALF + 1):
        bands += table[chosen, offset][:, None, None] * (distance == offset)[None]
    high, low = split_constant(bands)
    rows = np.zeros((BESIDE_ROWS, NFACTORS * BLOCK), ml_dtypes.bfloat16)
    for plane, band in enumerate(np.concatenate([high, high, low], axis=2)):
        row, lane = row_band_place(plane)
        rows[row : row + HALF, lane : lane + 3 * DEPTH] = band
    return np.concatenate([*columns, rows])


def row_band_place(plane):
    return plane // BESIDE * HALF, plane % BESIDE * 2 * BLOCK


def split(values):
    high = values.astype(jnp.bfloat16)
    low = (values - high.astype(jnp.float32)).astype(jnp.bfloat16)
    return high, low


def put_plane(planes, slot, row, values):
    for block in range(BLOCKS):
        at = (block * SLOTS + slot) * PITCH + row
        planes[at : at + values.shape[0], :] = values[:, block * BLOCK : (block + 1) * BLOCK]


def spread_kernel(tile, copies):
    for copy in range(PLANE):
        for block in range(BLOCKS):
            copies[copy, block * ROWS : (block + 1) * ROWS, :] = tile[
                :, block * BLOCK : (block + 1) * BLOCK
            ]


def spread(tile):
    return pl.pallas_call(
        spread_kernel,
        out_shape=jax.ShapeDtypeStruct((PLANE, TALL, BLOCK), jnp.float32),
        in_specs=[VMEM],
        out_specs=VMEM,
        compiler_params=pltpu.CompilerParams(vmem_limit_bytes=LIMIT),
        name="spread",
    )(tile)


def noted_number(sheet, part):
    return sheet[2 * ROWS : 2 * ROWS + 1, :BLOCK][0, part].astype(jnp.int32)


def prepare_kernel(
    entries, science, weight, table,
    sheet, table_out,
):
    lane = lax.broadcasted_iota(jnp.int32, (8, COLS), 1)
    noted = jnp.zeros((8, COLS), jnp.float32)
    for part in range(3):
        noted = jnp.where(lane == part, entries[...][0, part].astype(jnp.float32), noted)
    sheet[2 * ROWS :, :] = noted
    values = jnp.sqrt(weight[...])
    sheet[:ROWS, :] = values
    sheet[ROWS : 2 * ROWS, :] = values * science[...]
    table_out[...] = table[...]


def prepare(entries, science, weight, table):
    return pl.pallas_call(
        prepare_kernel,
        out_shape=(
            jax.ShapeDtypeStruct((2 * ROWS + 8, COLS), jnp.float32),
            jax.ShapeDtypeStruct(table.shape, table.dtype),
        ),
        in_specs=[VMEM] * 4,
        out_specs=(VMEM,) * 2,
        compiler_params=pltpu.CompilerParams(vmem_limit_bytes=LIMIT),
        name="prepare",
    )(entries, science, weight, table)


def serve_kernel(window, sheet, below, above, piece_own, piece_up, piece_down):
    base = (lax.axis_index("visit") // PLANE) * PLANE
    own = (noted_number(sheet, 0), noted_number(sheet, 1))
    others = [(entries[...][0, 0], entries[...][0, 1]) for entries in (below, above)]
    for (asked, row_move), piece in zip((own, *others), (piece_own, piece_down, piece_up)):
        start = (asked - base) * ROWS + row_move - KHALF
        first = lax.shift_right_arithmetic(start, 3)
        for part in range(SPAN // 8):
            strip = first + part
            inside = jnp.logical_and(strip >= 0, strip < PLANE * ROWS // 8)
            strip = jnp.clip(strip, 0, PLANE * ROWS // 8 - 1)
            tile = lax.shift_right_logical(strip, 3)
            row = pl.multiple_of(lax.bitwise_and(strip, 7) * 8, 8)
            for block in range(BLOCKS):
                rows = window[tile, pl.ds(block * ROWS + row, 8), :]
                piece[8 * part : 8 * part + 8, block * BLOCK : (block + 1) * BLOCK] = jnp.where(
                    inside, rows, 0.0
                )


def serve(window, sheet, below, above):
    shape = jax.ShapeDtypeStruct((SPAN, COLS), jnp.float32)
    return pl.pallas_call(
        serve_kernel,
        out_shape=(shape, shape, shape),
        in_specs=[VMEM] * 4,
        out_specs=(VMEM, VMEM, VMEM),
        compiler_params=pltpu.CompilerParams(vmem_limit_bytes=LIMIT),
        name="serve",
    )(window, sheet, below, above)


def basis_kernel(
    piece_a, piece_b, piece_c, sheet, table,
    planes, gram_out,
    high_rows, low_rows,
):
    remainder = lax.bitwise_and(noted_number(sheet, 1) + SHIFT, 7)
    rows = piece_a[...] + piece_b[...] + piece_c[...]
    rows = pltpu.roll(rows, lax.rem(SPAN - remainder, SPAN), axis=0)
    padded = jnp.concatenate([rows, jnp.zeros((SPAN, BLOCK), jnp.float32)], axis=1)
    cutout = pltpu.roll(padded, KHALF - noted_number(sheet, 2), axis=1)
    cut_high, cut_low = split(cutout)
    col_high, col_low = table[: 2 * BLOCK, :], table[2 * BLOCK : 4 * BLOCK, :]
    for block in range(COLS // BLOCK):
        cols = slice(block * BLOCK, (block + 2) * BLOCK)
        both = jnp.concatenate([cut_high[:, cols], cut_low[:, cols]], axis=0)
        main = jnp.dot(both, col_high, preferred_element_type=jnp.float32)
        rest = jnp.dot(cut_high[:, cols], col_low, preferred_element_type=jnp.float32)
        across = main[:SPAN] + main[SPAN:] + rest
        across_high, across_low = split(across)
        for factor in range(NFACTORS):
            take = slice(factor * BLOCK, (factor + 1) * BLOCK)
            put = slice(block * BLOCK, (block + 1) * BLOCK)
            high_rows[factor, :, put] = across_high[:, take]
            low_rows[factor, :, put] = across_low[:, take]
    first = 0
    for factor, group in enumerate(GROUPS):
        bands = []
        for member in range(len(group)):
            row, lane = row_band_place(first + member)
            row += 4 * BLOCK
            bands.append(table[row : row + HALF, lane : lane + 3 * DEPTH])
        bands = jnp.concatenate(bands, axis=0)
        for half in range(ROWS // HALF):
            take = slice(half * HALF, half * HALF + DEPTH)
            high = high_rows[factor, take, :]
            stacked = jnp.concatenate([high, low_rows[factor, take, :], high], axis=0)
            out = jnp.dot(bands, stacked, preferred_element_type=jnp.float32)
            for member in range(len(group)):
                scaled = (
                    out[member * HALF : (member + 1) * HALF]
                    * sheet[half * HALF : (half + 1) * HALF, :]
                )
                put_plane(planes, first + member, half * HALF, scaled)
        first += len(group)
    put_plane(planes, NBASIS - 1, 0, sheet[:ROWS, :])
    put_plane(planes, NBASIS, 0, sheet[ROWS : 2 * ROWS, :])
    for slot in range(NBASIS + 1, SLOTS):
        put_plane(planes, slot, 0, jnp.zeros((ROWS, COLS), jnp.float32))
    def gram_step(chunk, total):
        highs, lows = [], []
        for inner in range(CHUNK):
            for block in range(BLOCKS):
                row = block * SLOTS * PITCH + chunk * CHUNK + inner
                high, low = split(planes[pl.ds(row, SLOTS, stride=PITCH), :])
                highs.append(high)
                lows.append(low)
        high = jnp.concatenate(highs, axis=1)
        low = jnp.concatenate(lows, axis=1)
        both = jnp.concatenate([high, low], axis=0)
        return total + lax.dot_general(
            high, both, (((1,), (1,)), ((), ())), preferred_element_type=jnp.float32
        )

    total = lax.fori_loop(0, ROWS // CHUNK, gram_step, jnp.zeros((SLOTS, 2 * SLOTS), jnp.float32))
    gram_out[...] = jnp.concatenate(
        [total, jnp.zeros((SLOTS, BLOCK - 2 * SLOTS), jnp.float32)], axis=1
    )


def basis(pieces, *operands):
    return pl.pallas_call(
        basis_kernel,
        out_shape=(
            jax.ShapeDtypeStruct((BLOCKS * SLOTS * PITCH, BLOCK), jnp.float32),
            jax.ShapeDtypeStruct((SLOTS, BLOCK), jnp.float32),
        ),
        in_specs=[VMEM] * 5,
        out_specs=(VMEM, VMEM),
        scratch_shapes=[
            pltpu.VMEM((NFACTORS, SPAN, COLS), jnp.bfloat16),
            pltpu.VMEM((NFACTORS, SPAN, COLS), jnp.bfloat16),
        ],
        compiler_params=pltpu.CompilerParams(vmem_limit_bytes=LIMIT),
        name="basis",
    )(*pieces, *operands)


def solve_pair(corner, heads):
    (a, b), (c, d) = corner
    inverse = 1.0 / (a * d - b * c)
    return (d * heads[0] - b * heads[1]) * inverse, (a * heads[1] - c * heads[0]) * inverse


def solve_corner(corner, heads):
    first = [row[:2] for row in corner[:2]]
    right = [solve_pair(first, [corner[0][col], corner[1][col]]) for col in (2, 3)]
    upper = solve_pair(first, heads[:2])
    rest = [
        [
            corner[row][col] - corner[row][0] * right[col - 2][0] - corner[row][1] * right[col - 2][1]
            for col in (2, 3)
        ]
        for row in (2, 3)
    ]
    lower = solve_pair(
        rest,
        [heads[row] - corner[row][0] * upper[0] - corner[row][1] * upper[1] for row in (2, 3)],
    )
    return (
        *(upper[row] - right[0][row] * lower[0] - right[1][row] * lower[1] for row in range(2)),
        *lower,
    )


def solve_kernel(grams, planes, sheet, model_out, stamps):
    total = grams[0] + grams[1] + grams[2] + grams[3]
    cross = total[:, SLOTS : 2 * SLOTS]
    normal = total[:, :SLOTS] + cross + cross.T
    row_id = lax.broadcasted_iota(jnp.int32, (SLOTS, SLOTS), 0)
    col_id = lax.broadcasted_iota(jnp.int32, (SLOTS, SLOTS), 1)
    diagonal = jnp.logical_and(row_id == col_id, row_id < NBASIS)
    trace = jnp.sum(jnp.where(diagonal, normal, 0.0), keepdims=True)
    matrix = normal + jnp.where(diagonal, RIDGE * trace / NBASIS, 0.0)
    for step in range(0, NBASIS, 4):
        columns = [
            jnp.broadcast_to(matrix[:, step + part : step + part + 1], (SLOTS, SLOTS))
            for part in range(4)
        ]
        heads = [matrix[step + part : step + part + 1] for part in range(4)]
        corner = [[columns[col][step + row : step + row + 1] for col in range(4)] for row in range(4)]
        solved = solve_corner(corner, heads)
        others = matrix
        for part in range(4):
            others = others - columns[part] * solved[part]
        matrix = others
        for part in range(4):
            matrix = jnp.where(row_id == step + part, solved[part], matrix)
    answer = jnp.broadcast_to(matrix[:, NBASIS : NBASIS + 1], (SLOTS, BLOCK))
    for block in range(BLOCKS):
        model = jnp.zeros((ROWS, BLOCK), jnp.float32)
        for plane in range(NBASIS):
            factor = jnp.broadcast_to(answer[plane : plane + 1, :], (ROWS, BLOCK))
            at = (block * SLOTS + plane) * PITCH
            model = model + factor * planes[at : at + ROWS, :]
        model_out[:, block * BLOCK : (block + 1) * BLOCK] = model
    difference = sheet[ROWS : 2 * ROWS, :] - model_out[...]
    tile, row_move, col_move = (noted_number(sheet, part) for part in range(3))
    moved = pltpu.roll(difference, lax.rem(row_move + ROWS, ROWS), axis=0)
    moved = pltpu.roll(moved, lax.rem(col_move + COLS, COLS), axis=1)
    from_row = lax.broadcasted_iota(jnp.int32, (ROWS, COLS), 0) - row_move
    from_col = lax.broadcasted_iota(jnp.int32, (ROWS, COLS), 1) - col_move
    inside = (from_row >= 0) & (from_row < ROWS) & (from_col >= 0) & (from_col < COLS)
    placed = jnp.where(inside, moved, 0.0)
    for place in range(LINE):
        mine = lax.bitwise_and(tile, LINE - 1) == place
        for block in range(BLOCKS):
            stamps[place, block * ROWS : (block + 1) * ROWS, :] = jnp.where(
                mine, placed[:, block * BLOCK : (block + 1) * BLOCK], 0.0
            )
        stamps[place, TALL:, :] = jnp.full(
            (NOTED - TALL, BLOCK), tile.astype(jnp.float32), jnp.float32
        )


def solve(grams, planes, sheet):
    return pl.pallas_call(
        solve_kernel,
        out_shape=(
            jax.ShapeDtypeStruct((ROWS, COLS), jnp.float32),
            jax.ShapeDtypeStruct((LINE, NOTED, BLOCK), jnp.float32),
        ),
        in_specs=[VMEM, VMEM, VMEM],
        out_specs=(VMEM, VMEM),
        compiler_params=pltpu.CompilerParams(vmem_limit_bytes=LIMIT),
        name="solve",
    )(grams, planes, sheet)


def gather_kernel(stamps, to_own, to_flip, to_next, to_far):
    visit = lax.axis_index("visit")
    even = lax.rem(visit // LINE, 2) == 0
    low = lax.rem(visit, LINE) < LINE // 2
    targets = (
        visit,
        jnp.where(even, visit + LINE, visit - LINE),
        jnp.where(even, visit - LINE, visit + LINE),
        jnp.where(low, visit + 2 * LINE, visit - 2 * LINE),
    )
    for target, out in zip(targets, (to_own, to_flip, to_next, to_far)):
        number = target.astype(jnp.float32)
        hits = [stamps[place, TALL:, :] == number for place in range(LINE)]
        count = jnp.zeros((NOTED - TALL, BLOCK), jnp.float32)
        for hit in hits:
            count = count + jnp.where(hit, 1.0, 0.0)
        out[TALL:, :] = count
        for block in range(BLOCKS):
            rows = slice(block * ROWS, (block + 1) * ROWS)
            total = jnp.zeros((ROWS, BLOCK), jnp.float32)
            for place in range(LINE):
                total = total + jnp.where(hits[place][:1], stamps[place, rows, :], 0.0)
            out[rows, :] = total


def gather(stamps):
    shape = jax.ShapeDtypeStruct((NOTED, BLOCK), jnp.float32)
    return pl.pallas_call(
        gather_kernel,
        out_shape=(shape,) * 4,
        in_specs=[VMEM],
        out_specs=(VMEM,) * 4,
        compiler_params=pltpu.CompilerParams(vmem_limit_bytes=LIMIT),
        name="gather",
    )(stamps)


def mean_kernel(part_a, part_b, part_c, part_d, coadd):
    parts = (part_a, part_b, part_c, part_d)
    count = sum(part[TALL:, :] for part in parts)
    count = jnp.maximum(count[:1], 1.0)
    for block in range(BLOCKS):
        rows = slice(block * ROWS, (block + 1) * ROWS)
        total = sum(part[rows, :] for part in parts)
        coadd[:, block * BLOCK : (block + 1) * BLOCK] = total / count


def mean(*parts):
    return pl.pallas_call(
        mean_kernel,
        out_shape=jax.ShapeDtypeStruct((ROWS, COLS), jnp.float32),
        in_specs=[VMEM] * 4,
        out_specs=VMEM,
        compiler_params=pltpu.CompilerParams(vmem_limit_bytes=LIMIT),
        name="mean",
    )(*parts)


def shards(template, science, inverse_variance, intersections):
    visits = lax.axis_size("visit")
    groups = [list(range(first, first + PLANE)) for first in range(0, visits, PLANE)]
    upward = [(i, i + PLANE) for i in range(visits - PLANE)]
    downward = [(target, source) for source, target in upward]
    own = intersections[0]
    below = lax.ppermute(own, "visit", upward)
    above = lax.ppermute(own, "visit", downward)
    sheet, table = prepare(
        own, science[0, 0], inverse_variance[0, 0], jnp.asarray(tables())
    )
    window = lax.all_to_all(spread(template[0]), "visit", 0, 0, axis_index_groups=groups)
    piece_own, piece_up, piece_down = serve(window, sheet, below, above)
    from_above = lax.ppermute(piece_down, "visit", downward)
    from_below = lax.ppermute(piece_up, "visit", upward)
    planes, gram = basis((piece_own, from_above, from_below), sheet, table)
    grams = lax.all_gather(gram, "patch")
    model, stamps = solve(grams, planes, sheet)
    lines = [list(range(first, first + LINE)) for first in range(0, visits, LINE)]
    to_own, to_flip, to_next, to_far = gather(
        lax.all_to_all(stamps, "visit", 0, 0, axis_index_groups=lines)
    )
    flip = [(i, i ^ LINE) for i in range(visits)]
    following = [(i, ((i + LINE) ^ LINE) - LINE) for i in range(LINE, visits - LINE)]
    far = [(i, i + 2 * LINE if i % LINE < LINE // 2 else i - 2 * LINE) for i in range(visits)]
    far = [(source, target) for source, target in far if 0 <= target < visits]
    from_far = lax.ppermute(to_far, "visit", far)
    from_flip = lax.ppermute(to_flip, "visit", flip)
    from_next = lax.ppermute(to_next, "visit", following)
    difference = sheet[ROWS : 2 * ROWS] - model
    return (difference[None, None], mean(to_own, from_next, from_flip, from_far)[None])


def solution(mesh):
    in_specs = (
        P("patch", "visit", None),
        P("visit", "patch", None, None),
        P("visit", "patch", None, None),
        P("visit", "patch", None),
    )
    out_specs = (P("visit", "patch", None, None), P("patch", "visit", None))
    return jax.shard_map(shards, mesh=mesh, in_specs=in_specs, out_specs=out_specs, check_vma=False)
```

```python
import functools
import math

import jax
import jax.numpy as jnp
import ml_dtypes
import numpy as np
from jax import lax
from jax.experimental import pallas as pl
from jax.experimental.pallas import tpu as pltpu
from jax.sharding import PartitionSpec as P

KHALF = 10
SHIFT = 6
REACH = 6
NBASIS = 28
ROWS = 64
COLS = 512
PLANE = 8
LINE = 4
SPAN = 96
SENT = 88
SLOTS = 32
BLOCK = 128
BLOCKS = COLS // BLOCK
PITCH = 72
TALL = BLOCKS * ROWS
NOTED = TALL + 8
HALF = 32
CHUNK = 32
DEPTH = 64

SIGMAS = (1.0, 2.0, 4.0)
DEGREES = (4, 2, 2)
RIDGE = 0.01
LIMIT = 32 * 1024 * 1024
BESIDE = 5
BESIDE_ROWS = -(-(NBASIS - 1) // BESIDE) * HALF

VMEM = pl.BlockSpec(memory_space=pltpu.VMEM)
HBM = pl.BlockSpec(memory_space=pltpu.HBM)


def factor_table():
    listed = []
    for width_sigma, degree in zip(SIGMAS, DEGREES):
        for exponent in range(degree + 1):
            values = [
                math.exp(-(offset * offset) / (2.0 * width_sigma * width_sigma))
                * (offset / KHALF) ** exponent
                for offset in range(-KHALF, KHALF + 1)
            ]
            scale_norm = math.sqrt(sum((entry * entry for entry in values)))
            listed.append([entry / scale_norm for entry in values])
    return np.array(listed, dtype=np.float32)


def row_factors_by_column_factor():
    groups = []
    first = 0
    for degree in DEGREES:
        for power_col in range(degree + 1):
            groups.append([first + power_row for power_row in range(degree + 1 - power_col)])
        first += degree + 1
    return groups


GROUPS = row_factors_by_column_factor()
NFACTORS = len(GROUPS)


def split_constant(values):
    high = values.astype(ml_dtypes.bfloat16)
    low = (values - high.astype(np.float32)).astype(ml_dtypes.bfloat16)
    return high, low


def tables():
    table = factor_table()
    distance = np.arange(2 * BLOCK)[:, None] - np.arange(BLOCK)[None, :]
    bands = np.zeros((2 * BLOCK, NFACTORS, BLOCK), np.float32)
    for offset in range(2 * KHALF + 1):
        bands += table[None, :, offset, None] * (distance == offset)[:, None, :]
    columns = split_constant(bands.reshape(2 * BLOCK, NFACTORS * BLOCK))
    distance = np.arange(DEPTH)[None, :] - np.arange(HALF)[:, None]
    chosen = [index for group in GROUPS for index in group]
    bands = np.zeros((len(chosen), HALF, DEPTH), np.float32)
    for offset in range(2 * KHALF + 1):
        bands += table[chosen, offset][:, None, None] * (distance == offset)[None]
    high, low = split_constant(bands)
    rows = np.zeros((BESIDE_ROWS, NFACTORS * BLOCK), ml_dtypes.bfloat16)
    for plane, band in enumerate(np.concatenate([high, high, low], axis=2)):
        row, lane = row_band_place(plane)
        rows[row : row + HALF, lane : lane + 3 * DEPTH] = band
    return np.concatenate([*columns, rows])


def row_band_place(plane):
    return plane // BESIDE * HALF, plane % BESIDE * 2 * BLOCK


def split(values):
    high = values.astype(jnp.bfloat16)
    low = (values - high.astype(jnp.float32)).astype(jnp.bfloat16)
    return high, low


def put_plane(planes, slot, row, values):
    for block in range(BLOCKS):
        at = (block * SLOTS + slot) * PITCH + row
        planes[at : at + values.shape[0], :] = values[:, block * BLOCK : (block + 1) * BLOCK]


def spread_kernel(tile, copies):
    for copy in range(PLANE):
        for block in range(BLOCKS):
            copies[copy, block * ROWS : (block + 1) * ROWS, :] = tile[
                :, block * BLOCK : (block + 1) * BLOCK
            ]


def spread(tile):
    return pl.pallas_call(
        spread_kernel,
        out_shape=jax.ShapeDtypeStruct((PLANE, TALL, BLOCK), jnp.float32),
        in_specs=[VMEM],
        out_specs=VMEM,
        compiler_params=pltpu.CompilerParams(vmem_limit_bytes=LIMIT),
        name="spread",
    )(tile)


def noted_number(sheet, part):
    return sheet[2 * ROWS : 2 * ROWS + 1, :BLOCK][0, part].astype(jnp.int32)


def prepare_kernel(
    entries, science, weight, table,
    sheet, table_out,
):
    lane = lax.broadcasted_iota(jnp.int32, (8, COLS), 1)
    noted = jnp.zeros((8, COLS), jnp.float32)
    for part in range(3):
        noted = jnp.where(lane == part, entries[...][0, part].astype(jnp.float32), noted)
    sheet[2 * ROWS :, :] = noted
    values = jnp.sqrt(weight[...])
    sheet[:ROWS, :] = values
    sheet[ROWS : 2 * ROWS, :] = values * science[...]
    table_out[...] = table[...]


def prepare(entries, science, weight, table):
    return pl.pallas_call(
        prepare_kernel,
        out_shape=(
            jax.ShapeDtypeStruct((2 * ROWS + 8, COLS), jnp.float32),
            jax.ShapeDtypeStruct(table.shape, table.dtype),
        ),
        in_specs=[VMEM] * 4,
        out_specs=(VMEM,) * 2,
        compiler_params=pltpu.CompilerParams(vmem_limit_bytes=LIMIT),
        name="prepare",
    )(entries, science, weight, table)


def serve_kernel(window, sheet, below, above, piece_own, piece_up, piece_down, strips):
    base = (lax.axis_index("visit") // PLANE) * PLANE
    own = (noted_number(sheet, 0), noted_number(sheet, 1))
    others = [(entries[...][0, 0], entries[...][0, 1]) for entries in (below, above)]
    for (asked, row_move), piece in zip((own, *others), (piece_own, piece_down, piece_up)):
        start = (asked - base) * ROWS + row_move - KHALF
        first = lax.shift_right_arithmetic(start, 3)
        for part in range(SPAN // 8):
            strip = first + part
            inside = jnp.logical_and(strip >= 0, strip < PLANE * ROWS // 8)
            strip = jnp.clip(strip, 0, PLANE * ROWS // 8 - 1)
            tile = lax.shift_right_logical(strip, 3)
            row = pl.multiple_of(lax.bitwise_and(strip, 7) * 8, 8)
            for block in range(BLOCKS):
                rows = window[tile, pl.ds(block * ROWS + row, 8), :]
                strips[8 * part : 8 * part + 8, block * BLOCK : (block + 1) * BLOCK] = jnp.where(
                    inside, rows, 0.0
                )
        shift = lax.rem(SPAN - lax.bitwise_and(start, 7), SPAN)
        piece[...] = pltpu.roll(strips[...], shift, axis=0)[:SENT]


def serve(window, sheet, below, above):
    shape = jax.ShapeDtypeStruct((SENT, COLS), jnp.float32)
    return pl.pallas_call(
        serve_kernel,
        out_shape=(shape, shape, shape),
        in_specs=[VMEM] * 4,
        out_specs=(VMEM, VMEM, VMEM),
        scratch_shapes=[pltpu.VMEM((SPAN, COLS), jnp.float32)],
        compiler_params=pltpu.CompilerParams(vmem_limit_bytes=LIMIT),
        name="serve",
    )(window, sheet, below, above)


def basis_kernel(
    piece_a, piece_b, piece_c, sheet, table,
    planes, gram_out,
    high_rows, low_rows,
):
    rows = piece_a[...] + piece_b[...] + piece_c[...]
    rows = jnp.concatenate([rows, jnp.zeros((SPAN - SENT, COLS), jnp.float32)], axis=0)
    padded = jnp.concatenate([rows, jnp.zeros((SPAN, BLOCK), jnp.float32)], axis=1)
    cutout = pltpu.roll(padded, KHALF - noted_number(sheet, 2), axis=1)
    cut_high, cut_low = split(cutout)
    col_high, col_low = table[: 2 * BLOCK, :], table[2 * BLOCK : 4 * BLOCK, :]
    for block in range(COLS // BLOCK):
        cols = slice(block * BLOCK, (block + 2) * BLOCK)
        both = jnp.concatenate([cut_high[:, cols], cut_low[:, cols]], axis=0)
        main = jnp.dot(both, col_high, preferred_element_type=jnp.float32)
        rest = jnp.dot(cut_high[:, cols], col_low, preferred_element_type=jnp.float32)
        across = main[:SPAN] + main[SPAN:] + rest
        across_high, across_low = split(across)
        for factor in range(NFACTORS):
            take = slice(factor * BLOCK, (factor + 1) * BLOCK)
            put = slice(block * BLOCK, (block + 1) * BLOCK)
            high_rows[factor, :, put] = across_high[:, take]
            low_rows[factor, :, put] = across_low[:, take]
    first = 0
    for factor, group in enumerate(GROUPS):
        bands = []
        for member in range(len(group)):
            row, lane = row_band_place(first + member)
            row += 4 * BLOCK
            bands.append(table[row : row + HALF, lane : lane + 3 * DEPTH])
        bands = jnp.concatenate(bands, axis=0)
        for half in range(ROWS // HALF):
            take = slice(half * HALF, half * HALF + DEPTH)
            high = high_rows[factor, take, :]
            stacked = jnp.concatenate([high, low_rows[factor, take, :], high], axis=0)
            out = jnp.dot(bands, stacked, preferred_element_type=jnp.float32)
            for member in range(len(group)):
                scaled = (
                    out[member * HALF : (member + 1) * HALF]
                    * sheet[half * HALF : (half + 1) * HALF, :]
                )
                put_plane(planes, first + member, half * HALF, scaled)
        first += len(group)
    put_plane(planes, NBASIS - 1, 0, sheet[:ROWS, :])
    put_plane(planes, NBASIS, 0, sheet[ROWS : 2 * ROWS, :])
    for slot in range(NBASIS + 1, SLOTS):
        put_plane(planes, slot, 0, jnp.zeros((ROWS, COLS), jnp.float32))
    def gram_step(chunk, total):
        highs, lows = [], []
        for inner in range(CHUNK):
            for block in range(BLOCKS):
                row = block * SLOTS * PITCH + chunk * CHUNK + inner
                high, low = split(planes[pl.ds(row, SLOTS, stride=PITCH), :])
                highs.append(high)
                lows.append(low)
        high = jnp.concatenate(highs, axis=1)
        low = jnp.concatenate(lows, axis=1)
        both = jnp.concatenate([high, low], axis=0)
        return total + lax.dot_general(
            high, both, (((1,), (1,)), ((), ())), preferred_element_type=jnp.float32
        )

    total = lax.fori_loop(0, ROWS // CHUNK, gram_step, jnp.zeros((SLOTS, 2 * SLOTS), jnp.float32))
    gram_out[...] = jnp.concatenate(
        [total, jnp.zeros((SLOTS, BLOCK - 2 * SLOTS), jnp.float32)], axis=1
    )


def basis(pieces, *operands):
    return pl.pallas_call(
        basis_kernel,
        out_shape=(
            jax.ShapeDtypeStruct((BLOCKS * SLOTS * PITCH, BLOCK), jnp.float32),
            jax.ShapeDtypeStruct((SLOTS, BLOCK), jnp.float32),
        ),
        in_specs=[VMEM] * 5,
        out_specs=(VMEM, VMEM),
        scratch_shapes=[
            pltpu.VMEM((NFACTORS, SPAN, COLS), jnp.bfloat16),
            pltpu.VMEM((NFACTORS, SPAN, COLS), jnp.bfloat16),
        ],
        compiler_params=pltpu.CompilerParams(vmem_limit_bytes=LIMIT),
        name="basis",
    )(*pieces, *operands)


def solve_pair(corner, heads):
    (a, b), (c, d) = corner
    inverse = 1.0 / (a * d - b * c)
    return (d * heads[0] - b * heads[1]) * inverse, (a * heads[1] - c * heads[0]) * inverse


def solve_corner(corner, heads):
    first = [row[:2] for row in corner[:2]]
    right = [solve_pair(first, [corner[0][col], corner[1][col]]) for col in (2, 3)]
    upper = solve_pair(first, heads[:2])
    rest = [
        [
            corner[row][col] - corner[row][0] * right[col - 2][0] - corner[row][1] * right[col - 2][1]
            for col in (2, 3)
        ]
        for row in (2, 3)
    ]
    lower = solve_pair(
        rest,
        [heads[row] - corner[row][0] * upper[0] - corner[row][1] * upper[1] for row in (2, 3)],
    )
    return (
        *(upper[row] - right[0][row] * lower[0] - right[1][row] * lower[1] for row in range(2)),
        *lower,
    )


def solve_kernel(grams, planes, sheet, model_out, stamps):
    total = grams[0] + grams[1] + grams[2] + grams[3]
    cross = total[:, SLOTS : 2 * SLOTS]
    normal = total[:, :SLOTS] + cross + cross.T
    row_id = lax.broadcasted_iota(jnp.int32, (SLOTS, SLOTS), 0)
    col_id = lax.broadcasted_iota(jnp.int32, (SLOTS, SLOTS), 1)
    diagonal = jnp.logical_and(row_id == col_id, row_id < NBASIS)
    trace = jnp.sum(jnp.where(diagonal, normal, 0.0), keepdims=True)
    matrix = normal + jnp.where(diagonal, RIDGE * trace / NBASIS, 0.0)
    for step in range(0, NBASIS, 4):
        columns = [
            jnp.broadcast_to(matrix[:, step + part : step + part + 1], (SLOTS, SLOTS))
            for part in range(4)
        ]
        heads = [matrix[step + part : step + part + 1] for part in range(4)]
        corner = [[columns[col][step + row : step + row + 1] for col in range(4)] for row in range(4)]
        solved = solve_corner(corner, heads)
        others = matrix
        for part in range(4):
            others = others - columns[part] * solved[part]
        matrix = others
        for part in range(4):
            matrix = jnp.where(row_id == step + part, solved[part], matrix)
    answer = jnp.broadcast_to(matrix[:, NBASIS : NBASIS + 1], (SLOTS, BLOCK))
    for block in range(BLOCKS):
        model = jnp.zeros((ROWS, BLOCK), jnp.float32)
        for plane in range(NBASIS):
            factor = jnp.broadcast_to(answer[plane : plane + 1, :], (ROWS, BLOCK))
            at = (block * SLOTS + plane) * PITCH
            model = model + factor * planes[at : at + ROWS, :]
        model_out[:, block * BLOCK : (block + 1) * BLOCK] = model
    difference = sheet[ROWS : 2 * ROWS, :] - model_out[...]
    tile, row_move, col_move = (noted_number(sheet, part) for part in range(3))
    moved = pltpu.roll(difference, lax.rem(row_move + ROWS, ROWS), axis=0)
    moved = pltpu.roll(moved, lax.rem(col_move + COLS, COLS), axis=1)
    from_row = lax.broadcasted_iota(jnp.int32, (ROWS, COLS), 0) - row_move
    from_col = lax.broadcasted_iota(jnp.int32, (ROWS, COLS), 1) - col_move
    inside = (from_row >= 0) & (from_row < ROWS) & (from_col >= 0) & (from_col < COLS)
    placed = jnp.where(inside, moved, 0.0)
    for place in range(LINE):
        mine = lax.bitwise_and(tile, LINE - 1) == place
        for block in range(BLOCKS):
            stamps[place, block * ROWS : (block + 1) * ROWS, :] = jnp.where(
                mine, placed[:, block * BLOCK : (block + 1) * BLOCK], 0.0
            )
        stamps[place, TALL:, :] = jnp.full(
            (NOTED - TALL, BLOCK), tile.astype(jnp.float32), jnp.float32
        )


def solve(grams, planes, sheet):
    return pl.pallas_call(
        solve_kernel,
        out_shape=(
            jax.ShapeDtypeStruct((ROWS, COLS), jnp.float32),
            jax.ShapeDtypeStruct((LINE, NOTED, BLOCK), jnp.float32),
        ),
        in_specs=[VMEM, VMEM, VMEM],
        out_specs=(VMEM, VMEM),
        compiler_params=pltpu.CompilerParams(vmem_limit_bytes=LIMIT),
        name="solve",
    )(grams, planes, sheet)


def gather_kernel(stamps, to_own, to_flip, to_next, to_far):
    visit = lax.axis_index("visit")
    even = lax.rem(visit // LINE, 2) == 0
    low = lax.rem(visit, LINE) < LINE // 2
    targets = (
        visit,
        jnp.where(even, visit + LINE, visit - LINE),
        jnp.where(even, visit - LINE, visit + LINE),
        jnp.where(low, visit + 2 * LINE, visit - 2 * LINE),
    )
    for target, out in zip(targets, (to_own, to_flip, to_next, to_far)):
        number = target.astype(jnp.float32)
        hits = [stamps[place, TALL:, :] == number for place in range(LINE)]
        count = jnp.zeros((NOTED - TALL, BLOCK), jnp.float32)
        for hit in hits:
            count = count + jnp.where(hit, 1.0, 0.0)
        out[TALL:, :] = count
        for block in range(BLOCKS):
            rows = slice(block * ROWS, (block + 1) * ROWS)
            total = jnp.zeros((ROWS, BLOCK), jnp.float32)
            for place in range(LINE):
                total = total + jnp.where(hits[place][:1], stamps[place, rows, :], 0.0)
            out[rows, :] = total


def gather(stamps):
    shape = jax.ShapeDtypeStruct((NOTED, BLOCK), jnp.float32)
    return pl.pallas_call(
        gather_kernel,
        out_shape=(shape,) * 4,
        in_specs=[VMEM],
        out_specs=(VMEM,) * 4,
        compiler_params=pltpu.CompilerParams(vmem_limit_bytes=LIMIT),
        name="gather",
    )(stamps)


def mean_kernel(part_a, part_b, part_c, part_d, coadd):
    parts = (part_a, part_b, part_c, part_d)
    count = sum(part[TALL:, :] for part in parts)
    count = jnp.maximum(count[:1], 1.0)
    for block in range(BLOCKS):
        rows = slice(block * ROWS, (block + 1) * ROWS)
        total = sum(part[rows, :] for part in parts)
        coadd[:, block * BLOCK : (block + 1) * BLOCK] = total / count


def mean(*parts):
    return pl.pallas_call(
        mean_kernel,
        out_shape=jax.ShapeDtypeStruct((ROWS, COLS), jnp.float32),
        in_specs=[VMEM] * 4,
        out_specs=VMEM,
        compiler_params=pltpu.CompilerParams(vmem_limit_bytes=LIMIT),
        name="mean",
    )(*parts)


def shards(template, science, inverse_variance, intersections):
    visits = lax.axis_size("visit")
    groups = [list(range(first, first + PLANE)) for first in range(0, visits, PLANE)]
    upward = [(i, i + PLANE) for i in range(visits - PLANE)]
    downward = [(target, source) for source, target in upward]
    own = intersections[0]
    below = lax.ppermute(own, "visit", upward)
    above = lax.ppermute(own, "visit", downward)
    sheet, table = prepare(
        own, science[0, 0], inverse_variance[0, 0], jnp.asarray(tables())
    )
    window = lax.all_to_all(spread(template[0]), "visit", 0, 0, axis_index_groups=groups)
    piece_own, piece_up, piece_down = serve(window, sheet, below, above)
    from_above = lax.ppermute(piece_down, "visit", downward)
    from_below = lax.ppermute(piece_up, "visit", upward)
    planes, gram = basis((piece_own, from_above, from_below), sheet, table)
    grams = lax.all_gather(gram, "patch")
    model, stamps = solve(grams, planes, sheet)
    lines = [list(range(first, first + LINE)) for first in range(0, visits, LINE)]
    to_own, to_flip, to_next, to_far = gather(
        lax.all_to_all(stamps, "visit", 0, 0, axis_index_groups=lines)
    )
    flip = [(i, i ^ LINE) for i in range(visits)]
    following = [(i, ((i + LINE) ^ LINE) - LINE) for i in range(LINE, visits - LINE)]
    far = [(i, i + 2 * LINE if i % LINE < LINE // 2 else i - 2 * LINE) for i in range(visits)]
    far = [(source, target) for source, target in far if 0 <= target < visits]
    from_far = lax.ppermute(to_far, "visit", far)
    from_flip = lax.ppermute(to_flip, "visit", flip)
    from_next = lax.ppermute(to_next, "visit", following)
    difference = sheet[ROWS : 2 * ROWS] - model
    return (difference[None, None], mean(to_own, from_next, from_flip, from_far)[None])


def solution(mesh):
    in_specs = (
        P("patch", "visit", None),
        P("visit", "patch", None, None),
        P("visit", "patch", None, None),
        P("visit", "patch", None),
    )
    out_specs = (P("visit", "patch", None, None), P("patch", "visit", None))
    return jax.shard_map(shards, mesh=mesh, in_specs=in_specs, out_specs=out_specs, check_vma=False)
```

```python
import functools
import math

import jax
import jax.numpy as jnp
import ml_dtypes
import numpy as np
from jax import lax
from jax.experimental import pallas as pl
from jax.experimental.pallas import tpu as pltpu
from jax.sharding import PartitionSpec as P

KHALF = 10
SHIFT = 6
REACH = 6
NBASIS = 28
ROWS = 64
COLS = 512
PLANE = 8
LINE = 4
SPAN = 96
SENT = 88
SLOTS = 32
BLOCK = 128
BLOCKS = COLS // BLOCK
PITCH = 72
TALL = BLOCKS * ROWS
NOTED = TALL + 8
HALF = 32
CHUNK = 32
DEPTH = 64

SIGMAS = (1.0, 2.0, 4.0)
DEGREES = (4, 2, 2)
RIDGE = 0.01
LIMIT = 32 * 1024 * 1024
BESIDE = 5
BESIDE_ROWS = -(-(NBASIS - 1) // BESIDE) * HALF

VMEM = pl.BlockSpec(memory_space=pltpu.VMEM)
HBM = pl.BlockSpec(memory_space=pltpu.HBM)


def factor_table():
    listed = []
    for width_sigma, degree in zip(SIGMAS, DEGREES):
        for exponent in range(degree + 1):
            values = [
                math.exp(-(offset * offset) / (2.0 * width_sigma * width_sigma))
                * (offset / KHALF) ** exponent
                for offset in range(-KHALF, KHALF + 1)
            ]
            scale_norm = math.sqrt(sum((entry * entry for entry in values)))
            listed.append([entry / scale_norm for entry in values])
    return np.array(listed, dtype=np.float32)


def row_factors_by_column_factor():
    groups = []
    first = 0
    for degree in DEGREES:
        for power_col in range(degree + 1):
            groups.append([first + power_row for power_row in range(degree + 1 - power_col)])
        first += degree + 1
    return groups


GROUPS = row_factors_by_column_factor()
NFACTORS = len(GROUPS)


def split_constant(values):
    high = values.astype(ml_dtypes.bfloat16)
    low = (values - high.astype(np.float32)).astype(ml_dtypes.bfloat16)
    return high, low


def tables():
    table = factor_table()
    distance = np.arange(2 * BLOCK)[:, None] - np.arange(BLOCK)[None, :]
    bands = np.zeros((2 * BLOCK, NFACTORS, BLOCK), np.float32)
    for offset in range(2 * KHALF + 1):
        bands += table[None, :, offset, None] * (distance == offset)[:, None, :]
    columns = split_constant(bands.reshape(2 * BLOCK, NFACTORS * BLOCK))
    distance = np.arange(DEPTH)[None, :] - np.arange(HALF)[:, None]
    chosen = [index for group in GROUPS for index in group]
    bands = np.zeros((len(chosen), HALF, DEPTH), np.float32)
    for offset in range(2 * KHALF + 1):
        bands += table[chosen, offset][:, None, None] * (distance == offset)[None]
    high, low = split_constant(bands)
    rows = np.zeros((BESIDE_ROWS, NFACTORS * BLOCK), ml_dtypes.bfloat16)
    for plane, band in enumerate(np.concatenate([high, high, low], axis=2)):
        row, lane = row_band_place(plane)
        rows[row : row + HALF, lane : lane + 3 * DEPTH] = band
    return np.concatenate([*columns, rows])


def row_band_place(plane):
    return plane // BESIDE * HALF, plane % BESIDE * 2 * BLOCK


def split(values):
    high = values.astype(jnp.bfloat16)
    low = (values - high.astype(jnp.float32)).astype(jnp.bfloat16)
    return high, low


def put_plane(planes, slot, row, values):
    for block in range(BLOCKS):
        at = (block * SLOTS + slot) * PITCH + row
        planes[at : at + values.shape[0], :] = values[:, block * BLOCK : (block + 1) * BLOCK]


def spread_kernel(tile, copies):
    for copy in range(PLANE):
        for block in range(BLOCKS):
            copies[copy, block * ROWS : (block + 1) * ROWS, :] = tile[
                :, block * BLOCK : (block + 1) * BLOCK
            ]


def spread(tile):
    return pl.pallas_call(
        spread_kernel,
        out_shape=jax.ShapeDtypeStruct((PLANE, TALL, BLOCK), jnp.float32),
        in_specs=[VMEM],
        out_specs=VMEM,
        compiler_params=pltpu.CompilerParams(vmem_limit_bytes=LIMIT),
        name="spread",
    )(tile)


def noted_number(sheet, part):
    return sheet[2 * ROWS : 2 * ROWS + 1, :BLOCK][0, part].astype(jnp.int32)


def prepare_kernel(
    entries, science, weight, table,
    sheet, table_out,
):
    lane = lax.broadcasted_iota(jnp.int32, (8, COLS), 1)
    noted = jnp.zeros((8, COLS), jnp.float32)
    for part in range(3):
        noted = jnp.where(lane == part, entries[...][0, part].astype(jnp.float32), noted)
    sheet[2 * ROWS :, :] = noted
    values = jnp.sqrt(weight[...])
    sheet[:ROWS, :] = values
    sheet[ROWS : 2 * ROWS, :] = values * science[...]
    table_out[...] = table[...]


def prepare(entries, science, weight, table):
    return pl.pallas_call(
        prepare_kernel,
        out_shape=(
            jax.ShapeDtypeStruct((2 * ROWS + 8, COLS), jnp.float32),
            jax.ShapeDtypeStruct(table.shape, table.dtype),
        ),
        in_specs=[VMEM] * 4,
        out_specs=(VMEM,) * 2,
        compiler_params=pltpu.CompilerParams(vmem_limit_bytes=LIMIT),
        name="prepare",
    )(entries, science, weight, table)


def cut_rows(window, requests, pieces, strips):
    base = (lax.axis_index("visit") // PLANE) * PLANE
    for (asked, row_move), piece in zip(requests, pieces):
        start = (asked - base) * ROWS + row_move - KHALF
        first = lax.shift_right_arithmetic(start, 3)
        for part in range(SPAN // 8):
            strip = first + part
            inside = jnp.logical_and(strip >= 0, strip < PLANE * ROWS // 8)
            strip = jnp.clip(strip, 0, PLANE * ROWS // 8 - 1)
            tile = lax.shift_right_logical(strip, 3)
            row = pl.multiple_of(lax.bitwise_and(strip, 7) * 8, 8)
            for block in range(BLOCKS):
                rows = window[tile, pl.ds(block * ROWS + row, 8), :]
                strips[8 * part : 8 * part + 8, block * BLOCK : (block + 1) * BLOCK] = jnp.where(
                    inside, rows, 0.0
                )
        shift = lax.rem(SPAN - lax.bitwise_and(start, 7), SPAN)
        piece[...] = pltpu.roll(strips[...], shift, axis=0)[:SENT]


def serve_kernel(window, below, above, piece_down, piece_up, strips):
    requests = [(entries[...][0, 0], entries[...][0, 1]) for entries in (below, above)]
    cut_rows(window, requests, (piece_down, piece_up), strips)


def serve_own_kernel(window, sheet, piece, strips):
    cut_rows(window, [(noted_number(sheet, 0), noted_number(sheet, 1))], (piece,), strips)


def serve(kernel, name, count, *operands):
    return pl.pallas_call(
        kernel,
        out_shape=(jax.ShapeDtypeStruct((SENT, COLS), jnp.float32),) * count,
        in_specs=[VMEM] * len(operands),
        out_specs=(VMEM,) * count,
        scratch_shapes=[pltpu.VMEM((SPAN, COLS), jnp.float32)],
        compiler_params=pltpu.CompilerParams(vmem_limit_bytes=LIMIT),
        name=name,
    )(*operands)


def basis_kernel(
    piece_a, piece_b, piece_c, sheet, table,
    planes, gram_out,
    high_rows, low_rows,
):
    rows = piece_a[...] + piece_b[...] + piece_c[...]
    rows = jnp.concatenate([rows, jnp.zeros((SPAN - SENT, COLS), jnp.float32)], axis=0)
    padded = jnp.concatenate([rows, jnp.zeros((SPAN, BLOCK), jnp.float32)], axis=1)
    cutout = pltpu.roll(padded, KHALF - noted_number(sheet, 2), axis=1)
    cut_high, cut_low = split(cutout)
    col_high, col_low = table[: 2 * BLOCK, :], table[2 * BLOCK : 4 * BLOCK, :]
    for block in range(COLS // BLOCK):
        cols = slice(block * BLOCK, (block + 2) * BLOCK)
        both = jnp.concatenate([cut_high[:, cols], cut_low[:, cols]], axis=0)
        main = jnp.dot(both, col_high, preferred_element_type=jnp.float32)
        rest = jnp.dot(cut_high[:, cols], col_low, preferred_element_type=jnp.float32)
        across = main[:SPAN] + main[SPAN:] + rest
        across_high, across_low = split(across)
        for factor in range(NFACTORS):
            take = slice(factor * BLOCK, (factor + 1) * BLOCK)
            put = slice(block * BLOCK, (block + 1) * BLOCK)
            high_rows[factor, :, put] = across_high[:, take]
            low_rows[factor, :, put] = across_low[:, take]
    first = 0
    for factor, group in enumerate(GROUPS):
        bands = []
        for member in range(len(group)):
            row, lane = row_band_place(first + member)
            row += 4 * BLOCK
            bands.append(table[row : row + HALF, lane : lane + 3 * DEPTH])
        bands = jnp.concatenate(bands, axis=0)
        for half in range(ROWS // HALF):
            take = slice(half * HALF, half * HALF + DEPTH)
            high = high_rows[factor, take, :]
            stacked = jnp.concatenate([high, low_rows[factor, take, :], high], axis=0)
            out = jnp.dot(bands, stacked, preferred_element_type=jnp.float32)
            for member in range(len(group)):
                scaled = (
                    out[member * HALF : (member + 1) * HALF]
                    * sheet[half * HALF : (half + 1) * HALF, :]
                )
                put_plane(planes, first + member, half * HALF, scaled)
        first += len(group)
    put_plane(planes, NBASIS - 1, 0, sheet[:ROWS, :])
    put_plane(planes, NBASIS, 0, sheet[ROWS : 2 * ROWS, :])
    for slot in range(NBASIS + 1, SLOTS):
        put_plane(planes, slot, 0, jnp.zeros((ROWS, COLS), jnp.float32))
    def gram_step(chunk, total):
        highs, lows = [], []
        for inner in range(CHUNK):
            for block in range(BLOCKS):
                row = block * SLOTS * PITCH + chunk * CHUNK + inner
                high, low = split(planes[pl.ds(row, SLOTS, stride=PITCH), :])
                highs.append(high)
                lows.append(low)
        high = jnp.concatenate(highs, axis=1)
        low = jnp.concatenate(lows, axis=1)
        both = jnp.concatenate([high, low], axis=0)
        return total + lax.dot_general(
            high, both, (((1,), (1,)), ((), ())), preferred_element_type=jnp.float32
        )

    total = lax.fori_loop(0, ROWS // CHUNK, gram_step, jnp.zeros((SLOTS, 2 * SLOTS), jnp.float32))
    gram_out[...] = jnp.concatenate(
        [total, jnp.zeros((SLOTS, BLOCK - 2 * SLOTS), jnp.float32)], axis=1
    )


def basis(pieces, *operands):
    return pl.pallas_call(
        basis_kernel,
        out_shape=(
            jax.ShapeDtypeStruct((BLOCKS * SLOTS * PITCH, BLOCK), jnp.float32),
            jax.ShapeDtypeStruct((SLOTS, BLOCK), jnp.float32),
        ),
        in_specs=[VMEM] * 5,
        out_specs=(VMEM, VMEM),
        scratch_shapes=[
            pltpu.VMEM((NFACTORS, SPAN, COLS), jnp.bfloat16),
            pltpu.VMEM((NFACTORS, SPAN, COLS), jnp.bfloat16),
        ],
        compiler_params=pltpu.CompilerParams(vmem_limit_bytes=LIMIT),
        name="basis",
    )(*pieces, *operands)


def solve_pair(corner, heads):
    (a, b), (c, d) = corner
    inverse = 1.0 / (a * d - b * c)
    return (d * heads[0] - b * heads[1]) * inverse, (a * heads[1] - c * heads[0]) * inverse


def solve_corner(corner, heads):
    first = [row[:2] for row in corner[:2]]
    right = [solve_pair(first, [corner[0][col], corner[1][col]]) for col in (2, 3)]
    upper = solve_pair(first, heads[:2])
    rest = [
        [
            corner[row][col] - corner[row][0] * right[col - 2][0] - corner[row][1] * right[col - 2][1]
            for col in (2, 3)
        ]
        for row in (2, 3)
    ]
    lower = solve_pair(
        rest,
        [heads[row] - corner[row][0] * upper[0] - corner[row][1] * upper[1] for row in (2, 3)],
    )
    return (
        *(upper[row] - right[0][row] * lower[0] - right[1][row] * lower[1] for row in range(2)),
        *lower,
    )


def solve_kernel(grams, planes, sheet, model_out, stamps):
    total = grams[0] + grams[1] + grams[2] + grams[3]
    cross = total[:, SLOTS : 2 * SLOTS]
    normal = total[:, :SLOTS] + cross + cross.T
    row_id = lax.broadcasted_iota(jnp.int32, (SLOTS, SLOTS), 0)
    col_id = lax.broadcasted_iota(jnp.int32, (SLOTS, SLOTS), 1)
    diagonal = jnp.logical_and(row_id == col_id, row_id < NBASIS)
    trace = jnp.sum(jnp.where(diagonal, normal, 0.0), keepdims=True)
    matrix = normal + jnp.where(diagonal, RIDGE * trace / NBASIS, 0.0)
    for step in range(0, NBASIS, 4):
        columns = [
            jnp.broadcast_to(matrix[:, step + part : step + part + 1], (SLOTS, SLOTS))
            for part in range(4)
        ]
        heads = [matrix[step + part : step + part + 1] for part in range(4)]
        corner = [[columns[col][step + row : step + row + 1] for col in range(4)] for row in range(4)]
        solved = solve_corner(corner, heads)
        others = matrix
        for part in range(4):
            others = others - columns[part] * solved[part]
        matrix = others
        for part in range(4):
            matrix = jnp.where(row_id == step + part, solved[part], matrix)
    answer = jnp.broadcast_to(matrix[:, NBASIS : NBASIS + 1], (SLOTS, BLOCK))
    for block in range(BLOCKS):
        model = jnp.zeros((ROWS, BLOCK), jnp.float32)
        for plane in range(NBASIS):
            factor = jnp.broadcast_to(answer[plane : plane + 1, :], (ROWS, BLOCK))
            at = (block * SLOTS + plane) * PITCH
            model = model + factor * planes[at : at + ROWS, :]
        model_out[:, block * BLOCK : (block + 1) * BLOCK] = model
    difference = sheet[ROWS : 2 * ROWS, :] - model_out[...]
    tile, row_move, col_move = (noted_number(sheet, part) for part in range(3))
    moved = pltpu.roll(difference, lax.rem(row_move + ROWS, ROWS), axis=0)
    moved = pltpu.roll(moved, lax.rem(col_move + COLS, COLS), axis=1)
    from_row = lax.broadcasted_iota(jnp.int32, (ROWS, COLS), 0) - row_move
    from_col = lax.broadcasted_iota(jnp.int32, (ROWS, COLS), 1) - col_move
    inside = (from_row >= 0) & (from_row < ROWS) & (from_col >= 0) & (from_col < COLS)
    placed = jnp.where(inside, moved, 0.0)
    for place in range(LINE):
        mine = lax.bitwise_and(tile, LINE - 1) == place
        for block in range(BLOCKS):
            stamps[place, block * ROWS : (block + 1) * ROWS, :] = jnp.where(
                mine, placed[:, block * BLOCK : (block + 1) * BLOCK], 0.0
            )
        stamps[place, TALL:, :] = jnp.full(
            (NOTED - TALL, BLOCK), tile.astype(jnp.float32), jnp.float32
        )


def solve(grams, planes, sheet):
    return pl.pallas_call(
        solve_kernel,
        out_shape=(
            jax.ShapeDtypeStruct((ROWS, COLS), jnp.float32),
            jax.ShapeDtypeStruct((LINE, NOTED, BLOCK), jnp.float32),
        ),
        in_specs=[VMEM, VMEM, VMEM],
        out_specs=(VMEM, VMEM),
        compiler_params=pltpu.CompilerParams(vmem_limit_bytes=LIMIT),
        name="solve",
    )(grams, planes, sheet)


def gather_kernel(stamps, to_own, to_flip, to_next, to_far):
    visit = lax.axis_index("visit")
    even = lax.rem(visit // LINE, 2) == 0
    low = lax.rem(visit, LINE) < LINE // 2
    targets = (
        visit,
        jnp.where(even, visit + LINE, visit - LINE),
        jnp.where(even, visit - LINE, visit + LINE),
        jnp.where(low, visit + 2 * LINE, visit - 2 * LINE),
    )
    for target, out in zip(targets, (to_own, to_flip, to_next, to_far)):
        number = target.astype(jnp.float32)
        hits = [stamps[place, TALL:, :] == number for place in range(LINE)]
        count = jnp.zeros((NOTED - TALL, BLOCK), jnp.float32)
        for hit in hits:
            count = count + jnp.where(hit, 1.0, 0.0)
        out[TALL:, :] = count
        for block in range(BLOCKS):
            rows = slice(block * ROWS, (block + 1) * ROWS)
            total = jnp.zeros((ROWS, BLOCK), jnp.float32)
            for place in range(LINE):
                total = total + jnp.where(hits[place][:1], stamps[place, rows, :], 0.0)
            out[rows, :] = total


def gather(stamps):
    shape = jax.ShapeDtypeStruct((NOTED, BLOCK), jnp.float32)
    return pl.pallas_call(
        gather_kernel,
        out_shape=(shape,) * 4,
        in_specs=[VMEM],
        out_specs=(VMEM,) * 4,
        compiler_params=pltpu.CompilerParams(vmem_limit_bytes=LIMIT),
        name="gather",
    )(stamps)


def mean_kernel(part_a, part_b, part_c, part_d, coadd):
    parts = (part_a, part_b, part_c, part_d)
    count = sum(part[TALL:, :] for part in parts)
    count = jnp.maximum(count[:1], 1.0)
    for block in range(BLOCKS):
        rows = slice(block * ROWS, (block + 1) * ROWS)
        total = sum(part[rows, :] for part in parts)
        coadd[:, block * BLOCK : (block + 1) * BLOCK] = total / count


def mean(*parts):
    return pl.pallas_call(
        mean_kernel,
        out_shape=jax.ShapeDtypeStruct((ROWS, COLS), jnp.float32),
        in_specs=[VMEM] * 4,
        out_specs=VMEM,
        compiler_params=pltpu.CompilerParams(vmem_limit_bytes=LIMIT),
        name="mean",
    )(*parts)


def shards(template, science, inverse_variance, intersections):
    visits = lax.axis_size("visit")
    groups = [list(range(first, first + PLANE)) for first in range(0, visits, PLANE)]
    upward = [(i, i + PLANE) for i in range(visits - PLANE)]
    downward = [(target, source) for source, target in upward]
    own = intersections[0]
    below = lax.ppermute(own, "visit", upward)
    above = lax.ppermute(own, "visit", downward)
    sheet, table = prepare(
        own, science[0, 0], inverse_variance[0, 0], jnp.asarray(tables())
    )
    window = lax.all_to_all(spread(template[0]), "visit", 0, 0, axis_index_groups=groups)
    piece_down, piece_up = serve(serve_kernel, "serve", 2, window, below, above)
    (piece_own,) = serve(serve_own_kernel, "serve_own", 1, window, sheet)
    from_above = lax.ppermute(piece_down, "visit", downward)
    from_below = lax.ppermute(piece_up, "visit", upward)
    planes, gram = basis((piece_own, from_above, from_below), sheet, table)
    grams = lax.all_gather(gram, "patch")
    model, stamps = solve(grams, planes, sheet)
    lines = [list(range(first, first + LINE)) for first in range(0, visits, LINE)]
    to_own, to_flip, to_next, to_far = gather(
        lax.all_to_all(stamps, "visit", 0, 0, axis_index_groups=lines)
    )
    flip = [(i, i ^ LINE) for i in range(visits)]
    following = [(i, ((i + LINE) ^ LINE) - LINE) for i in range(LINE, visits - LINE)]
    far = [(i, i + 2 * LINE if i % LINE < LINE // 2 else i - 2 * LINE) for i in range(visits)]
    far = [(source, target) for source, target in far if 0 <= target < visits]
    from_far = lax.ppermute(to_far, "visit", far)
    from_flip = lax.ppermute(to_flip, "visit", flip)
    from_next = lax.ppermute(to_next, "visit", following)
    difference = sheet[ROWS : 2 * ROWS] - model
    return (difference[None, None], mean(to_own, from_next, from_flip, from_far)[None])


def solution(mesh):
    in_specs = (
        P("patch", "visit", None),
        P("visit", "patch", None, None),
        P("visit", "patch", None, None),
        P("visit", "patch", None),
    )
    out_specs = (P("visit", "patch", None, None), P("patch", "visit", None))
    return jax.shard_map(shards, mesh=mesh, in_specs=in_specs, out_specs=out_specs, check_vma=False)
```

```python
import functools
import math

import jax
import jax.numpy as jnp
import ml_dtypes
import numpy as np
from jax import lax
from jax.experimental import pallas as pl
from jax.experimental.pallas import tpu as pltpu
from jax.sharding import PartitionSpec as P

KHALF = 10
SHIFT = 6
REACH = 6
NBASIS = 28
ROWS = 64
COLS = 512
PLANE = 8
LINE = 4
SPAN = 96
SENT = 88
SLOTS = 32
BLOCK = 128
BLOCKS = COLS // BLOCK
PITCH = 72
TALL = BLOCKS * ROWS
NOTED = TALL + 8
HALF = 32
CHUNK = 32
DEPTH = 64

SIGMAS = (1.0, 2.0, 4.0)
DEGREES = (4, 2, 2)
RIDGE = 0.01
LIMIT = 32 * 1024 * 1024
BESIDE = 5
BESIDE_ROWS = -(-(NBASIS - 1) // BESIDE) * HALF

VMEM = pl.BlockSpec(memory_space=pltpu.VMEM)
HBM = pl.BlockSpec(memory_space=pltpu.HBM)


def factor_table():
    listed = []
    for width_sigma, degree in zip(SIGMAS, DEGREES):
        for exponent in range(degree + 1):
            values = [
                math.exp(-(offset * offset) / (2.0 * width_sigma * width_sigma))
                * (offset / KHALF) ** exponent
                for offset in range(-KHALF, KHALF + 1)
            ]
            scale_norm = math.sqrt(sum((entry * entry for entry in values)))
            listed.append([entry / scale_norm for entry in values])
    return np.array(listed, dtype=np.float32)


def row_factors_by_column_factor():
    groups = []
    first = 0
    for degree in DEGREES:
        for power_col in range(degree + 1):
            groups.append([first + power_row for power_row in range(degree + 1 - power_col)])
        first += degree + 1
    return groups


GROUPS = row_factors_by_column_factor()
NFACTORS = len(GROUPS)


def split_constant(values):
    high = values.astype(ml_dtypes.bfloat16)
    low = (values - high.astype(np.float32)).astype(ml_dtypes.bfloat16)
    return high, low


def tables():
    table = factor_table()
    distance = np.arange(2 * BLOCK)[:, None] - np.arange(BLOCK)[None, :]
    bands = np.zeros((2 * BLOCK, NFACTORS, BLOCK), np.float32)
    for offset in range(2 * KHALF + 1):
        bands += table[None, :, offset, None] * (distance == offset)[:, None, :]
    columns = split_constant(bands.reshape(2 * BLOCK, NFACTORS * BLOCK))
    distance = np.arange(DEPTH)[None, :] - np.arange(HALF)[:, None]
    chosen = [index for group in GROUPS for index in group]
    bands = np.zeros((len(chosen), HALF, DEPTH), np.float32)
    for offset in range(2 * KHALF + 1):
        bands += table[chosen, offset][:, None, None] * (distance == offset)[None]
    high, low = split_constant(bands)
    rows = np.zeros((BESIDE_ROWS, NFACTORS * BLOCK), ml_dtypes.bfloat16)
    for plane, band in enumerate(np.concatenate([high, high, low], axis=2)):
        row, lane = row_band_place(plane)
        rows[row : row + HALF, lane : lane + 3 * DEPTH] = band
    return np.concatenate([*columns, rows])


def row_band_place(plane):
    return plane // BESIDE * HALF, plane % BESIDE * 2 * BLOCK


def split(values):
    high = values.astype(jnp.bfloat16)
    low = (values - high.astype(jnp.float32)).astype(jnp.bfloat16)
    return high, low


def put_plane(planes, slot, row, values):
    for block in range(BLOCKS):
        at = (block * SLOTS + slot) * PITCH + row
        planes[at : at + values.shape[0], :] = values[:, block * BLOCK : (block + 1) * BLOCK]


def spread_kernel(tile, copies):
    for copy in range(PLANE):
        for block in range(BLOCKS):
            copies[copy, block * ROWS : (block + 1) * ROWS, :] = tile[
                :, block * BLOCK : (block + 1) * BLOCK
            ]


def spread(tile):
    return pl.pallas_call(
        spread_kernel,
        out_shape=jax.ShapeDtypeStruct((PLANE, TALL, BLOCK), jnp.float32),
        in_specs=[VMEM],
        out_specs=VMEM,
        compiler_params=pltpu.CompilerParams(vmem_limit_bytes=LIMIT),
        name="spread",
    )(tile)


def noted_number(sheet, part):
    return sheet[2 * ROWS : 2 * ROWS + 1, :BLOCK][0, part].astype(jnp.int32)


def prepare_kernel(
    entries, science, weight, table,
    sheet, table_out,
):
    lane = lax.broadcasted_iota(jnp.int32, (8, COLS), 1)
    noted = jnp.zeros((8, COLS), jnp.float32)
    for part in range(3):
        noted = jnp.where(lane == part, entries[...][0, part].astype(jnp.float32), noted)
    sheet[2 * ROWS :, :] = noted
    values = jnp.sqrt(weight[...])
    sheet[:ROWS, :] = values
    sheet[ROWS : 2 * ROWS, :] = values * science[...]
    table_out[...] = table[...]


def prepare(entries, science, weight, table):
    return pl.pallas_call(
        prepare_kernel,
        out_shape=(
            jax.ShapeDtypeStruct((2 * ROWS + 8, COLS), jnp.float32),
            jax.ShapeDtypeStruct(table.shape, table.dtype),
        ),
        in_specs=[VMEM] * 4,
        out_specs=(VMEM,) * 2,
        compiler_params=pltpu.CompilerParams(vmem_limit_bytes=LIMIT),
        name="prepare",
    )(entries, science, weight, table)


def cut_rows(window, requests, pieces, strips):
    base = (lax.axis_index("visit") // PLANE) * PLANE
    for (asked, row_move), piece in zip(requests, pieces):
        start = (asked - base) * ROWS + row_move - KHALF
        first = lax.shift_right_arithmetic(start, 3)
        for part in range(SPAN // 8):
            strip = first + part
            inside = jnp.logical_and(strip >= 0, strip < PLANE * ROWS // 8)
            strip = jnp.clip(strip, 0, PLANE * ROWS // 8 - 1)
            tile = lax.shift_right_logical(strip, 3)
            row = pl.multiple_of(lax.bitwise_and(strip, 7) * 8, 8)
            for block in range(BLOCKS):
                rows = window[tile, pl.ds(block * ROWS + row, 8), :]
                strips[8 * part : 8 * part + 8, block * BLOCK : (block + 1) * BLOCK] = jnp.where(
                    inside, rows, 0.0
                )
        shift = lax.rem(SPAN - lax.bitwise_and(start, 7), SPAN)
        piece[...] = pltpu.roll(strips[...], shift, axis=0)[:SENT]


def serve_kernel(window, sheet, below, above, piece_down, piece_up, strips):
    requests = [(entries[...][0, 0], entries[...][0, 1]) for entries in (below, above)]
    cut_rows(window, requests, (piece_down, piece_up), strips)


def serve_own_kernel(window, sheet, piece, strips):
    cut_rows(window, [(noted_number(sheet, 0), noted_number(sheet, 1))], (piece,), strips)


def serve(kernel, name, count, *operands):
    return pl.pallas_call(
        kernel,
        out_shape=(jax.ShapeDtypeStruct((SENT, COLS), jnp.float32),) * count,
        in_specs=[VMEM] * len(operands),
        out_specs=(VMEM,) * count,
        scratch_shapes=[pltpu.VMEM((SPAN, COLS), jnp.float32)],
        compiler_params=pltpu.CompilerParams(vmem_limit_bytes=LIMIT),
        name=name,
    )(*operands)


def basis_kernel(
    piece_a, piece_b, piece_c, sheet, table,
    planes, gram_out,
    high_rows, low_rows,
):
    rows = piece_a[...] + piece_b[...] + piece_c[...]
    rows = jnp.concatenate([rows, jnp.zeros((SPAN - SENT, COLS), jnp.float32)], axis=0)
    padded = jnp.concatenate([rows, jnp.zeros((SPAN, BLOCK), jnp.float32)], axis=1)
    cutout = pltpu.roll(padded, KHALF - noted_number(sheet, 2), axis=1)
    cut_high, cut_low = split(cutout)
    col_high, col_low = table[: 2 * BLOCK, :], table[2 * BLOCK : 4 * BLOCK, :]
    for block in range(COLS // BLOCK):
        cols = slice(block * BLOCK, (block + 2) * BLOCK)
        both = jnp.concatenate([cut_high[:, cols], cut_low[:, cols]], axis=0)
        main = jnp.dot(both, col_high, preferred_element_type=jnp.float32)
        rest = jnp.dot(cut_high[:, cols], col_low, preferred_element_type=jnp.float32)
        across = main[:SPAN] + main[SPAN:] + rest
        across_high, across_low = split(across)
        for factor in range(NFACTORS):
            take = slice(factor * BLOCK, (factor + 1) * BLOCK)
            put = slice(block * BLOCK, (block + 1) * BLOCK)
            high_rows[factor, :, put] = across_high[:, take]
            low_rows[factor, :, put] = across_low[:, take]
    first = 0
    for factor, group in enumerate(GROUPS):
        bands = []
        for member in range(len(group)):
            row, lane = row_band_place(first + member)
            row += 4 * BLOCK
            bands.append(table[row : row + HALF, lane : lane + 3 * DEPTH])
        bands = jnp.concatenate(bands, axis=0)
        for half in range(ROWS // HALF):
            take = slice(half * HALF, half * HALF + DEPTH)
            high = high_rows[factor, take, :]
            stacked = jnp.concatenate([high, low_rows[factor, take, :], high], axis=0)
            out = jnp.dot(bands, stacked, preferred_element_type=jnp.float32)
            for member in range(len(group)):
                scaled = (
                    out[member * HALF : (member + 1) * HALF]
                    * sheet[half * HALF : (half + 1) * HALF, :]
                )
                put_plane(planes, first + member, half * HALF, scaled)
        first += len(group)
    put_plane(planes, NBASIS - 1, 0, sheet[:ROWS, :])
    put_plane(planes, NBASIS, 0, sheet[ROWS : 2 * ROWS, :])
    for slot in range(NBASIS + 1, SLOTS):
        put_plane(planes, slot, 0, jnp.zeros((ROWS, COLS), jnp.float32))
    def gram_step(chunk, total):
        highs, lows = [], []
        for inner in range(CHUNK):
            for block in range(BLOCKS):
                row = block * SLOTS * PITCH + chunk * CHUNK + inner
                high, low = split(planes[pl.ds(row, SLOTS, stride=PITCH), :])
                highs.append(high)
                lows.append(low)
        high = jnp.concatenate(highs, axis=1)
        low = jnp.concatenate(lows, axis=1)
        both = jnp.concatenate([high, low], axis=0)
        return total + lax.dot_general(
            high, both, (((1,), (1,)), ((), ())), preferred_element_type=jnp.float32
        )

    total = lax.fori_loop(0, ROWS // CHUNK, gram_step, jnp.zeros((SLOTS, 2 * SLOTS), jnp.float32))
    gram_out[...] = jnp.concatenate(
        [total, jnp.zeros((SLOTS, BLOCK - 2 * SLOTS), jnp.float32)], axis=1
    )


def basis(pieces, *operands):
    return pl.pallas_call(
        basis_kernel,
        out_shape=(
            jax.ShapeDtypeStruct((BLOCKS * SLOTS * PITCH, BLOCK), jnp.float32),
            jax.ShapeDtypeStruct((SLOTS, BLOCK), jnp.float32),
        ),
        in_specs=[VMEM] * 5,
        out_specs=(VMEM, VMEM),
        scratch_shapes=[
            pltpu.VMEM((NFACTORS, SPAN, COLS), jnp.bfloat16),
            pltpu.VMEM((NFACTORS, SPAN, COLS), jnp.bfloat16),
        ],
        compiler_params=pltpu.CompilerParams(vmem_limit_bytes=LIMIT),
        name="basis",
    )(*pieces, *operands)


def solve_pair(corner, heads):
    (a, b), (c, d) = corner
    inverse = 1.0 / (a * d - b * c)
    return (d * heads[0] - b * heads[1]) * inverse, (a * heads[1] - c * heads[0]) * inverse


def solve_corner(corner, heads):
    first = [row[:2] for row in corner[:2]]
    right = [solve_pair(first, [corner[0][col], corner[1][col]]) for col in (2, 3)]
    upper = solve_pair(first, heads[:2])
    rest = [
        [
            corner[row][col] - corner[row][0] * right[col - 2][0] - corner[row][1] * right[col - 2][1]
            for col in (2, 3)
        ]
        for row in (2, 3)
    ]
    lower = solve_pair(
        rest,
        [heads[row] - corner[row][0] * upper[0] - corner[row][1] * upper[1] for row in (2, 3)],
    )
    return (
        *(upper[row] - right[0][row] * lower[0] - right[1][row] * lower[1] for row in range(2)),
        *lower,
    )


def solve_kernel(grams, planes, sheet, model_out, stamps):
    total = grams[0] + grams[1] + grams[2] + grams[3]
    cross = total[:, SLOTS : 2 * SLOTS]
    normal = total[:, :SLOTS] + cross + cross.T
    row_id = lax.broadcasted_iota(jnp.int32, (SLOTS, SLOTS), 0)
    col_id = lax.broadcasted_iota(jnp.int32, (SLOTS, SLOTS), 1)
    diagonal = jnp.logical_and(row_id == col_id, row_id < NBASIS)
    trace = jnp.sum(jnp.where(diagonal, normal, 0.0), keepdims=True)
    matrix = normal + jnp.where(diagonal, RIDGE * trace / NBASIS, 0.0)
    for step in range(0, NBASIS, 4):
        columns = [
            jnp.broadcast_to(matrix[:, step + part : step + part + 1], (SLOTS, SLOTS))
            for part in range(4)
        ]
        heads = [matrix[step + part : step + part + 1] for part in range(4)]
        corner = [[columns[col][step + row : step + row + 1] for col in range(4)] for row in range(4)]
        solved = solve_corner(corner, heads)
        others = matrix
        for part in range(4):
            others = others - columns[part] * solved[part]
        matrix = others
        for part in range(4):
            matrix = jnp.where(row_id == step + part, solved[part], matrix)
    answer = jnp.broadcast_to(matrix[:, NBASIS : NBASIS + 1], (SLOTS, BLOCK))
    for block in range(BLOCKS):
        model = jnp.zeros((ROWS, BLOCK), jnp.float32)
        for plane in range(NBASIS):
            factor = jnp.broadcast_to(answer[plane : plane + 1, :], (ROWS, BLOCK))
            at = (block * SLOTS + plane) * PITCH
            model = model + factor * planes[at : at + ROWS, :]
        model_out[:, block * BLOCK : (block + 1) * BLOCK] = model
    difference = sheet[ROWS : 2 * ROWS, :] - model_out[...]
    tile, row_move, col_move = (noted_number(sheet, part) for part in range(3))
    moved = pltpu.roll(difference, lax.rem(row_move + ROWS, ROWS), axis=0)
    moved = pltpu.roll(moved, lax.rem(col_move + COLS, COLS), axis=1)
    from_row = lax.broadcasted_iota(jnp.int32, (ROWS, COLS), 0) - row_move
    from_col = lax.broadcasted_iota(jnp.int32, (ROWS, COLS), 1) - col_move
    inside = (from_row >= 0) & (from_row < ROWS) & (from_col >= 0) & (from_col < COLS)
    placed = jnp.where(inside, moved, 0.0)
    for place in range(LINE):
        mine = lax.bitwise_and(tile, LINE - 1) == place
        for block in range(BLOCKS):
            stamps[place, block * ROWS : (block + 1) * ROWS, :] = jnp.where(
                mine, placed[:, block * BLOCK : (block + 1) * BLOCK], 0.0
            )
        stamps[place, TALL:, :] = jnp.full(
            (NOTED - TALL, BLOCK), tile.astype(jnp.float32), jnp.float32
        )


def solve(grams, planes, sheet):
    return pl.pallas_call(
        solve_kernel,
        out_shape=(
            jax.ShapeDtypeStruct((ROWS, COLS), jnp.float32),
            jax.ShapeDtypeStruct((LINE, NOTED, BLOCK), jnp.float32),
        ),
        in_specs=[VMEM, VMEM, VMEM],
        out_specs=(VMEM, VMEM),
        compiler_params=pltpu.CompilerParams(vmem_limit_bytes=LIMIT),
        name="solve",
    )(grams, planes, sheet)


def gather_kernel(stamps, to_own, to_flip, to_next, to_far):
    visit = lax.axis_index("visit")
    even = lax.rem(visit // LINE, 2) == 0
    low = lax.rem(visit, LINE) < LINE // 2
    targets = (
        visit,
        jnp.where(even, visit + LINE, visit - LINE),
        jnp.where(even, visit - LINE, visit + LINE),
        jnp.where(low, visit + 2 * LINE, visit - 2 * LINE),
    )
    for target, out in zip(targets, (to_own, to_flip, to_next, to_far)):
        number = target.astype(jnp.float32)
        hits = [stamps[place, TALL:, :] == number for place in range(LINE)]
        count = jnp.zeros((NOTED - TALL, BLOCK), jnp.float32)
        for hit in hits:
            count = count + jnp.where(hit, 1.0, 0.0)
        out[TALL:, :] = count
        for block in range(BLOCKS):
            rows = slice(block * ROWS, (block + 1) * ROWS)
            total = jnp.zeros((ROWS, BLOCK), jnp.float32)
            for place in range(LINE):
                total = total + jnp.where(hits[place][:1], stamps[place, rows, :], 0.0)
            out[rows, :] = total


def gather(stamps):
    shape = jax.ShapeDtypeStruct((NOTED, BLOCK), jnp.float32)
    return pl.pallas_call(
        gather_kernel,
        out_shape=(shape,) * 4,
        in_specs=[VMEM],
        out_specs=(VMEM,) * 4,
        compiler_params=pltpu.CompilerParams(vmem_limit_bytes=LIMIT),
        name="gather",
    )(stamps)


def mean_kernel(part_a, part_b, part_c, part_d, coadd):
    parts = (part_a, part_b, part_c, part_d)
    count = sum(part[TALL:, :] for part in parts)
    count = jnp.maximum(count[:1], 1.0)
    for block in range(BLOCKS):
        rows = slice(block * ROWS, (block + 1) * ROWS)
        total = sum(part[rows, :] for part in parts)
        coadd[:, block * BLOCK : (block + 1) * BLOCK] = total / count


def mean(*parts):
    return pl.pallas_call(
        mean_kernel,
        out_shape=jax.ShapeDtypeStruct((ROWS, COLS), jnp.float32),
        in_specs=[VMEM] * 4,
        out_specs=VMEM,
        compiler_params=pltpu.CompilerParams(vmem_limit_bytes=LIMIT),
        name="mean",
    )(*parts)


def shards(template, science, inverse_variance, intersections):
    visits = lax.axis_size("visit")
    groups = [list(range(first, first + PLANE)) for first in range(0, visits, PLANE)]
    upward = [(i, i + PLANE) for i in range(visits - PLANE)]
    downward = [(target, source) for source, target in upward]
    own = intersections[0]
    below = lax.ppermute(own, "visit", upward)
    above = lax.ppermute(own, "visit", downward)
    sheet, table = prepare(
        own, science[0, 0], inverse_variance[0, 0], jnp.asarray(tables())
    )
    window = lax.all_to_all(spread(template[0]), "visit", 0, 0, axis_index_groups=groups)
    piece_down, piece_up = serve(serve_kernel, "serve", 2, window, sheet, below, above)
    (piece_own,) = serve(serve_own_kernel, "serve_own", 1, window, sheet)
    from_above = lax.ppermute(piece_down, "visit", downward)
    from_below = lax.ppermute(piece_up, "visit", upward)
    planes, gram = basis((piece_own, from_above, from_below), sheet, table)
    grams = lax.all_gather(gram, "patch")
    model, stamps = solve(grams, planes, sheet)
    lines = [list(range(first, first + LINE)) for first in range(0, visits, LINE)]
    to_own, to_flip, to_next, to_far = gather(
        lax.all_to_all(stamps, "visit", 0, 0, axis_index_groups=lines)
    )
    flip = [(i, i ^ LINE) for i in range(visits)]
    following = [(i, ((i + LINE) ^ LINE) - LINE) for i in range(LINE, visits - LINE)]
    far = [(i, i + 2 * LINE if i % LINE < LINE // 2 else i - 2 * LINE) for i in range(visits)]
    far = [(source, target) for source, target in far if 0 <= target < visits]
    from_far = lax.ppermute(to_far, "visit", far)
    from_flip = lax.ppermute(to_flip, "visit", flip)
    from_next = lax.ppermute(to_next, "visit", following)
    difference = sheet[ROWS : 2 * ROWS] - model
    return (difference[None, None], mean(to_own, from_next, from_flip, from_far)[None])


def solution(mesh):
    in_specs = (
        P("patch", "visit", None),
        P("visit", "patch", None, None),
        P("visit", "patch", None, None),
        P("visit", "patch", None),
    )
    out_specs = (P("visit", "patch", None, None), P("patch", "visit", None))
    return jax.shard_map(shards, mesh=mesh, in_specs=in_specs, out_specs=out_specs, check_vma=False)
```

```python
import functools
import math

import jax
import jax.numpy as jnp
import ml_dtypes
import numpy as np
from jax import lax
from jax.experimental import pallas as pl
from jax.experimental.pallas import tpu as pltpu
from jax.sharding import PartitionSpec as P

KHALF = 10
SHIFT = 6
REACH = 6
NBASIS = 28
ROWS = 64
COLS = 512
PLANE = 8
LINE = 4
SPAN = 96
SENT = 88
SLOTS = 32
BLOCK = 128
BLOCKS = COLS // BLOCK
PITCH = 72
TALL = BLOCKS * ROWS
NOTED = TALL + 8
HALF = 32
CHUNK = 32
DEPTH = 64

SIGMAS = (1.0, 2.0, 4.0)
DEGREES = (4, 2, 2)
RIDGE = 0.01
LIMIT = 32 * 1024 * 1024
BESIDE = 5
BESIDE_ROWS = -(-(NBASIS - 1) // BESIDE) * HALF

VMEM = pl.BlockSpec(memory_space=pltpu.VMEM)
HBM = pl.BlockSpec(memory_space=pltpu.HBM)


def factor_table():
    listed = []
    for width_sigma, degree in zip(SIGMAS, DEGREES):
        for exponent in range(degree + 1):
            values = [
                math.exp(-(offset * offset) / (2.0 * width_sigma * width_sigma))
                * (offset / KHALF) ** exponent
                for offset in range(-KHALF, KHALF + 1)
            ]
            scale_norm = math.sqrt(sum((entry * entry for entry in values)))
            listed.append([entry / scale_norm for entry in values])
    return np.array(listed, dtype=np.float32)


def row_factors_by_column_factor():
    groups = []
    first = 0
    for degree in DEGREES:
        for power_col in range(degree + 1):
            groups.append([first + power_row for power_row in range(degree + 1 - power_col)])
        first += degree + 1
    return groups


GROUPS = row_factors_by_column_factor()
NFACTORS = len(GROUPS)


def split_constant(values):
    high = values.astype(ml_dtypes.bfloat16)
    low = (values - high.astype(np.float32)).astype(ml_dtypes.bfloat16)
    return high, low


def tables():
    table = factor_table()
    distance = np.arange(2 * BLOCK)[:, None] - np.arange(BLOCK)[None, :]
    bands = np.zeros((2 * BLOCK, NFACTORS, BLOCK), np.float32)
    for offset in range(2 * KHALF + 1):
        bands += table[None, :, offset, None] * (distance == offset)[:, None, :]
    columns = split_constant(bands.reshape(2 * BLOCK, NFACTORS * BLOCK))
    distance = np.arange(DEPTH)[None, :] - np.arange(HALF)[:, None]
    chosen = [index for group in GROUPS for index in group]
    bands = np.zeros((len(chosen), HALF, DEPTH), np.float32)
    for offset in range(2 * KHALF + 1):
        bands += table[chosen, offset][:, None, None] * (distance == offset)[None]
    high, low = split_constant(bands)
    rows = np.zeros((BESIDE_ROWS, NFACTORS * BLOCK), ml_dtypes.bfloat16)
    for plane, band in enumerate(np.concatenate([high, high, low], axis=2)):
        row, lane = row_band_place(plane)
        rows[row : row + HALF, lane : lane + 3 * DEPTH] = band
    return np.concatenate([*columns, rows])


def row_band_place(plane):
    return plane // BESIDE * HALF, plane % BESIDE * 2 * BLOCK


def split(values):
    high = values.astype(jnp.bfloat16)
    low = (values - high.astype(jnp.float32)).astype(jnp.bfloat16)
    return high, low


def put_plane(planes, slot, row, values):
    for block in range(BLOCKS):
        at = (block * SLOTS + slot) * PITCH + row
        planes[at : at + values.shape[0], :] = values[:, block * BLOCK : (block + 1) * BLOCK]


def spread_kernel(tile, copies):
    for copy in range(PLANE):
        for block in range(BLOCKS):
            copies[copy, block * ROWS : (block + 1) * ROWS, :] = tile[
                :, block * BLOCK : (block + 1) * BLOCK
            ]


def spread(tile):
    return pl.pallas_call(
        spread_kernel,
        out_shape=jax.ShapeDtypeStruct((PLANE, TALL, BLOCK), jnp.float32),
        in_specs=[VMEM],
        out_specs=VMEM,
        compiler_params=pltpu.CompilerParams(vmem_limit_bytes=LIMIT),
        name="spread",
    )(tile)


def noted_number(sheet, part):
    return sheet[2 * ROWS : 2 * ROWS + 1, :BLOCK][0, part].astype(jnp.int32)


def prepare_kernel(
    entries, science, weight, table,
    sheet, table_out,
):
    lane = lax.broadcasted_iota(jnp.int32, (8, COLS), 1)
    noted = jnp.zeros((8, COLS), jnp.float32)
    for part in range(3):
        noted = jnp.where(lane == part, entries[...][0, part].astype(jnp.float32), noted)
    sheet[2 * ROWS :, :] = noted
    values = jnp.sqrt(weight[...])
    sheet[:ROWS, :] = values
    sheet[ROWS : 2 * ROWS, :] = values * science[...]
    table_out[...] = table[...]


def prepare(entries, science, weight, table):
    return pl.pallas_call(
        prepare_kernel,
        out_shape=(
            jax.ShapeDtypeStruct((2 * ROWS + 8, COLS), jnp.float32),
            jax.ShapeDtypeStruct(table.shape, table.dtype),
        ),
        in_specs=[VMEM] * 4,
        out_specs=(VMEM,) * 2,
        compiler_params=pltpu.CompilerParams(vmem_limit_bytes=LIMIT),
        name="prepare",
    )(entries, science, weight, table)


def serve_kernel(window, sheet, below, above, piece_own, piece_up, piece_down, strips):
    base = (lax.axis_index("visit") // PLANE) * PLANE
    own = (noted_number(sheet, 0), noted_number(sheet, 1))
    others = [(entries[...][0, 0], entries[...][0, 1]) for entries in (below, above)]
    for (asked, row_move), piece in zip((own, *others), (piece_own, piece_down, piece_up)):
        start = (asked - base) * ROWS + row_move - KHALF
        first = lax.shift_right_arithmetic(start, 3)
        for part in range(SPAN // 8):
            strip = first + part
            inside = jnp.logical_and(strip >= 0, strip < PLANE * ROWS // 8)
            strip = jnp.clip(strip, 0, PLANE * ROWS // 8 - 1)
            tile = lax.shift_right_logical(strip, 3)
            row = pl.multiple_of(lax.bitwise_and(strip, 7) * 8, 8)
            for block in range(BLOCKS):
                rows = window[tile, pl.ds(block * ROWS + row, 8), :]
                strips[8 * part : 8 * part + 8, block * BLOCK : (block + 1) * BLOCK] = jnp.where(
                    inside, rows, 0.0
                )
        shift = lax.rem(SPAN - lax.bitwise_and(start, 7), SPAN)
        piece[...] = pltpu.roll(strips[...], shift, axis=0)[:SENT]


def serve(window, sheet, below, above):
    shape = jax.ShapeDtypeStruct((SENT, COLS), jnp.float32)
    return pl.pallas_call(
        serve_kernel,
        out_shape=(shape, shape, shape),
        in_specs=[VMEM] * 4,
        out_specs=(VMEM, VMEM, VMEM),
        scratch_shapes=[pltpu.VMEM((SPAN, COLS), jnp.float32)],
        compiler_params=pltpu.CompilerParams(vmem_limit_bytes=LIMIT),
        name="serve",
    )(window, sheet, below, above)


def basis_kernel(
    piece_a, piece_b, piece_c, sheet, table,
    planes, gram_out,
    high_rows, low_rows,
):
    rows = piece_a[...] + piece_b[...] + piece_c[...]
    rows = jnp.concatenate([rows, jnp.zeros((SPAN - SENT, COLS), jnp.float32)], axis=0)
    padded = jnp.concatenate([rows, jnp.zeros((SPAN, BLOCK), jnp.float32)], axis=1)
    cutout = pltpu.roll(padded, KHALF - noted_number(sheet, 2), axis=1)
    cut_high, cut_low = split(cutout)
    col_high, col_low = table[: 2 * BLOCK, :], table[2 * BLOCK : 4 * BLOCK, :]
    for block in range(COLS // BLOCK):
        cols = slice(block * BLOCK, (block + 2) * BLOCK)
        both = jnp.concatenate([cut_high[:, cols], cut_low[:, cols]], axis=0)
        main = jnp.dot(both, col_high, preferred_element_type=jnp.float32)
        rest = jnp.dot(cut_high[:, cols], col_low, preferred_element_type=jnp.float32)
        across = main[:SPAN] + main[SPAN:] + rest
        across_high, across_low = split(across)
        for factor in range(NFACTORS):
            take = slice(factor * BLOCK, (factor + 1) * BLOCK)
            put = slice(block * BLOCK, (block + 1) * BLOCK)
            high_rows[factor, :, put] = across_high[:, take]
            low_rows[factor, :, put] = across_low[:, take]
    first = 0
    for factor, group in enumerate(GROUPS):
        bands = []
        for member in range(len(group)):
            row, lane = row_band_place(first + member)
            row += 4 * BLOCK
            bands.append(table[row : row + HALF, lane : lane + 3 * DEPTH])
        bands = jnp.concatenate(bands, axis=0)
        for half in range(ROWS // HALF):
            take = slice(half * HALF, half * HALF + DEPTH)
            high = high_rows[factor, take, :]
            stacked = jnp.concatenate([high, low_rows[factor, take, :], high], axis=0)
            out = jnp.dot(bands, stacked, preferred_element_type=jnp.float32)
            for member in range(len(group)):
                scaled = (
                    out[member * HALF : (member + 1) * HALF]
                    * sheet[half * HALF : (half + 1) * HALF, :]
                )
                put_plane(planes, first + member, half * HALF, scaled)
        first += len(group)
    put_plane(planes, NBASIS - 1, 0, sheet[:ROWS, :])
    put_plane(planes, NBASIS, 0, sheet[ROWS : 2 * ROWS, :])
    for slot in range(NBASIS + 1, SLOTS):
        put_plane(planes, slot, 0, jnp.zeros((ROWS, COLS), jnp.float32))
    def gram_step(chunk, total):
        highs, lows = [], []
        for inner in range(CHUNK):
            for block in range(BLOCKS):
                row = block * SLOTS * PITCH + chunk * CHUNK + inner
                high, low = split(planes[pl.ds(row, SLOTS, stride=PITCH), :])
                highs.append(high)
                lows.append(low)
        high = jnp.concatenate(highs, axis=1)
        low = jnp.concatenate(lows, axis=1)
        both = jnp.concatenate([high, low], axis=0)
        return total + lax.dot_general(
            high, both, (((1,), (1,)), ((), ())), preferred_element_type=jnp.float32
        )

    total = lax.fori_loop(0, ROWS // CHUNK, gram_step, jnp.zeros((SLOTS, 2 * SLOTS), jnp.float32))
    gram_out[...] = jnp.concatenate(
        [total, jnp.zeros((SLOTS, BLOCK - 2 * SLOTS), jnp.float32)], axis=1
    )


def basis(pieces, *operands):
    return pl.pallas_call(
        basis_kernel,
        out_shape=(
            jax.ShapeDtypeStruct((BLOCKS * SLOTS * PITCH, BLOCK), jnp.float32),
            jax.ShapeDtypeStruct((SLOTS, BLOCK), jnp.float32),
        ),
        in_specs=[VMEM] * 5,
        out_specs=(VMEM, VMEM),
        scratch_shapes=[
            pltpu.VMEM((NFACTORS, SPAN, COLS), jnp.bfloat16),
            pltpu.VMEM((NFACTORS, SPAN, COLS), jnp.bfloat16),
        ],
        compiler_params=pltpu.CompilerParams(vmem_limit_bytes=LIMIT),
        name="basis",
    )(*pieces, *operands)


def solve_pair(corner, heads):
    (a, b), (c, d) = corner
    inverse = 1.0 / (a * d - b * c)
    return (d * heads[0] - b * heads[1]) * inverse, (a * heads[1] - c * heads[0]) * inverse


def solve_corner(corner, heads):
    first = [row[:2] for row in corner[:2]]
    right = [solve_pair(first, [corner[0][col], corner[1][col]]) for col in (2, 3)]
    upper = solve_pair(first, heads[:2])
    rest = [
        [
            corner[row][col] - corner[row][0] * right[col - 2][0] - corner[row][1] * right[col - 2][1]
            for col in (2, 3)
        ]
        for row in (2, 3)
    ]
    lower = solve_pair(
        rest,
        [heads[row] - corner[row][0] * upper[0] - corner[row][1] * upper[1] for row in (2, 3)],
    )
    return (
        *(upper[row] - right[0][row] * lower[0] - right[1][row] * lower[1] for row in range(2)),
        *lower,
    )


def solve_kernel(grams, planes, sheet, model_out, stamps):
    total = grams[0] + grams[1] + grams[2] + grams[3]
    cross = total[:, SLOTS : 2 * SLOTS]
    normal = total[:, :SLOTS] + cross + cross.T
    row_id = lax.broadcasted_iota(jnp.int32, (SLOTS, SLOTS), 0)
    col_id = lax.broadcasted_iota(jnp.int32, (SLOTS, SLOTS), 1)
    diagonal = jnp.logical_and(row_id == col_id, row_id < NBASIS)
    trace = jnp.sum(jnp.where(diagonal, normal, 0.0), keepdims=True)
    matrix = normal + jnp.where(diagonal, RIDGE * trace / NBASIS, 0.0)
    for step in range(0, NBASIS, 4):
        columns = [
            jnp.broadcast_to(matrix[:, step + part : step + part + 1], (SLOTS, SLOTS))
            for part in range(4)
        ]
        heads = [matrix[step + part : step + part + 1] for part in range(4)]
        corner = [[columns[col][step + row : step + row + 1] for col in range(4)] for row in range(4)]
        solved = solve_corner(corner, heads)
        others = matrix
        for part in range(4):
            others = others - columns[part] * solved[part]
        matrix = others
        for part in range(4):
            matrix = jnp.where(row_id == step + part, solved[part], matrix)
    answer = jnp.broadcast_to(matrix[:, NBASIS : NBASIS + 1], (SLOTS, BLOCK))
    for block in range(BLOCKS):
        model = jnp.zeros((ROWS, BLOCK), jnp.float32)
        for plane in range(NBASIS):
            factor = jnp.broadcast_to(answer[plane : plane + 1, :], (ROWS, BLOCK))
            at = (block * SLOTS + plane) * PITCH
            model = model + factor * planes[at : at + ROWS, :]
        model_out[:, block * BLOCK : (block + 1) * BLOCK] = model
    difference = sheet[ROWS : 2 * ROWS, :] - model_out[...]
    tile, row_move, col_move = (noted_number(sheet, part) for part in range(3))
    moved = pltpu.roll(difference, lax.rem(row_move + ROWS, ROWS), axis=0)
    moved = pltpu.roll(moved, lax.rem(col_move + COLS, COLS), axis=1)
    from_row = lax.broadcasted_iota(jnp.int32, (ROWS, COLS), 0) - row_move
    from_col = lax.broadcasted_iota(jnp.int32, (ROWS, COLS), 1) - col_move
    inside = (from_row >= 0) & (from_row < ROWS) & (from_col >= 0) & (from_col < COLS)
    placed = jnp.where(inside, moved, 0.0)
    for place in range(LINE):
        mine = lax.bitwise_and(tile, LINE - 1) == place
        for block in range(BLOCKS):
            stamps[place, block * ROWS : (block + 1) * ROWS, :] = jnp.where(
                mine, placed[:, block * BLOCK : (block + 1) * BLOCK], 0.0
            )
        stamps[place, TALL:, :] = jnp.full(
            (NOTED - TALL, BLOCK), tile.astype(jnp.float32), jnp.float32
        )


def solve(grams, planes, sheet):
    return pl.pallas_call(
        solve_kernel,
        out_shape=(
            jax.ShapeDtypeStruct((ROWS, COLS), jnp.float32),
            jax.ShapeDtypeStruct((LINE, NOTED, BLOCK), jnp.float32),
        ),
        in_specs=[VMEM, VMEM, VMEM],
        out_specs=(VMEM, VMEM),
        compiler_params=pltpu.CompilerParams(vmem_limit_bytes=LIMIT),
        name="solve",
    )(grams, planes, sheet)


def gather_kernel(stamps, to_own, to_flip, to_next, to_far):
    visit = lax.axis_index("visit")
    even = lax.rem(visit // LINE, 2) == 0
    low = lax.rem(visit, LINE) < LINE // 2
    targets = (
        visit,
        jnp.where(even, visit + LINE, visit - LINE),
        jnp.where(even, visit - LINE, visit + LINE),
        jnp.where(low, visit + 2 * LINE, visit - 2 * LINE),
    )
    for target, out in zip(targets, (to_own, to_flip, to_next, to_far)):
        number = target.astype(jnp.float32)
        hits = [stamps[place, TALL:, :] == number for place in range(LINE)]
        count = jnp.zeros((NOTED - TALL, BLOCK), jnp.float32)
        for hit in hits:
            count = count + jnp.where(hit, 1.0, 0.0)
        out[TALL:, :] = count
        for block in range(BLOCKS):
            rows = slice(block * ROWS, (block + 1) * ROWS)
            total = jnp.zeros((ROWS, BLOCK), jnp.float32)
            for place in range(LINE):
                total = total + jnp.where(hits[place][:1], stamps[place, rows, :], 0.0)
            out[rows, :] = total


def gather(stamps):
    shape = jax.ShapeDtypeStruct((NOTED, BLOCK), jnp.float32)
    return pl.pallas_call(
        gather_kernel,
        out_shape=(shape,) * 4,
        in_specs=[VMEM],
        out_specs=(VMEM,) * 4,
        compiler_params=pltpu.CompilerParams(vmem_limit_bytes=LIMIT),
        name="gather",
    )(stamps)


def mean_kernel(part_a, part_b, part_c, part_d, coadd):
    parts = (part_a, part_b, part_c, part_d)
    count = sum(part[TALL:, :] for part in parts)
    inverse = 1.0 / jnp.maximum(count[:1], 1.0)
    for block in range(BLOCKS):
        rows = slice(block * ROWS, (block + 1) * ROWS)
        total = sum(part[rows, :] for part in parts)
        coadd[:, block * BLOCK : (block + 1) * BLOCK] = total * inverse


def mean(*parts):
    return pl.pallas_call(
        mean_kernel,
        out_shape=jax.ShapeDtypeStruct((ROWS, COLS), jnp.float32),
        in_specs=[VMEM] * 4,
        out_specs=VMEM,
        compiler_params=pltpu.CompilerParams(vmem_limit_bytes=LIMIT),
        name="mean",
    )(*parts)


def shards(template, science, inverse_variance, intersections):
    visits = lax.axis_size("visit")
    groups = [list(range(first, first + PLANE)) for first in range(0, visits, PLANE)]
    upward = [(i, i + PLANE) for i in range(visits - PLANE)]
    downward = [(target, source) for source, target in upward]
    own = intersections[0]
    below = lax.ppermute(own, "visit", upward)
    above = lax.ppermute(own, "visit", downward)
    sheet, table = prepare(
        own, science[0, 0], inverse_variance[0, 0], jnp.asarray(tables())
    )
    window = lax.all_to_all(spread(template[0]), "visit", 0, 0, axis_index_groups=groups)
    piece_own, piece_up, piece_down = serve(window, sheet, below, above)
    from_above = lax.ppermute(piece_down, "visit", downward)
    from_below = lax.ppermute(piece_up, "visit", upward)
    planes, gram = basis((piece_own, from_above, from_below), sheet, table)
    grams = lax.all_gather(gram, "patch")
    model, stamps = solve(grams, planes, sheet)
    lines = [list(range(first, first + LINE)) for first in range(0, visits, LINE)]
    to_own, to_flip, to_next, to_far = gather(
        lax.all_to_all(stamps, "visit", 0, 0, axis_index_groups=lines)
    )
    flip = [(i, i ^ LINE) for i in range(visits)]
    following = [(i, ((i + LINE) ^ LINE) - LINE) for i in range(LINE, visits - LINE)]
    far = [(i, i + 2 * LINE if i % LINE < LINE // 2 else i - 2 * LINE) for i in range(visits)]
    far = [(source, target) for source, target in far if 0 <= target < visits]
    from_far = lax.ppermute(to_far, "visit", far)
    from_flip = lax.ppermute(to_flip, "visit", flip)
    from_next = lax.ppermute(to_next, "visit", following)
    difference = sheet[ROWS : 2 * ROWS] - model
    return (difference[None, None], mean(to_own, from_next, from_flip, from_far)[None])


def solution(mesh):
    in_specs = (
        P("patch", "visit", None),
        P("visit", "patch", None, None),
        P("visit", "patch", None, None),
        P("visit", "patch", None),
    )
    out_specs = (P("visit", "patch", None, None), P("patch", "visit", None))
    return jax.shard_map(shards, mesh=mesh, in_specs=in_specs, out_specs=out_specs, check_vma=False)
```
